32 devices in a mesh: ctx: 8 (over z, core), ws: 4 (over y, x).
Axes of the slice: x: 2, y: 2, z: 4, core: 2. Of those that a mesh axis runs over, the one named last changes fastest.
Arguments:
- hidden_in: bfloat16 [1024, 4, 1536], P('ctx', 'ws'), may hold values from -6 to 6
- attn_gain: bfloat16 [1536], P('ws'), may hold values from 0.099609375 to 1.8984375
- w_query: bfloat16 [1536, 1536], P('ws'), may hold values from -0.21875 to 0.21875
- key_weight: bfloat16 [1536, 768], P('ws'), may hold values from -0.21875 to 0.21875
- value_weight: bfloat16 [1536, 768], P('ws'), may hold values from -0.15625 to 0.15625
- w_out: bfloat16 [1536, 1536], P('ws'), may hold values from -1.25 to 1.25
- ffn_gain: bfloat16 [1536], P('ws'), may hold values from 0.099609375 to 1.8984375
- w_gate: bfloat16 [1536, 4096], P('ws'), may hold values from -0.15625 to 0.15625
- w_up: bfloat16 [1536, 4096], P('ws'), may hold values from -0.15625 to 0.15625
- w_down: bfloat16 [4096, 1536], P('ws'), may hold values from -0.09375 to 0.09375
- cotangent: bfloat16 [1024, 4, 1536], P('ctx', 'ws'), may hold values from -6 to 6
Outputs:
- output: bfloat16 [1024, 4, 1536], P('ctx', 'ws')
- grad_hidden_in: float32 [1024, 4, 1536], P('ctx', 'ws')
- grad_attn_gain: float32 [1536], P('ws')
- grad_w_query: float32 [1536, 1536], P('ws')
- grad_w_key: float32 [1536, 768], P('ws')
- grad_w_value: float32 [1536, 768], P('ws')
- grad_w_out: float32 [1536, 1536], P('ws')
- grad_ffn_gain: float32 [1536], P('ws')
- grad_w_gate: float32 [1536, 4096], P('ws')
- grad_w_up: float32 [1536, 4096], P('ws')
- grad_w_down: float32 [4096, 1536], P('ws')
The draws below stay inside these ranges and needn't reach their ends.
All inputs are finite; a program needn't handle non-finite values.
Results may differ from the reference program's by a relative error of at most 0.023.
Values may be sent and summed in bfloat16 or wider, within the bound.
A program may use at most 320 MiB of HBM per device.

```python
import jax
import jax.numpy as jnp
from jax import lax

D = 1536
FF = 4096
QUERY_HEADS = 16
KEY_VALUE_HEADS = 8
HEAD_DIM = 96
QW = 1536
KW = 768
SEQ_LEN = 1024
SEQS = 4


def levels(rng, shape, shards, low, top_value):
    def one(position, parts):
        steps = jax.random.uniform(jax.random.fold_in(jax.random.fold_in(rng, 6), position), (parts,), jnp.float32, low / len(shards), top_value / len(shards))
        return jnp.repeat(jnp.exp(steps), shape[position] // parts).reshape((-1,) + (1,) * (len(shape) - position - 1))

    factor_of = one(*shards[0])
    for cut in shards[1:]:
        factor_of = factor_of * one(*cut)
    return factor_of


def normal_values(own_key, shape, scale, most, shards=(), held_as=jnp.bfloat16):
    array = jax.random.normal(own_key, shape, jnp.float32) * scale
    if len(shards) > 0:
        array = levels(own_key, shape, shards, -0.22, 0.18) * array
    return jnp.clip(array, min=-most, max=most).astype(held_as)


def setup_inputs(seed: int = 0) -> dict:
    arg_keys = jax.random.split(jax.random.key(seed), 12)
    return {
        "hidden_in": normal_values(arg_keys[0], (SEQ_LEN, SEQS, D), 1.0, 6.0, ((0, 8), (1, 4))),
        "attn_gain": jnp.clip(1.0 + 0.18 * jax.random.normal(arg_keys[1], (D,), jnp.float32), 0.099609375, 1.8984375).astype(jnp.bfloat16),
        "w_query": normal_values(arg_keys[2], (D, QW), (D // 2) ** -0.5, 0.21875, ((0, 4),)),
        "key_weight": normal_values(arg_keys[3], (D, KW), (D // 2) ** -0.5, 0.21875, ((0, 4),)),
        "value_weight": normal_values(arg_keys[4], (D, KW), D ** -0.5, 0.15625, ((0, 4),)),
        "w_out": normal_values(arg_keys[5], (QW, D), (QW // 64) ** -0.5, 1.25, ((0, 4),)),
        "ffn_gain": jnp.clip(1.0 + 0.18 * jax.random.normal(arg_keys[6], (D,), jnp.float32), 0.099609375, 1.8984375).astype(jnp.bfloat16),
        "w_gate": normal_values(arg_keys[7], (D, FF), D ** -0.5, 0.15625, ((0, 4),)),
        "w_up": normal_values(arg_keys[8], (D, FF), D ** -0.5, 0.15625, ((0, 4),)),
        "w_down": normal_values(arg_keys[9], (FF, D), FF ** -0.5, 0.09375, ((0, 4),)),
        "cotangent": normal_values(arg_keys[10], (SEQ_LEN, SEQS, D), 1.0, 6.0, ((0, 8), (1, 4))),
    }


EPSILON = 1e-05
ROPE_BASE = 100000.0
MASK_FILL = -1e+30

@jax.custom_vjp
def rms_normalize(v):
    return lax.optimization_barrier(v.astype(jnp.bfloat16)).astype(jnp.float32)

@jax.custom_vjp
def rms_normalize_backward(v):
    return v

def low_keep(v):
    return (rms_normalize(v), None)

def low_pass(kept, grad):
    return (grad,)

def back_keep(v):
    return (v, None)

def back_low(kept, grad):
    return (rms_normalize(grad),)
rms_normalize.defvjp(low_keep, low_pass)
rms_normalize_backward.defvjp(back_keep, back_low)

def matrix_product(left, right):
    return jnp.dot(left, right, precision=lax.Precision.HIGHEST, preferred_element_type=jnp.float32)

def normalize(matrix):
    return matrix * lax.rsqrt(lax.optimization_barrier(jnp.mean(matrix * matrix, axis=-1, keepdims=True)) + EPSILON)

def tables(positions):
    half_size = HEAD_DIM // 2
    frequency = ROPE_BASE ** (-(jnp.arange(half_size, dtype=jnp.float32) * 2.0 / HEAD_DIM))
    angles = positions.astype(jnp.float32)[:, None] * frequency[None, :]
    return (jnp.cos(angles)[:, None, :], jnp.sin(angles)[:, None, :])

def apply_rotary(vectors, cosine_table, sine_table):
    half_size = vectors.shape[-1] // 2
    first_half = vectors[..., :half_size]
    second_half = vectors[..., half_size:]
    return jnp.concatenate([first_half * cosine_table - second_half * sine_table, second_half * cosine_table + first_half * sine_table], axis=-1)

def one_sequence(sequence, attn_gain, w_query, key_weight, value_weight, w_out, ffn_gain, w_gate, w_up, w_down):
    sequence_length = sequence.shape[0]
    query_group = QUERY_HEADS // KEY_VALUE_HEADS
    attention_normed_input = rms_normalize(normalize(sequence) * attn_gain)
    query_unrotated = rms_normalize_backward(matrix_product(attention_normed_input, w_query)).reshape(sequence_length, QUERY_HEADS, HEAD_DIM)
    key_unrotated = rms_normalize_backward(matrix_product(attention_normed_input, key_weight)).reshape(sequence_length, KEY_VALUE_HEADS, HEAD_DIM)
    value_matrix = rms_normalize(rms_normalize_backward(matrix_product(attention_normed_input, value_weight))).reshape(sequence_length, KEY_VALUE_HEADS, HEAD_DIM)
    cosine_table, sine_table = tables(jnp.arange(sequence_length, dtype=jnp.int32))
    query_matrix = rms_normalize(apply_rotary(query_unrotated, cosine_table, sine_table)).reshape(sequence_length, KEY_VALUE_HEADS, query_group, HEAD_DIM)
    key_rot = rms_normalize(apply_rotary(key_unrotated, cosine_table, sine_table))
    block_rows = min(512, sequence_length)
    key_positions = jnp.arange(sequence_length, dtype=jnp.int32)

    def attend(block_index):
        start_row = block_index * block_rows
        query_rows = lax.dynamic_slice_in_dim(query_matrix, start_row, block_rows, 0)
        scores = jnp.einsum('qgjd,kgd->gjqk', query_rows, key_rot, precision=lax.Precision.HIGHEST) * HEAD_DIM ** (-0.5)
        scores = rms_normalize_backward(scores)
        allowed = (start_row + jnp.arange(block_rows, dtype=jnp.int32))[:, None] >= key_positions[None, :]
        scores = jnp.where(allowed, scores, MASK_FILL)
        row_max = lax.optimization_barrier(jnp.max(scores, axis=-1, keepdims=True))
        weights = jnp.exp(scores - row_max)
        row_total = lax.optimization_barrier(jnp.sum(weights, axis=-1))
        mixture = jnp.einsum('gjqk,kgd->qgjd', rms_normalize(weights), value_matrix, precision=lax.Precision.HIGHEST)
        return mixture / jnp.transpose(row_total, (2, 0, 1))[..., None]
    attn_blocks = lax.map(jax.checkpoint(attend), jnp.arange(sequence_length // block_rows, dtype=jnp.int32))
    attended = rms_normalize(rms_normalize_backward(attn_blocks.reshape(sequence_length, QUERY_HEADS * HEAD_DIM)))
    residual = sequence + rms_normalize_backward(matrix_product(attended, w_out))
    normed_ffn = rms_normalize(normalize(residual) * ffn_gain)
    gate_proj = rms_normalize_backward(matrix_product(normed_ffn, w_gate))
    up_proj = rms_normalize_backward(matrix_product(normed_ffn, w_up))
    hidden = rms_normalize(jax.nn.silu(gate_proj) * up_proj)
    return residual + rms_normalize_backward(matrix_product(hidden, w_down))

def forward(hidden_in, attn_gain, w_query, key_weight, value_weight, w_out, ffn_gain, w_gate, w_up, w_down):

    def scan_step(carried, sequence):
        result = jax.checkpoint(one_sequence)(sequence, attn_gain, w_query, key_weight, value_weight, w_out, ffn_gain, w_gate, w_up, w_down)
        return (carried, result)
    unused, results = lax.scan(scan_step, None, jnp.swapaxes(hidden_in, 0, 1))
    return jnp.swapaxes(results, 0, 1)

def reference(hidden_in, attn_gain, w_query, key_weight, value_weight, w_out, ffn_gain, w_gate, w_up, w_down, cotangent):
    float_args = tuple((argument.astype(jnp.float32) for argument in (hidden_in, attn_gain, w_query, key_weight, value_weight, w_out, ffn_gain, w_gate, w_up, w_down)))
    output, pullback = jax.vjp(forward, *float_args)
    gradients = pullback(cotangent.astype(jnp.float32))
    return (output.astype(jnp.bfloat16), gradients[0], gradients[1], gradients[2], gradients[3], gradients[4], gradients[5], gradients[6], gradients[7], gradients[8], gradients[9])
```

```python
import jax
import jax.numpy as jnp
from jax import lax
from jax.sharding import PartitionSpec as P

HEAD_DIM = 96
EPSILON = 1e-05
ROPE_BASE = 100000.0
MASK_FILL = -1e30
BF = jnp.bfloat16
F32 = jnp.float32


def normalize(matrix):
    factor = lax.rsqrt(jnp.mean(matrix * matrix, axis=-1, keepdims=True) + EPSILON)
    return (matrix * factor, factor)


def norm_back(grad_normed, normed, factor):
    return factor * (grad_normed - normed * jnp.mean(grad_normed * normed, axis=-1, keepdims=True))


def rope_tables(positions, rotated_heads, plain_heads, groups):
    half = HEAD_DIM // 2
    frequency = ROPE_BASE ** (-(jnp.arange(half, dtype=F32) * 2.0 / HEAD_DIM))
    angles = positions.astype(F32)[:, None] * frequency[None, :]
    cosine, sine = jnp.cos(angles), jnp.sin(angles)
    plain = jnp.zeros((positions.shape[0], plain_heads * HEAD_DIM), F32)
    cosines = [cosine, cosine] * rotated_heads + [plain + 1.0]
    sines = [-sine, sine] * rotated_heads + [plain]
    return (
        jnp.concatenate(cosines * groups, axis=-1),
        jnp.concatenate(sines * groups, axis=-1),
    )


def swap_halves(vectors):
    rows, width = vectors.shape
    half = HEAD_DIM // 2
    parts = vectors.reshape(rows, width // HEAD_DIM, 2, half)
    return jnp.flip(parts, axis=2).reshape(rows, width)


def against(left, weight):
    return lax.dot_general(
        left, weight, (((1,), (1,)), ((), ())), preferred_element_type=F32
    )


def outer_sum(left, right):
    return lax.dot_general(
        left, right, (((0,), (0,)), ((), ())), preferred_element_type=F32
    )


def dot(left, right):
    return jnp.dot(left, right, preferred_element_type=F32)


def gather_rows(block):
    return lax.all_gather(block, "ws", axis=0, tiled=True)


def sum_rows(partial, ws):
    blocks = partial.astype(BF).reshape(ws, partial.shape[0] // ws, partial.shape[1])
    return jnp.sum(lax.all_to_all(blocks, "ws", 0, 0).astype(F32), axis=0)


def attend_pair(qkv, group):
    length = qkv.shape[0]
    width = group * HEAD_DIM
    query = qkv[:, :width].reshape(length, group, HEAD_DIM)
    key = qkv[:, width : width + HEAD_DIM]
    value = qkv[:, width + HEAD_DIM :]
    rows = min(512, length)

    def one(index):
        start = index * rows
        part = lax.dynamic_slice_in_dim(query, start, rows, 0)
        scores = jnp.einsum("qjd,kd->jqk", part, key, preferred_element_type=F32) * HEAD_DIM**-0.5
        allowed = (start + jnp.arange(rows))[:, None] >= jnp.arange(length)[None, :]
        scores = jnp.where(allowed, scores, MASK_FILL)
        top = jnp.max(scores, axis=-1, keepdims=True)
        weights = jnp.exp(scores - top)
        total = jnp.sum(weights, axis=-1, keepdims=True)
        mixed = jnp.einsum("jqk,kd->jqd", weights.astype(BF), value, preferred_element_type=F32)
        return (mixed / total, top, total)

    attended, top, total = lax.map(one, jnp.arange(length // rows))
    return attended, top, total


def attend_pair_back(qkv, grad, attended, top, total, group):
    length = qkv.shape[0]
    width = group * HEAD_DIM
    query = qkv[:, :width].reshape(length, group, HEAD_DIM)
    grad = grad.reshape(length, group, HEAD_DIM)
    key = qkv[:, width : width + HEAD_DIM]
    value = qkv[:, width + HEAD_DIM :]
    rows = min(512, length)

    def one(carried, inputs):
        index, out, peak, sums = inputs
        grad_key, grad_value = carried
        start = index * rows
        part = lax.dynamic_slice_in_dim(query, start, rows, 0)
        grad_part = lax.dynamic_slice_in_dim(grad, start, rows, 0)
        scores = jnp.einsum("qjd,kd->jqk", part, key, preferred_element_type=F32) * HEAD_DIM**-0.5
        allowed = (start + jnp.arange(rows))[:, None] >= jnp.arange(length)[None, :]
        scores = jnp.where(allowed, scores, MASK_FILL)
        weights = jnp.exp(scores - peak)
        wide = jnp.swapaxes(grad_part.astype(F32), 0, 1)
        delta = jnp.sum(wide * out, axis=-1, keepdims=True)
        grad_probs = jnp.einsum("qjd,kd->jqk", grad_part, value, preferred_element_type=F32)
        grad_scores = (weights / sums * (grad_probs - delta)).astype(BF)
        grad_query = jnp.einsum("jqk,kd->qjd", grad_scores, key, preferred_element_type=F32)
        grad_key = grad_key + jnp.einsum(
            "jqk,qjd->kd", grad_scores, part, preferred_element_type=F32
        )
        grad_value = grad_value + jnp.einsum(
            "jqk,jqd->kd", weights.astype(BF), (wide / sums).astype(BF), preferred_element_type=F32
        )
        return (grad_key, grad_value), grad_query

    zero = jnp.zeros((length, HEAD_DIM), F32)
    (grad_key, grad_value), grad_query = lax.scan(
        one, (zero, zero), (jnp.arange(length // rows), attended, top, total)
    )
    return grad_query.reshape(length, width), grad_key, grad_value


def body(
    hidden_in,
    attn_gain,
    w_query,
    key_weight,
    value_weight,
    w_out,
    ffn_gain,
    w_gate,
    w_up,
    w_down,
    cotangent,
):
    ws, ctx = lax.axis_size("ws"), lax.axis_size("ctx")
    local_len, local_seqs, features = hidden_in.shape
    row_count = local_len * local_seqs
    q_heads = w_query.shape[1] // HEAD_DIM
    kv_heads = key_weight.shape[1] // HEAD_DIM
    group = q_heads // kv_heads
    own_heads = kv_heads // ws
    wide = (group + 2) * HEAD_DIM
    q_wide = group * HEAD_DIM
    pairs = ws * local_seqs * own_heads
    copies = ctx // pairs
    depth = features // ws
    positions = lax.axis_index("ctx") * local_len + jnp.arange(local_len, dtype=jnp.int32)
    cosines, sines = rope_tables(positions, group + 1, 1, own_heads)
    cosines = jnp.tile(cosines, (ws * local_seqs, 1))
    sines = jnp.tile(sines, (ws * local_seqs, 1))

    gain_attn = lax.all_gather(attn_gain, "ws", axis=0, tiled=True).astype(F32)
    gain_ffn = lax.all_gather(ffn_gain, "ws", axis=0, tiled=True).astype(F32)
    columns = jnp.concatenate(
        [
            w_query.reshape(depth, kv_heads, q_wide),
            key_weight.reshape(depth, kv_heads, HEAD_DIM),
            value_weight.reshape(depth, kv_heads, HEAD_DIM),
        ],
        axis=-1,
    ).reshape(depth, ws, own_heads * wide)
    w_qkv = lax.all_to_all(columns, "ws", 1, 0, tiled=False).reshape(features, own_heads * wide)
    hidden_units = w_gate.shape[1] // ws
    gate = lax.all_to_all(w_gate.reshape(depth, ws, hidden_units), "ws", 1, 0).reshape(features, hidden_units)
    up = lax.all_to_all(w_up.reshape(depth, ws, hidden_units), "ws", 1, 0).reshape(features, hidden_units)

    inputs = jnp.swapaxes(hidden_in, 0, 1).reshape(row_count, features).astype(F32)
    grad_low = jnp.swapaxes(cotangent, 0, 1).reshape(row_count, features)
    attn_unit, attn_factor = normalize(inputs)
    normed_attn = gather_rows((attn_unit * gain_attn).astype(BF))
    grad_low_all = gather_rows(grad_low)

    raw = dot(normed_attn, w_qkv)
    qkv = (raw * cosines + swap_halves(raw) * sines).astype(BF)

    def to_pairs(rows):
        width = rows.shape[1] // own_heads
        blocks = rows.reshape(ws * local_seqs, local_len, own_heads, width)
        blocks = jnp.swapaxes(blocks, 1, 2).reshape(pairs, local_len, width)
        blocks = jnp.concatenate([blocks] * copies, axis=0)
        return lax.all_to_all(blocks, "ctx", 0, 0).reshape(ctx * local_len, width)

    def from_pairs(rows):
        width = rows.shape[1]
        blocks = lax.all_to_all(rows.reshape(ctx, local_len, width), "ctx", 0, 0)
        first = lax.axis_index("ctx") // pairs * pairs
        blocks = lax.dynamic_slice_in_dim(blocks, first, pairs, 0)
        blocks = blocks.reshape(ws * local_seqs, own_heads, local_len, width)
        return jnp.swapaxes(blocks, 1, 2).reshape(ws * row_count, own_heads * width)

    pair = to_pairs(qkv)
    attended, top, total = attend_pair(pair, group)
    flat = jnp.swapaxes(attended, 1, 2).reshape(ctx * local_len, q_wide)
    attn_low = from_pairs(flat.astype(BF))
    residual = inputs + sum_rows(dot(attn_low, w_out), ws)
    ffn_unit, ffn_factor = normalize(residual)
    normed_ffn = gather_rows((ffn_unit * gain_ffn).astype(BF))
    gate_proj, up_proj = dot(normed_ffn, gate), dot(normed_ffn, up)
    sigmoid_gate = jax.nn.sigmoid(gate_proj)
    activation = gate_proj * sigmoid_gate
    hidden = (activation * up_proj).astype(BF)
    output = (residual + sum_rows(dot(hidden, w_down), ws)).astype(BF)
    grad_hidden = against(grad_low_all, w_down)
    grad_up = (grad_hidden * activation).astype(BF)
    grad_gate = (
        grad_hidden * up_proj * sigmoid_gate * (1.0 + gate_proj * (1.0 - sigmoid_gate))
    ).astype(BF)
    grad_normed_ffn = sum_rows(against(grad_gate, gate) + against(grad_up, up), ws)
    grad_ffn_gain = jnp.sum(grad_normed_ffn * ffn_unit, axis=0)
    grad_residual = grad_low.astype(F32) + norm_back(
        grad_normed_ffn * gain_ffn, ffn_unit, ffn_factor
    )
    grad_branch = gather_rows(grad_residual.astype(BF))
    grad_attended = against(grad_branch, w_out).astype(BF)
    grad_q, grad_k, grad_v = attend_pair_back(
        pair, to_pairs(grad_attended), attended, top, total, group
    )
    scale = HEAD_DIM**-0.5
    back = jnp.concatenate([grad_q * scale, grad_k * scale, grad_v], axis=-1)
    whole = jnp.arange(ctx * local_len, dtype=jnp.int32)
    pair_cos, pair_sin = rope_tables(whole, group + 1, 1, 1)
    back = (back * pair_cos - swap_halves(back) * pair_sin).astype(BF)
    grad_qkv = from_pairs(back)
    grad_normed_attn = sum_rows(against(grad_qkv, w_qkv), ws)
    grad_attn_gain = jnp.sum(grad_normed_attn * attn_unit, axis=0)
    grad_input = grad_residual + norm_back(grad_normed_attn * gain_attn, attn_unit, attn_factor)

    def to_owner(columns_sum):
        width = columns_sum.shape[1]
        moved = lax.all_to_all(columns_sum.astype(BF).reshape(ws, depth, width), "ws", 0, 0)
        return jnp.swapaxes(moved, 0, 1)

    grad_w_qkv = to_owner(outer_sum(normed_attn, grad_qkv)).reshape(depth, kv_heads, wide)
    sums = lax.psum(
        (
            grad_w_qkv[..., :q_wide].reshape(depth, q_heads * HEAD_DIM),
            grad_w_qkv[..., q_wide : q_wide + HEAD_DIM].reshape(depth, kv_heads * HEAD_DIM),
            grad_w_qkv[..., q_wide + HEAD_DIM :].reshape(depth, kv_heads * HEAD_DIM),
            outer_sum(attn_low, grad_branch).astype(BF),
            to_owner(outer_sum(normed_ffn, grad_gate)).reshape(depth, ws * hidden_units),
            to_owner(outer_sum(normed_ffn, grad_up)).reshape(depth, ws * hidden_units),
            outer_sum(hidden, grad_low_all).astype(BF),
        ),
        "ctx",
    )
    gains = lax.psum(
        lax.psum_scatter(
            jnp.stack([grad_attn_gain, grad_ffn_gain], axis=1), "ws", scatter_dimension=0, tiled=True
        ),
        "ctx",
    )
    sums = [s.astype(F32) for s in sums]

    def place(rows):
        return jnp.swapaxes(rows.reshape(local_seqs, local_len, features), 0, 1)

    return (
        place(output),
        place(grad_input),
        gains[:, 0],
        *sums[:4],
        gains[:, 1],
        *sums[4:],
    )


def solution(mesh):
    tokens, rows, one = P("ctx", "ws", None), P("ws", None), P("ws")
    return jax.shard_map(
        body,
        mesh=mesh,
        in_specs=(tokens, one, rows, rows, rows, rows, one, rows, rows, rows, tokens),
        out_specs=(tokens, tokens, one, rows, rows, rows, rows, one, rows, rows, rows),
        check_vma=False,
    )
```

```python
import functools

import jax
import jax.numpy as jnp
from jax import lax
from jax.experimental import pallas as pl
from jax.experimental.pallas import tpu as pltpu
from jax.sharding import PartitionSpec as P

HEAD_DIM = 96
EPSILON = 1e-05
ROPE_BASE = 100000.0
MASK_FILL = -1e30
BF = jnp.bfloat16
F32 = jnp.float32


def normalize(matrix):
    factor = lax.rsqrt(jnp.mean(matrix * matrix, axis=-1, keepdims=True) + EPSILON)
    return (matrix * factor, factor)


def norm_back(grad_normed, normed, factor):
    return factor * (grad_normed - normed * jnp.mean(grad_normed * normed, axis=-1, keepdims=True))


def rope_tables(positions, rotated_heads, plain_heads, groups):
    half = HEAD_DIM // 2
    frequency = ROPE_BASE ** (-(jnp.arange(half, dtype=F32) * 2.0 / HEAD_DIM))
    angles = positions.astype(F32)[:, None] * frequency[None, :]
    cosine, sine = jnp.cos(angles), jnp.sin(angles)
    plain = jnp.zeros((positions.shape[0], plain_heads * HEAD_DIM), F32)
    cosines = [cosine, cosine] * rotated_heads + [plain + 1.0]
    sines = [-sine, sine] * rotated_heads + [plain]
    return (
        jnp.concatenate(cosines * groups, axis=-1),
        jnp.concatenate(sines * groups, axis=-1),
    )


def swap_halves(vectors):
    rows, width = vectors.shape
    half = HEAD_DIM // 2
    parts = vectors.reshape(rows, width // HEAD_DIM, 2, half)
    return jnp.flip(parts, axis=2).reshape(rows, width)


def against(left, weight):
    return lax.dot_general(
        left, weight, (((1,), (1,)), ((), ())), preferred_element_type=F32
    )


def outer_sum(left, right):
    return lax.dot_general(
        left, right, (((0,), (0,)), ((), ())), preferred_element_type=F32
    )


def dot(left, right):
    return jnp.dot(left, right, preferred_element_type=F32)


def gather_rows(block):
    return lax.all_gather(block, "ws", axis=0, tiled=True)


def sum_rows(partial, ws):
    blocks = partial.astype(BF).reshape(ws, partial.shape[0] // ws, partial.shape[1])
    return jnp.sum(lax.all_to_all(blocks, "ws", 0, 0).astype(F32), axis=0)


def attend_pair(qkv, group):
    length = qkv.shape[0]
    width = group * HEAD_DIM
    query = qkv[:, :width].reshape(length, group, HEAD_DIM)
    key = qkv[:, width : width + HEAD_DIM]
    value = qkv[:, width + HEAD_DIM :]
    rows = min(512, length)

    def one(index):
        start = index * rows
        part = lax.dynamic_slice_in_dim(query, start, rows, 0)
        scores = jnp.einsum("qjd,kd->jqk", part, key, preferred_element_type=F32) * HEAD_DIM**-0.5
        allowed = (start + jnp.arange(rows))[:, None] >= jnp.arange(length)[None, :]
        scores = jnp.where(allowed, scores, MASK_FILL)
        top = jnp.max(scores, axis=-1, keepdims=True)
        weights = jnp.exp(scores - top)
        total = jnp.sum(weights, axis=-1, keepdims=True)
        mixed = jnp.einsum("jqk,kd->jqd", weights.astype(BF), value, preferred_element_type=F32)
        return (mixed / total, top, total)

    attended, top, total = lax.map(one, jnp.arange(length // rows))
    return attended, top, total


def attend_pair_back(qkv, grad, attended, top, total, group):
    length = qkv.shape[0]
    width = group * HEAD_DIM
    query = qkv[:, :width].reshape(length, group, HEAD_DIM)
    grad = grad.reshape(length, group, HEAD_DIM)
    key = qkv[:, width : width + HEAD_DIM]
    value = qkv[:, width + HEAD_DIM :]
    rows = min(512, length)

    def one(carried, inputs):
        index, out, peak, sums = inputs
        grad_key, grad_value = carried
        start = index * rows
        part = lax.dynamic_slice_in_dim(query, start, rows, 0)
        grad_part = lax.dynamic_slice_in_dim(grad, start, rows, 0)
        scores = jnp.einsum("qjd,kd->jqk", part, key, preferred_element_type=F32) * HEAD_DIM**-0.5
        allowed = (start + jnp.arange(rows))[:, None] >= jnp.arange(length)[None, :]
        scores = jnp.where(allowed, scores, MASK_FILL)
        weights = jnp.exp(scores - peak)
        wide = jnp.swapaxes(grad_part.astype(F32), 0, 1)
        delta = jnp.sum(wide * out, axis=-1, keepdims=True)
        grad_probs = jnp.einsum("qjd,kd->jqk", grad_part, value, preferred_element_type=F32)
        grad_scores = (weights / sums * (grad_probs - delta)).astype(BF)
        grad_query = jnp.einsum("jqk,kd->qjd", grad_scores, key, preferred_element_type=F32)
        grad_key = grad_key + jnp.einsum(
            "jqk,qjd->kd", grad_scores, part, preferred_element_type=F32
        )
        grad_value = grad_value + jnp.einsum(
            "jqk,jqd->kd", weights.astype(BF), (wide / sums).astype(BF), preferred_element_type=F32
        )
        return (grad_key, grad_value), grad_query

    zero = jnp.zeros((length, HEAD_DIM), F32)
    (grad_key, grad_value), grad_query = lax.scan(
        one, (zero, zero), (jnp.arange(length // rows), attended, top, total)
    )
    return grad_query.reshape(length, width), grad_key, grad_value


SKEW = 2
MESH = pl.DeviceIdType.MESH


def remote(src, dst, send_sem, recv_sem, device):
    return pltpu.make_async_remote_copy(
        src_ref=src, dst_ref=dst, send_sem=send_sem, recv_sem=recv_sem,
        device_id=device, device_id_type=MESH,
    )


def grads_kernel(ws, line, moved, rows, *refs):
    count = len(moved)
    parts, outs = refs[:count], refs[count : 2 * count]
    scratch = refs[2 * count :]
    sib_buf, stage, acc, red_in = (scratch[i * count : (i + 1) * count] for i in range(4))
    sems = scratch[4 * count : 10 * count]
    red_send, red_recv, bc_send, bc_recv, core_send, core_recv = (
        sems[i * count : (i + 1) * count] for i in range(6)
    )
    sib_send, sib_recv, mv_send, mv_recv, loc_sem, line_sem = scratch[10 * count :]
    c, w = lax.axis_index("ctx"), lax.axis_index("ws")
    core = lax.rem(c, 2)
    place = c // 2
    sibling = (c + 1 - 2 * core, w)
    before, after = (c - 2, w), (c + 2, w)
    peers = [(c, lax.rem(w + i, ws)) for i in range(1, ws)]

    barrier = pltpu.get_barrier_semaphore()
    for device in peers + [sibling]:
        pl.semaphore_signal(barrier, inc=1, device_id=device, device_id_type=MESH)

    @pl.when(place > 0)
    def _():
        pl.semaphore_signal(barrier, inc=1, device_id=before, device_id_type=MESH)

    @pl.when(place < line - 1)
    def _():
        pl.semaphore_signal(barrier, inc=1, device_id=after, device_id_type=MESH)

    inner = (place > 0).astype(jnp.int32) + (place < line - 1).astype(jnp.int32)
    pl.semaphore_wait(barrier, ws + inner)

    siblings = []
    for i in range(count):
        half = parts[i].at[:, 1 - core] if moved[i] else parts[i].at[1 - core]
        siblings.append(remote(half, sib_buf[i], sib_send.at[i], sib_recv.at[i], sibling))
        siblings[i].start()

    own_columns = [
        pl.ds(pl.multiple_of(w * parts[i].shape[-1], 128), parts[i].shape[-1]) for i in range(count)
    ]

    def move_of(i, step):
        owner = lax.rem(w + step, ws)
        return remote(
            stage[i].at[owner], acc[i].at[:, own_columns[i]],
            mv_send.at[i, step], mv_recv.at[i, step], (c, owner),
        )

    def keep_of(i):
        return pltpu.make_async_copy(stage[i].at[w], acc[i].at[:, own_columns[i]], loc_sem.at[i])

    def share(i):
        siblings[i].wait_recv()
        for step in list(range(1, ws)) + [0]:
            owner = lax.rem(w + step, ws)
            total = parts[i][owner, core].astype(F32) + sib_buf[i][owner].astype(F32)
            stage[i][owner] = total.astype(BF)
            if step:
                move_of(i, step).start()
            else:
                keep_of(i).start()

    def settle(i):
        for step in range(1, ws):
            move_of(i, step).wait_recv()
        keep_of(i).wait()

    def chunk(ref, i, j):
        return ref.at[pl.ds(pl.multiple_of(j * rows[i], rows[i]), rows[i]), :]

    def local(i, j):
        block = chunk(acc[i], i, j)[...].astype(F32)
        if moved[i]:
            return block
        here = chunk(parts[i].at[core], i, j)[...].astype(F32)
        return here + chunk(sib_buf[i], i, j)[...].astype(F32)

    def reduce_chunk(i, j, odd):
        start = (place == 0) if odd else (place == line - 1)
        end = (place == line - 1) if odd else (place == 0)
        step = remote(
            chunk(acc[i], i, j), chunk(red_in[i], i, j),
            red_send[i].at[j], red_recv[i].at[j], after if odd else before,
        )
        final = chunk(outs[i].at[core], i, j)
        down = remote(
            final, final, bc_send[i].at[j], bc_recv[i].at[j], before if odd else after
        )

        @pl.when(start)
        def _():
            if not moved[i]:
                chunk(acc[i], i, j)[...] = local(i, j).astype(BF)
            step.start()

        @pl.when(jnp.logical_not(start))
        def _():
            step.wait_recv()
            total = local(i, j) + chunk(red_in[i], i, j)[...].astype(F32)
            total = total.astype(BF)

            @pl.when(jnp.logical_not(end))
            def _():
                chunk(acc[i], i, j)[...] = total
                step.start()

            @pl.when(end)
            def _():
                chunk(outs[i].at[core], i, j)[...] = total
                down.start()

    def spread_chunk(i, j, odd):
        start = (place == line - 1) if odd else (place == 0)
        end = (place == 0) if odd else (place == line - 1)
        final = chunk(outs[i].at[core], i, j)
        down = remote(
            final, final, bc_send[i].at[j], bc_recv[i].at[j], before if odd else after
        )
        across = remote(final, final, core_send[i].at[j], core_recv[i].at[j], sibling)

        @pl.when(jnp.logical_not(start))
        def _():
            down.wait_recv()

            @pl.when(jnp.logical_not(end))
            def _():
                down.start()

        across.start()

    first, total_chunks = [], 0
    for i in range(count):
        first.append(total_chunks)
        total_chunks += acc[i].shape[0] // rows[i] // 2
    lasts = first[1:] + [total_chunks]
    hops = (line - 1 - place, place)
    skew = SKEW

    def step_at(t, _):
        for i in range(count):
            if moved[i]:
                @pl.when(t == max(first[i] - 8, 0))
                def _():
                    share(i)

                @pl.when(t == first[i])
                def _():
                    settle(i)
            else:
                @pl.when(t == first[i])
                def _():
                    siblings[i].wait_recv()

        for odd in range(2):
            at = t - skew * hops[odd]
            back = t - skew * (2 * (line - 1) - hops[odd])
            for i in range(count):
                @pl.when((at >= first[i]) & (at < lasts[i]))
                def _():
                    reduce_chunk(i, 2 * (at - first[i]) + odd, odd)

                @pl.when((back >= first[i]) & (back < lasts[i]))
                def _():
                    spread_chunk(i, 2 * (back - first[i]) + odd, odd)

        return 0

    lax.fori_loop(0, total_chunks + 2 * skew * (line - 1), step_at, 0)

    for i in range(count):
        chunks = acc[i].shape[0] // rows[i]

        def finish_pair(p, _):
            for odd in range(2):
                j = 2 * p + odd
                reduce_end = (place == line - 1) if odd else (place == 0)
                spread_end = (place == 0) if odd else (place == line - 1)
                final = chunk(outs[i].at[core], i, j)
                there = chunk(outs[i].at[1 - core], i, j)
                step = remote(
                    chunk(acc[i], i, j), chunk(red_in[i], i, j),
                    red_send[i].at[j], red_recv[i].at[j], before,
                )
                down = remote(final, final, bc_send[i].at[j], bc_recv[i].at[j], before)
                across = remote(there, there, core_send[i].at[j], core_recv[i].at[j], sibling)

                @pl.when(jnp.logical_not(reduce_end))
                def _():
                    step.wait_send()

                @pl.when(jnp.logical_not(spread_end))
                def _():
                    down.wait_send()

                across.wait_send()
                across.wait_recv()
            return 0

        lax.fori_loop(0, chunks // 2, finish_pair, 0)
    for i in range(count):
        siblings[i].wait_send()
        if moved[i]:
            for step in range(1, ws):
                move_of(i, step).wait_send()


def sum_grads(parts, moved, rows, ws, line, collective_id):
    shaped, outs, sib, stage, acc, red, counts = [], [], [], [], [], [], []
    for part, is_moved in zip(parts, moved):
        n = part.shape[1]
        half = part.shape[0] // (2 * ws if is_moved else 2)
        wide = ws * n if is_moved else n
        lead = (ws,) if is_moved else ()
        shaped.append(part.reshape(lead + (2, half, n)))
        outs.append(jax.ShapeDtypeStruct((2, half, wide), BF))
        sib.append(pltpu.VMEM(lead + (half, n), BF))
        stage.append(pltpu.VMEM(lead + (half, n) if is_moved else (16, 128), BF))
        acc.append(pltpu.VMEM((half, wide), BF))
        red.append(pltpu.VMEM((half, wide), BF))
    counts = [a.shape[0] // r for a, r in zip(acc, rows)]
    dma = pltpu.SemaphoreType.DMA
    sems = [dma((n,)) for _ in range(6) for n in counts]
    k = len(parts)
    last = [dma((k,)), dma((k,)), dma((k, ws)), dma((k, ws)), dma((k,)), dma((1,))]
    vmem = pl.BlockSpec(memory_space=pltpu.VMEM)
    sums = pl.pallas_call(
        functools.partial(grads_kernel, ws, line, moved, rows),
        out_shape=outs,
        in_specs=[vmem] * k,
        out_specs=[vmem] * k,
        scratch_shapes=sib + stage + acc + red + sems + last,
        compiler_params=pltpu.CompilerParams(
            collective_id=collective_id, has_side_effects=True, vmem_limit_bytes=60 << 20
        ),
        name="sum_grads",
    )(*shaped)
    return [s.reshape(s.shape[0] * s.shape[1], s.shape[2]) for s in sums]


def body(
    hidden_in,
    attn_gain,
    w_query,
    key_weight,
    value_weight,
    w_out,
    ffn_gain,
    w_gate,
    w_up,
    w_down,
    cotangent,
):
    ws, ctx = lax.axis_size("ws"), lax.axis_size("ctx")
    local_len, local_seqs, features = hidden_in.shape
    row_count = local_len * local_seqs
    q_heads = w_query.shape[1] // HEAD_DIM
    kv_heads = key_weight.shape[1] // HEAD_DIM
    group = q_heads // kv_heads
    own_heads = kv_heads // ws
    wide = (group + 2) * HEAD_DIM
    q_wide = group * HEAD_DIM
    pairs = ws * local_seqs * own_heads
    copies = ctx // pairs
    depth = features // ws
    positions = lax.axis_index("ctx") * local_len + jnp.arange(local_len, dtype=jnp.int32)
    cosines, sines = rope_tables(positions, group + 1, 1, own_heads)
    cosines = jnp.tile(cosines, (ws * local_seqs, 1))
    sines = jnp.tile(sines, (ws * local_seqs, 1))

    gain_attn = lax.all_gather(attn_gain, "ws", axis=0, tiled=True).astype(F32)
    gain_ffn = lax.all_gather(ffn_gain, "ws", axis=0, tiled=True).astype(F32)
    columns = jnp.concatenate(
        [
            w_query.reshape(depth, kv_heads, q_wide),
            key_weight.reshape(depth, kv_heads, HEAD_DIM),
            value_weight.reshape(depth, kv_heads, HEAD_DIM),
        ],
        axis=-1,
    ).reshape(depth, ws, own_heads * wide)
    w_qkv = lax.all_to_all(columns, "ws", 1, 0, tiled=False).reshape(features, own_heads * wide)
    hidden_units = w_gate.shape[1] // ws
    gate = lax.all_to_all(w_gate.reshape(depth, ws, hidden_units), "ws", 1, 0).reshape(features, hidden_units)
    up = lax.all_to_all(w_up.reshape(depth, ws, hidden_units), "ws", 1, 0).reshape(features, hidden_units)

    inputs = jnp.swapaxes(hidden_in, 0, 1).reshape(row_count, features).astype(F32)
    grad_low = jnp.swapaxes(cotangent, 0, 1).reshape(row_count, features)
    attn_unit, attn_factor = normalize(inputs)
    normed_attn = gather_rows((attn_unit * gain_attn).astype(BF))
    grad_low_all = gather_rows(grad_low)

    raw = dot(normed_attn, w_qkv)
    qkv = (raw * cosines + swap_halves(raw) * sines).astype(BF)

    def to_pairs(rows):
        width = rows.shape[1] // own_heads
        blocks = rows.reshape(ws * local_seqs, local_len, own_heads, width)
        blocks = jnp.swapaxes(blocks, 1, 2).reshape(pairs, local_len, width)
        blocks = jnp.concatenate([blocks] * copies, axis=0)
        return lax.all_to_all(blocks, "ctx", 0, 0).reshape(ctx * local_len, width)

    def from_pairs(rows):
        width = rows.shape[1]
        blocks = lax.all_to_all(rows.reshape(ctx, local_len, width), "ctx", 0, 0)
        first = lax.axis_index("ctx") // pairs * pairs
        blocks = lax.dynamic_slice_in_dim(blocks, first, pairs, 0)
        blocks = blocks.reshape(ws * local_seqs, own_heads, local_len, width)
        return jnp.swapaxes(blocks, 1, 2).reshape(ws * row_count, own_heads * width)

    pair = to_pairs(qkv)
    attended, top, total = attend_pair(pair, group)
    flat = jnp.swapaxes(attended, 1, 2).reshape(ctx * local_len, q_wide)
    attn_low = from_pairs(flat.astype(BF))
    residual = inputs + sum_rows(dot(attn_low, w_out), ws)
    ffn_unit, ffn_factor = normalize(residual)
    normed_ffn = gather_rows((ffn_unit * gain_ffn).astype(BF))
    gate_proj, up_proj = dot(normed_ffn, gate), dot(normed_ffn, up)
    sigmoid_gate = jax.nn.sigmoid(gate_proj)
    activation = gate_proj * sigmoid_gate
    hidden = (activation * up_proj).astype(BF)
    output = (residual + sum_rows(dot(hidden, w_down), ws)).astype(BF)
    grad_hidden = against(grad_low_all, w_down)
    grad_up = (grad_hidden * activation).astype(BF)
    grad_gate = (
        grad_hidden * up_proj * sigmoid_gate * (1.0 + gate_proj * (1.0 - sigmoid_gate))
    ).astype(BF)
    grad_normed_ffn = sum_rows(against(grad_gate, gate) + against(grad_up, up), ws)
    grad_ffn_gain = jnp.sum(grad_normed_ffn * ffn_unit, axis=0)
    grad_residual = grad_low.astype(F32) + norm_back(
        grad_normed_ffn * gain_ffn, ffn_unit, ffn_factor
    )
    grad_branch = gather_rows(grad_residual.astype(BF))
    grad_attended = against(grad_branch, w_out).astype(BF)
    grad_q, grad_k, grad_v = attend_pair_back(
        pair, to_pairs(grad_attended), attended, top, total, group
    )
    scale = HEAD_DIM**-0.5
    back = jnp.concatenate([grad_q * scale, grad_k * scale, grad_v], axis=-1)
    whole = jnp.arange(ctx * local_len, dtype=jnp.int32)
    pair_cos, pair_sin = rope_tables(whole, group + 1, 1, 1)
    back = (back * pair_cos - swap_halves(back) * pair_sin).astype(BF)
    grad_qkv = from_pairs(back)
    grad_normed_attn = sum_rows(against(grad_qkv, w_qkv), ws)
    grad_attn_gain = jnp.sum(grad_normed_attn * attn_unit, axis=0)
    grad_input = grad_residual + norm_back(grad_normed_attn * gain_attn, attn_unit, attn_factor)

    sums = sum_grads(
        [
            outer_sum(hidden, grad_low_all).astype(BF),
            outer_sum(normed_ffn, grad_gate).astype(BF),
            outer_sum(normed_ffn, grad_up).astype(BF),
            outer_sum(attn_low, grad_branch).astype(BF),
            outer_sum(normed_attn, grad_qkv).astype(BF),
        ],
        (False, True, True, False, True),
        (32, 16, 16, 32, 16),
        ws,
        ctx // 2,
        0,
    )
    g_down, g_gate, g_up, g_out, g_qkv = sums
    g_qkv = g_qkv.reshape(depth, kv_heads, wide)
    sums = (
        g_qkv[..., :q_wide].reshape(depth, q_heads * HEAD_DIM),
        g_qkv[..., q_wide : q_wide + HEAD_DIM].reshape(depth, kv_heads * HEAD_DIM),
        g_qkv[..., q_wide + HEAD_DIM :].reshape(depth, kv_heads * HEAD_DIM),
        g_out,
        g_gate,
        g_up,
        g_down,
    )
    gains = lax.psum(
        lax.psum_scatter(
            jnp.stack([grad_attn_gain, grad_ffn_gain], axis=1), "ws", scatter_dimension=0, tiled=True
        ),
        "ctx",
    )
    sums = [s.astype(F32) for s in sums]

    def place(rows):
        return jnp.swapaxes(rows.reshape(local_seqs, local_len, features), 0, 1)

    return (
        place(output),
        place(grad_input),
        gains[:, 0],
        *sums[:4],
        gains[:, 1],
        *sums[4:],
    )


def solution(mesh):
    tokens, rows, one = P("ctx", "ws", None), P("ws", None), P("ws")
    return jax.shard_map(
        body,
        mesh=mesh,
        in_specs=(tokens, one, rows, rows, rows, rows, one, rows, rows, rows, tokens),
        out_specs=(tokens, tokens, one, rows, rows, rows, rows, one, rows, rows, rows),
        check_vma=False,
    )
```

```python
import functools

import jax
import jax.numpy as jnp
import numpy as np
from jax import lax
from jax.experimental import pallas as pl
from jax.experimental.pallas import tpu as pltpu
from jax.sharding import PartitionSpec as P

HEAD_DIM = 96
EPSILON = 1e-05
ROPE_BASE = 100000.0
MASK_FILL = -1e30
BF = jnp.bfloat16
F32 = jnp.float32


def normalize(matrix):
    factor = lax.rsqrt(jnp.mean(matrix * matrix, axis=-1, keepdims=True) + EPSILON)
    return (matrix * factor, factor)


def norm_back(grad_normed, normed, factor):
    return factor * (grad_normed - normed * jnp.mean(grad_normed * normed, axis=-1, keepdims=True))


def rope_tables(length, rotated_heads, plain_heads):
    half = HEAD_DIM // 2
    frequency = np.float32(ROPE_BASE) ** (-(np.arange(half, dtype=np.float32) * 2.0 / HEAD_DIM))
    angles = np.arange(length, dtype=np.float32)[:, None] * frequency[None, :].astype(np.float32)
    cosine, sine = np.cos(angles), np.sin(angles)
    plain = np.zeros((length, plain_heads * HEAD_DIM), np.float32)
    cosines = [cosine, cosine] * rotated_heads + [plain + 1.0]
    sines = [-sine, sine] * rotated_heads + [plain]
    return (
        jnp.asarray(np.concatenate(cosines, axis=-1), F32),
        jnp.asarray(np.concatenate(sines, axis=-1), F32),
    )


def swap_halves(vectors):
    rows, width = vectors.shape
    half = HEAD_DIM // 2
    parts = vectors.reshape(rows, width // HEAD_DIM, 2, half)
    return jnp.flip(parts, axis=2).reshape(rows, width)


def against(left, weight):
    return lax.dot_general(
        left, weight, (((1,), (1,)), ((), ())), preferred_element_type=F32
    )


def outer_sum(left, right):
    return lax.dot_general(
        left, right, (((0,), (0,)), ((), ())), preferred_element_type=F32
    )


def dot(left, right):
    return jnp.dot(left, right, preferred_element_type=F32)


def gather_rows(block):
    return lax.all_gather(block, "ws", axis=0, tiled=True)


def sum_rows(partial, ws):
    blocks = partial.astype(BF).reshape(ws, partial.shape[0] // ws, partial.shape[1])
    return jnp.sum(lax.all_to_all(blocks, "ws", 0, 0).astype(F32), axis=0)


def attend_pair_back(qkv, grad, attended, top, total, group):
    length = qkv.shape[0]
    width = group * HEAD_DIM
    query = qkv[:, :width].reshape(length, group, HEAD_DIM)
    grad = grad.reshape(length, group, HEAD_DIM)
    key = qkv[:, width : width + HEAD_DIM]
    value = qkv[:, width + HEAD_DIM :]
    rows = min(512, length)

    def one(carried, inputs):
        index, out, peak, sums = inputs
        grad_key, grad_value = carried
        start = index * rows
        part = lax.dynamic_slice_in_dim(query, start, rows, 0)
        grad_part = lax.dynamic_slice_in_dim(grad, start, rows, 0)
        scores = jnp.einsum("qjd,kd->jqk", part, key, preferred_element_type=F32) * HEAD_DIM**-0.5
        allowed = (start + jnp.arange(rows))[:, None] >= jnp.arange(length)[None, :]
        scores = jnp.where(allowed, scores, MASK_FILL)
        weights = jnp.exp(scores - peak)
        wide = jnp.swapaxes(grad_part.astype(F32), 0, 1)
        delta = jnp.sum(wide * out, axis=-1, keepdims=True)
        grad_probs = jnp.einsum("qjd,kd->jqk", grad_part, value, preferred_element_type=F32)
        grad_scores = (weights / sums * (grad_probs - delta)).astype(BF)
        grad_query = jnp.einsum("jqk,kd->qjd", grad_scores, key, preferred_element_type=F32)
        grad_key = grad_key + jnp.einsum(
            "jqk,qjd->kd", grad_scores, part, preferred_element_type=F32
        )
        grad_value = grad_value + jnp.einsum(
            "jqk,jqd->kd", weights.astype(BF), (wide / sums).astype(BF), preferred_element_type=F32
        )
        return (grad_key, grad_value), grad_query

    zero = jnp.zeros((length, HEAD_DIM), F32)
    (grad_key, grad_value), grad_query = lax.scan(
        one, (zero, zero), (jnp.arange(length // rows), attended, top, total)
    )
    return grad_query.reshape(length, width), grad_key, grad_value


SKEW = 2
MESH = pl.DeviceIdType.MESH


def remote(src, dst, send_sem, recv_sem, device):
    return pltpu.make_async_remote_copy(
        src_ref=src, dst_ref=dst, send_sem=send_sem, recv_sem=recv_sem,
        device_id=device, device_id_type=MESH,
    )


def grads_kernel(ws, line, moved, rows, *refs):
    count = len(moved)
    parts, outs = refs[:count], refs[count : 2 * count]
    scratch = refs[2 * count :]
    sib_buf, stage, acc, red_in = (scratch[i * count : (i + 1) * count] for i in range(4))
    sems = scratch[4 * count : 10 * count]
    red_send, red_recv, bc_send, bc_recv, core_send, core_recv = (
        sems[i * count : (i + 1) * count] for i in range(6)
    )
    sib_send, sib_recv, mv_send, mv_recv, loc_sem, line_sem = scratch[10 * count :]
    c, w = lax.axis_index("ctx"), lax.axis_index("ws")
    core = lax.rem(c, 2)
    place = c // 2
    sibling = (c + 1 - 2 * core, w)
    before, after = (c - 2, w), (c + 2, w)
    peers = [(c, lax.rem(w + i, ws)) for i in range(1, ws)]

    barrier = pltpu.get_barrier_semaphore()
    for device in peers + [sibling]:
        pl.semaphore_signal(barrier, inc=1, device_id=device, device_id_type=MESH)

    @pl.when(place > 0)
    def _():
        pl.semaphore_signal(barrier, inc=1, device_id=before, device_id_type=MESH)

    @pl.when(place < line - 1)
    def _():
        pl.semaphore_signal(barrier, inc=1, device_id=after, device_id_type=MESH)

    inner = (place > 0).astype(jnp.int32) + (place < line - 1).astype(jnp.int32)
    pl.semaphore_wait(barrier, ws + inner)

    siblings = []
    for i in range(count):
        half = parts[i].at[:, 1 - core] if moved[i] else parts[i].at[1 - core]
        siblings.append(remote(half, sib_buf[i], sib_send.at[i], sib_recv.at[i], sibling))
        siblings[i].start()

    own_columns = [
        pl.ds(pl.multiple_of(w * parts[i].shape[-1], 128), parts[i].shape[-1]) for i in range(count)
    ]

    def move_of(i, step):
        owner = lax.rem(w + step, ws)
        return remote(
            stage[i].at[owner], acc[i].at[:, own_columns[i]],
            mv_send.at[i, step], mv_recv.at[i, step], (c, owner),
        )

    def keep_of(i):
        return pltpu.make_async_copy(stage[i].at[w], acc[i].at[:, own_columns[i]], loc_sem.at[i])

    def share(i):
        siblings[i].wait_recv()
        for step in list(range(1, ws)) + [0]:
            owner = lax.rem(w + step, ws)
            total = parts[i][owner, core].astype(F32) + sib_buf[i][owner].astype(F32)
            stage[i][owner] = total.astype(BF)
            if step:
                move_of(i, step).start()
            else:
                keep_of(i).start()

    def settle(i):
        for step in range(1, ws):
            move_of(i, step).wait_recv()
        keep_of(i).wait()

    def chunk(ref, i, j):
        return ref.at[pl.ds(pl.multiple_of(j * rows[i], rows[i]), rows[i]), :]

    def local(i, j):
        block = chunk(acc[i], i, j)[...].astype(F32)
        if moved[i]:
            return block
        here = chunk(parts[i].at[core], i, j)[...].astype(F32)
        return here + chunk(sib_buf[i], i, j)[...].astype(F32)

    def reduce_chunk(i, j, odd):
        start = (place == 0) if odd else (place == line - 1)
        end = (place == line - 1) if odd else (place == 0)
        step = remote(
            chunk(acc[i], i, j), chunk(red_in[i], i, j),
            red_send[i].at[j], red_recv[i].at[j], after if odd else before,
        )
        final = chunk(outs[i].at[core], i, j)
        down = remote(
            final, final, bc_send[i].at[j], bc_recv[i].at[j], before if odd else after
        )

        @pl.when(start)
        def _():
            if not moved[i]:
                chunk(acc[i], i, j)[...] = local(i, j).astype(BF)
            step.start()

        @pl.when(jnp.logical_not(start))
        def _():
            step.wait_recv()
            total = local(i, j) + chunk(red_in[i], i, j)[...].astype(F32)
            total = total.astype(BF)

            @pl.when(jnp.logical_not(end))
            def _():
                chunk(acc[i], i, j)[...] = total
                step.start()

            @pl.when(end)
            def _():
                chunk(outs[i].at[core], i, j)[...] = total
                down.start()

    def spread_chunk(i, j, odd):
        start = (place == line - 1) if odd else (place == 0)
        end = (place == 0) if odd else (place == line - 1)
        final = chunk(outs[i].at[core], i, j)
        down = remote(
            final, final, bc_send[i].at[j], bc_recv[i].at[j], before if odd else after
        )
        across = remote(final, final, core_send[i].at[j], core_recv[i].at[j], sibling)

        @pl.when(jnp.logical_not(start))
        def _():
            down.wait_recv()

            @pl.when(jnp.logical_not(end))
            def _():
                down.start()

        across.start()

    first, total_chunks = [], 0
    for i in range(count):
        first.append(total_chunks)
        total_chunks += acc[i].shape[0] // rows[i] // 2
    lasts = first[1:] + [total_chunks]
    hops = (line - 1 - place, place)
    skew = SKEW

    def step_at(t, _):
        for i in range(count):
            if moved[i]:
                @pl.when(t == max(first[i] - 8, 0))
                def _():
                    share(i)

                @pl.when(t == first[i])
                def _():
                    settle(i)
            else:
                @pl.when(t == first[i])
                def _():
                    siblings[i].wait_recv()

        for odd in range(2):
            at = t - skew * hops[odd]
            back = t - skew * (2 * (line - 1) - hops[odd])
            for i in range(count):
                @pl.when((at >= first[i]) & (at < lasts[i]))
                def _():
                    reduce_chunk(i, 2 * (at - first[i]) + odd, odd)

                @pl.when((back >= first[i]) & (back < lasts[i]))
                def _():
                    spread_chunk(i, 2 * (back - first[i]) + odd, odd)

        return 0

    lax.fori_loop(0, total_chunks + 2 * skew * (line - 1), step_at, 0)

    for i in range(count):
        chunks = acc[i].shape[0] // rows[i]

        def finish_pair(p, _):
            for odd in range(2):
                j = 2 * p + odd
                reduce_end = (place == line - 1) if odd else (place == 0)
                spread_end = (place == 0) if odd else (place == line - 1)
                final = chunk(outs[i].at[core], i, j)
                there = chunk(outs[i].at[1 - core], i, j)
                step = remote(
                    chunk(acc[i], i, j), chunk(red_in[i], i, j),
                    red_send[i].at[j], red_recv[i].at[j], before,
                )
                down = remote(final, final, bc_send[i].at[j], bc_recv[i].at[j], before)
                across = remote(there, there, core_send[i].at[j], core_recv[i].at[j], sibling)

                @pl.when(jnp.logical_not(reduce_end))
                def _():
                    step.wait_send()

                @pl.when(jnp.logical_not(spread_end))
                def _():
                    down.wait_send()

                across.wait_send()
                across.wait_recv()
            return 0

        lax.fori_loop(0, chunks // 2, finish_pair, 0)
    for i in range(count):
        siblings[i].wait_send()
        if moved[i]:
            for step in range(1, ws):
                move_of(i, step).wait_send()


def sum_grads(parts, moved, rows, ws, line, collective_id):
    shaped, outs, sib, stage, acc, red, counts = [], [], [], [], [], [], []
    for part, is_moved in zip(parts, moved):
        n = part.shape[1]
        half = part.shape[0] // (2 * ws if is_moved else 2)
        wide = ws * n if is_moved else n
        lead = (ws,) if is_moved else ()
        shaped.append(part.reshape(lead + (2, half, n)))
        outs.append(jax.ShapeDtypeStruct((2, half, wide), BF))
        sib.append(pltpu.VMEM(lead + (half, n), BF))
        stage.append(pltpu.VMEM(lead + (half, n) if is_moved else (16, 128), BF))
        acc.append(pltpu.VMEM((half, wide), BF))
        red.append(pltpu.VMEM((half, wide), BF))
    counts = [a.shape[0] // r for a, r in zip(acc, rows)]
    dma = pltpu.SemaphoreType.DMA
    sems = [dma((n,)) for _ in range(6) for n in counts]
    k = len(parts)
    last = [dma((k,)), dma((k,)), dma((k, ws)), dma((k, ws)), dma((k,)), dma((1,))]
    vmem = pl.BlockSpec(memory_space=pltpu.VMEM)
    sums = pl.pallas_call(
        functools.partial(grads_kernel, ws, line, moved, rows),
        out_shape=outs,
        in_specs=[vmem] * k,
        out_specs=[vmem] * k,
        scratch_shapes=sib + stage + acc + red + sems + last,
        compiler_params=pltpu.CompilerParams(
            collective_id=collective_id, has_side_effects=True, vmem_limit_bytes=60 << 20
        ),
        name="sum_grads",
    )(*shaped)
    return [s.reshape(s.shape[0] * s.shape[1], s.shape[2]) for s in sums]


def dma(*shape):
    return pltpu.SemaphoreType.DMA(shape)


def at_rows(ref, start, size):
    return ref.at[pl.ds(pl.multiple_of(start, size), size), :]


def greet(devices):
    barrier = pltpu.get_barrier_semaphore()
    for device in devices:
        pl.semaphore_signal(barrier, inc=1, device_id=device, device_id_type=MESH)
    pl.semaphore_wait(barrier, len(devices))


def swap_lanes(vectors):
    lanes = lax.broadcasted_iota(jnp.int32, vectors.shape, 1)
    width, half = vectors.shape[1], HEAD_DIM // 2
    first = lax.rem(lanes, HEAD_DIM) < half
    return jnp.where(first, pltpu.roll(vectors, width - half, 1), pltpu.roll(vectors, half, 1))


def front_kernel(
    ws, ctx, own_heads, group,
    x, gains, wq, wk, wv, gate, up, cot, cosines, sines,
    normed, w_all, q_out, k_out, v_out, pack, attn_in, gate_all, up_all, cot_all, gains_all,
    x_all, g_in, w_stage, raw, qkv_stage, pair, attn_stage, cos, sin,
    x_sem, g_sem, w_sem, wf_sem, ffn_sem, ff_sem, cot_sem, pair_sem, back_sem, own_sem,
):
    c, w = lax.axis_index("ctx"), lax.axis_index("ws")
    core = lax.rem(c, 2)
    sibling = (c + 1 - 2 * core, w)
    rows = x.shape[0]
    depth = wq.shape[0]
    half = depth // 2
    q_wide = group * HEAD_DIM
    wide = q_wide + 2 * HEAD_DIM
    pairs = ws * own_heads
    units = gate_all.shape[1]
    peer = [lax.rem(w + i, ws) for i in range(ws)]
    origin = [lax.rem(w + ws - i, ws) for i in range(ws)]

    def rope_copy(i):
        table, kept = ((cosines, cos), (sines, sin))[i]
        return pltpu.make_async_copy(at_rows(table, c * rows, rows), kept, own_sem.at[i])

    rope_copy(0).start()
    rope_copy(1).start()
    near = [(lax.rem(c + i, ctx), w) for i in range(1, ctx)]
    greet(near + [(c, peer[i]) for i in range(1, ws)])

    def send_gain(i):
        return remote(gains, g_in.at[w], g_sem.at[0, i], g_sem.at[1, i], (c, peer[i]))

    def send_x(i):
        return remote(x, x_all.at[w], x_sem.at[0, i], x_sem.at[1, i], (c, peer[i]))

    def send_w(i):
        return remote(
            at_rows(w_stage.at[peer[i]], core * half, half),
            at_rows(w_all.at[w], core * half, half),
            w_sem.at[0, i], w_sem.at[1, i], (c, peer[i]),
        )

    def pass_w(i):
        block = at_rows(w_all.at[origin[i]], core * half, half)
        return remote(block, block, wf_sem.at[0, i], wf_sem.at[1, i], sibling)

    def send_ffn(which, i):
        held, everyone = ((gate, gate_all), (up, up_all))[which]
        columns = pl.ds(pl.multiple_of(peer[i] * units, 128), units)
        return remote(
            held.at[pl.ds(pl.multiple_of(core * half, half), half), columns],
            at_rows(everyone, w * depth + core * half, half),
            ffn_sem.at[0, which, i], ffn_sem.at[1, which, i], (c, peer[i]),
        )

    def pass_ffn(which, i):
        block = at_rows((gate_all, up_all)[which], origin[i] * depth + core * half, half)
        return remote(block, block, ff_sem.at[0, which, i], ff_sem.at[1, which, i], sibling)

    def keep_ffn(which):
        held, everyone = ((gate, gate_all), (up, up_all))[which]
        columns = pl.ds(pl.multiple_of(w * units, 128), units)
        return pltpu.make_async_copy(
            held.at[:, columns], at_rows(everyone, w * depth, depth), own_sem.at[2 + which]
        )

    def send_cot(i):
        return remote(cot, cot_all.at[w], cot_sem.at[0, i], cot_sem.at[1, i], (c, peer[i]))

    def keep_cot():
        return pltpu.make_async_copy(cot, cot_all.at[w], own_sem.at[4])

    def send_pair(i):
        to = lax.rem(c + i, ctx)
        return remote(
            qkv_stage.at[lax.rem(to, pairs)], pair.at[c],
            pair_sem.at[0, i], pair_sem.at[1, i], (to, w),
        )

    first_back = c // pairs * pairs
    own_pair = lax.rem(c, pairs)

    def back_copy(to, i):
        return remote(
            attn_stage.at[to], attn_in.at[own_pair],
            back_sem.at[0, i], back_sem.at[1, i], (to, w),
        )

    for i in range(1, ws):
        send_gain(i).start()
    for i in range(1, ws):
        send_x(i).start()
    keep_ffn(0).start()
    keep_ffn(1).start()
    keep_cot().start()
    for d in range(ws):
        for j in range(own_heads):
            h = d * own_heads + j
            w_stage[d, :, j * wide : (j + 1) * wide] = jnp.concatenate(
                [
                    wq[:, h * q_wide : (h + 1) * q_wide],
                    wk[:, h * HEAD_DIM : (h + 1) * HEAD_DIM],
                    wv[:, h * HEAD_DIM : (h + 1) * HEAD_DIM],
                ],
                axis=1,
            )
    for i in range(1, ws):
        send_w(i).start()
    w_all[w] = w_stage[w]
    total_gain = gains[...]
    for i in range(1, ws):
        send_gain(i).wait_recv()
        total_gain = total_gain + g_in[origin[i]]
    gains_all[...] = total_gain
    gain = total_gain[0:1]

    def norm_block(index, block):
        wide_block = block.astype(F32)
        factor = lax.rsqrt(jnp.mean(wide_block * wide_block, axis=-1, keepdims=True) + EPSILON)
        normed[index] = (wide_block * factor * gain).astype(BF)

    norm_block(w, x[...])
    for i in range(1, ws):
        send_x(i).wait_recv()
        norm_block(origin[i], x_all[origin[i]])
    for i in range(1, ws):
        send_w(i).wait_recv()
        pass_w(i).start()
    for i in range(1, ws):
        pass_w(i).wait_recv()
    for i in range(1, ws):
        for which in range(2):
            send_ffn(which, i).start()
    for i in range(1, ws):
        send_cot(i).start()

    left = normed[...].reshape(ws * rows, normed.shape[2])
    step = 256 if raw.shape[1] % 256 == 0 else 128
    for n in range(0, raw.shape[1], step):
        right = w_all[:, :, n : n + step].reshape(ws * depth, step)
        raw[:, n : n + step] = jnp.dot(left, right, preferred_element_type=F32)
    rope_copy(0).wait()
    rope_copy(1).wait()
    for s in range(ws):
        for j in range(own_heads):
            block = raw[s * rows : (s + 1) * rows, j * wide : (j + 1) * wide]
            turned = block * cos[...] + swap_lanes(block) * sin[...]
            qkv_stage[s * own_heads + j] = turned.astype(BF)
    for i in range(1, ctx):
        send_pair(i).start()
    pair[c] = qkv_stage[own_pair]

    def split(index):
        block = pair[index]
        here = pl.ds(pl.multiple_of(index * rows, rows), rows)
        for g in range(group):
            q_out[g, here, :] = block[:, g * HEAD_DIM : (g + 1) * HEAD_DIM]
        k_out[here, :] = block[:, q_wide : q_wide + HEAD_DIM]
        v_out[here, :] = block[:, q_wide + HEAD_DIM :]

    split(c)
    for i in range(1, ctx):
        from_c = lax.rem(c + ctx - i, ctx)
        send_pair(i).wait_recv()
        split(from_c)

    length = ctx * rows
    span = min(256, length)
    lane = lax.broadcasted_iota(jnp.int32, (span, HEAD_DIM), 1)

    def attend(start, keys, diagonal):
        here = pl.ds(start, span)
        heads = []
        allowed = start + lax.broadcasted_iota(
            jnp.int32, (span, keys), 0
        ) >= lax.broadcasted_iota(jnp.int32, (span, keys), 1)
        for g in range(group):
            scores = lax.dot_general(
                q_out[g, here, :], k_out[0:keys, :], (((1,), (1,)), ((), ())),
                preferred_element_type=F32,
            ) * HEAD_DIM**-0.5
            scores = jnp.where(allowed, scores, MASK_FILL)
            top = jnp.max(scores, axis=1, keepdims=True)
            weights = jnp.exp(scores - top)
            total = jnp.sum(weights, axis=1, keepdims=True)
            mixed = jnp.dot(
                weights.astype(BF), v_out[0:keys, :], preferred_element_type=F32
            ) / total
            pack[g, here, 0:HEAD_DIM] = mixed
            pack[g, here, HEAD_DIM:128] = jnp.where(
                lane[:, : 128 - HEAD_DIM] == 0, top, total
            )
            heads.append(mixed)
        low = jnp.concatenate(heads, axis=1).astype(BF)
        for b in range(span // rows):
            attn_stage[start // rows + b] = low[b * rows : (b + 1) * rows]

    if length <= 1024:
        for start in range(0, length, span):
            attend(start, start + span, start)
    else:

        def attend_at(index, _):
            attend(pl.multiple_of(index * span, span), length, 0)
            return 0

        lax.fori_loop(0, length // span, attend_at, 0)
    for i in range(1, pairs):
        back_copy(first_back + lax.rem(own_pair + i, pairs), i).start()
    attn_in[own_pair] = attn_stage[c]

    for i in range(1, ws):
        for which in range(2):
            send_ffn(which, i).wait_recv()
            pass_ffn(which, i).start()
    for i in range(1, pairs):
        source = lax.rem(own_pair + pairs - i, pairs)
        arriving = remote(
            attn_stage.at[c], attn_in.at[source],
            back_sem.at[0, i], back_sem.at[1, i], (first_back + source, w),
        )
        arriving.wait_recv()
    for i in range(1, ws):
        for which in range(2):
            pass_ffn(which, i).wait_recv()
        send_cot(i).wait_recv()
    keep_ffn(0).wait()
    keep_ffn(1).wait()
    keep_cot().wait()
    for i in range(1, ws):
        send_gain(i).wait_send()
        send_x(i).wait_send()
        send_w(i).wait_send()
        pass_w(i).wait_send()
        send_cot(i).wait_send()
        for which in range(2):
            send_ffn(which, i).wait_send()
            pass_ffn(which, i).wait_send()
    for i in range(1, ctx):
        send_pair(i).wait_send()
    for i in range(1, pairs):
        back_copy(first_back + lax.rem(own_pair + i, pairs), i).wait_send()


def front(x, gains, wq, wk, wv, gate, up, cot, cosines, sines, ws, ctx, own_heads, group):
    rows, features = x.shape
    depth = wq.shape[0]
    q_wide = group * HEAD_DIM
    wide = q_wide + 2 * HEAD_DIM
    pairs = ws * own_heads
    length = ctx * rows
    units = gate.shape[1] // ws
    vmem, anywhere = pl.BlockSpec(memory_space=pltpu.VMEM), pl.BlockSpec(memory_space=pl.ANY)
    shape = jax.ShapeDtypeStruct
    return pl.pallas_call(
        functools.partial(front_kernel, ws, ctx, own_heads, group),
        out_shape=[
            shape((ws, rows, features), BF),
            shape((ws, depth, own_heads * wide), BF),
            shape((group, length, HEAD_DIM), BF),
            shape((length, HEAD_DIM), BF),
            shape((length, HEAD_DIM), BF),
            shape((group, length, 128), F32),
            shape((pairs, rows, q_wide), BF),
            shape((features, units), BF),
            shape((features, units), BF),
            shape((ws, rows, features), BF),
            shape(gains.shape, F32),
        ],
        in_specs=[vmem] * 5 + [anywhere] * 5,
        out_specs=[vmem] * 7 + [anywhere] * 3 + [vmem],
        scratch_shapes=[
            pltpu.VMEM((ws, rows, features), BF),
            pltpu.VMEM((ws,) + gains.shape, F32),
            pltpu.VMEM((ws, depth, own_heads * wide), BF),
            pltpu.VMEM((ws * rows, own_heads * wide), F32),
            pltpu.VMEM((pairs, rows, wide), BF),
            pltpu.VMEM((ctx, rows, wide), BF),
            pltpu.VMEM((ctx, rows, q_wide), BF),
            pltpu.VMEM((rows, wide), F32),
            pltpu.VMEM((rows, wide), F32),
            dma(2, ws), dma(2, ws), dma(2, ws), dma(2, ws), dma(2, 2, ws), dma(2, 2, ws),
            dma(2, ws), dma(2, ctx), dma(2, pairs), dma(5),
        ],
        compiler_params=pltpu.CompilerParams(
            collective_id=1, has_side_effects=True, vmem_limit_bytes=60 << 20
        ),
        name="front",
    )(x, gains, wq, wk, wv, gate, up, cot, cosines, sines)


def body(
    hidden_in,
    attn_gain,
    w_query,
    key_weight,
    value_weight,
    w_out,
    ffn_gain,
    w_gate,
    w_up,
    w_down,
    cotangent,
):
    ws, ctx = lax.axis_size("ws"), lax.axis_size("ctx")
    local_len, local_seqs, features = hidden_in.shape
    row_count = local_len * local_seqs
    q_heads = w_query.shape[1] // HEAD_DIM
    kv_heads = key_weight.shape[1] // HEAD_DIM
    group = q_heads // kv_heads
    own_heads = kv_heads // ws
    wide = (group + 2) * HEAD_DIM
    q_wide = group * HEAD_DIM
    pairs = ws * local_seqs * own_heads
    copies = ctx // pairs
    depth = features // ws
    cosines, sines = rope_tables(ctx * local_len, group + 1, 1)
    gains = jnp.stack([attn_gain, ffn_gain]).astype(F32)
    gains = lax.dynamic_update_slice(
        jnp.zeros((8, features), F32), gains, (0, lax.axis_index("ws") * depth)
    )
    inputs = hidden_in.reshape(row_count, features)
    grad_low = cotangent.reshape(row_count, features)
    (
        normed_attn, w_qkv, q_pair, k_pair, v_pair, pack, attn_in, gate, up, grad_low_all, gains,
    ) = front(
        inputs, gains, w_query, key_weight, value_weight, w_gate, w_up, grad_low, cosines, sines,
        ws, ctx, own_heads, group,
    )
    inputs = inputs.astype(F32)
    attn_unit, attn_factor = normalize(inputs)
    gain_attn, gain_ffn = gains[0], gains[1]
    normed_attn = normed_attn.reshape(ws * row_count, features)
    grad_low_all = grad_low_all.reshape(ws * row_count, features)
    w_qkv = w_qkv.reshape(features, own_heads * wide)

    def to_pairs(rows):
        width = rows.shape[1] // own_heads
        blocks = rows.reshape(ws * local_seqs, local_len, own_heads, width)
        blocks = jnp.swapaxes(blocks, 1, 2).reshape(pairs, local_len, width)
        blocks = jnp.concatenate([blocks] * copies, axis=0)
        return lax.all_to_all(blocks, "ctx", 0, 0).reshape(ctx * local_len, width)

    def from_pairs(rows):
        width = rows.shape[1]
        blocks = lax.all_to_all(rows.reshape(ctx, local_len, width), "ctx", 0, 0)
        first = lax.axis_index("ctx") // pairs * pairs
        blocks = lax.dynamic_slice_in_dim(blocks, first, pairs, 0)
        blocks = blocks.reshape(ws * local_seqs, own_heads, local_len, width)
        return jnp.swapaxes(blocks, 1, 2).reshape(ws * row_count, own_heads * width)

    pair = jnp.concatenate([q_pair[0], q_pair[1], k_pair, v_pair], axis=1)
    blocks = min(512, ctx * local_len)
    split = (group, ctx * local_len // blocks, blocks)
    attended = jnp.swapaxes(pack[..., :HEAD_DIM].reshape(split + (HEAD_DIM,)), 0, 1)
    top = jnp.swapaxes(pack[..., HEAD_DIM : HEAD_DIM + 1].reshape(split + (1,)), 0, 1)
    total = jnp.swapaxes(pack[..., HEAD_DIM + 1 : HEAD_DIM + 2].reshape(split + (1,)), 0, 1)
    attn_low = jnp.swapaxes(attn_in.reshape(ws, own_heads, local_len, q_wide), 1, 2)
    attn_low = attn_low.reshape(ws * row_count, own_heads * q_wide)
    residual = inputs + sum_rows(dot(attn_low, w_out), ws)
    ffn_unit, ffn_factor = normalize(residual)
    normed_ffn = gather_rows((ffn_unit * gain_ffn).astype(BF))
    gate_proj, up_proj = dot(normed_ffn, gate), dot(normed_ffn, up)
    sigmoid_gate = jax.nn.sigmoid(gate_proj)
    activation = gate_proj * sigmoid_gate
    hidden = (activation * up_proj).astype(BF)
    output = (residual + sum_rows(dot(hidden, w_down), ws)).astype(BF)
    grad_hidden = against(grad_low_all, w_down)
    grad_up = (grad_hidden * activation).astype(BF)
    grad_gate = (
        grad_hidden * up_proj * sigmoid_gate * (1.0 + gate_proj * (1.0 - sigmoid_gate))
    ).astype(BF)
    grad_normed_ffn = sum_rows(against(grad_gate, gate) + against(grad_up, up), ws)
    grad_ffn_gain = jnp.sum(grad_normed_ffn * ffn_unit, axis=0)
    grad_residual = grad_low.astype(F32) + norm_back(
        grad_normed_ffn * gain_ffn, ffn_unit, ffn_factor
    )
    grad_branch = gather_rows(grad_residual.astype(BF))
    grad_attended = against(grad_branch, w_out).astype(BF)
    grad_q, grad_k, grad_v = attend_pair_back(
        pair, to_pairs(grad_attended), attended, top, total, group
    )
    scale = HEAD_DIM**-0.5
    back = jnp.concatenate([grad_q * scale, grad_k * scale, grad_v], axis=-1)
    pair_cos, pair_sin = cosines, sines
    back = (back * pair_cos - swap_halves(back) * pair_sin).astype(BF)
    grad_qkv = from_pairs(back)
    grad_normed_attn = sum_rows(against(grad_qkv, w_qkv), ws)
    grad_attn_gain = jnp.sum(grad_normed_attn * attn_unit, axis=0)
    grad_input = grad_residual + norm_back(grad_normed_attn * gain_attn, attn_unit, attn_factor)

    sums = sum_grads(
        [
            outer_sum(hidden, grad_low_all).astype(BF),
            outer_sum(normed_ffn, grad_gate).astype(BF),
            outer_sum(normed_ffn, grad_up).astype(BF),
            outer_sum(attn_low, grad_branch).astype(BF),
            outer_sum(normed_attn, grad_qkv).astype(BF),
        ],
        (False, True, True, False, True),
        (32, 16, 16, 32, 16),
        ws,
        ctx // 2,
        0,
    )
    g_down, g_gate, g_up, g_out, g_qkv = sums
    g_qkv = g_qkv.reshape(depth, kv_heads, wide)
    sums = (
        g_qkv[..., :q_wide].reshape(depth, q_heads * HEAD_DIM),
        g_qkv[..., q_wide : q_wide + HEAD_DIM].reshape(depth, kv_heads * HEAD_DIM),
        g_qkv[..., q_wide + HEAD_DIM :].reshape(depth, kv_heads * HEAD_DIM),
        g_out,
        g_gate,
        g_up,
        g_down,
    )
    gains = lax.psum(
        lax.psum_scatter(
            jnp.stack([grad_attn_gain, grad_ffn_gain], axis=1), "ws", scatter_dimension=0, tiled=True
        ),
        "ctx",
    )
    sums = [s.astype(F32) for s in sums]

    def place(rows):
        return jnp.swapaxes(rows.reshape(local_seqs, local_len, features), 0, 1)

    return (
        place(output),
        place(grad_input),
        gains[:, 0],
        *sums[:4],
        gains[:, 1],
        *sums[4:],
    )


def solution(mesh):
    tokens, rows, one = P("ctx", "ws", None), P("ws", None), P("ws")
    return jax.shard_map(
        body,
        mesh=mesh,
        in_specs=(tokens, one, rows, rows, rows, rows, one, rows, rows, rows, tokens),
        out_specs=(tokens, tokens, one, rows, rows, rows, rows, one, rows, rows, rows),
        check_vma=False,
    )
```

```python
import functools

import jax
import jax.numpy as jnp
import numpy as np
from jax import lax
from jax.experimental import pallas as pl
from jax.experimental.pallas import tpu as pltpu
from jax.sharding import PartitionSpec as P

HEAD_DIM = 96
EPSILON = 1e-05
ROPE_BASE = 100000.0
MASK_FILL = -1e30
BF = jnp.bfloat16
F32 = jnp.float32


def rope_tables(length, rotated_heads, plain_heads):
    half = HEAD_DIM // 2
    frequency = np.float32(ROPE_BASE) ** (-(np.arange(half, dtype=np.float32) * 2.0 / HEAD_DIM))
    angles = np.arange(length, dtype=np.float32)[:, None] * frequency[None, :].astype(np.float32)
    cosine, sine = np.cos(angles), np.sin(angles)
    plain = np.zeros((length, plain_heads * HEAD_DIM), np.float32)
    cosines = [cosine, cosine] * rotated_heads + [plain + 1.0]
    sines = [-sine, sine] * rotated_heads + [plain]
    return (
        jnp.asarray(np.concatenate(cosines, axis=-1), F32),
        jnp.asarray(np.concatenate(sines, axis=-1), F32),
    )


MESH = pl.DeviceIdType.MESH


def remote(src, dst, send_sem, recv_sem, device):
    return pltpu.make_async_remote_copy(
        src_ref=src, dst_ref=dst, send_sem=send_sem, recv_sem=recv_sem,
        device_id=device, device_id_type=MESH,
    )


def dma(*shape):
    return pltpu.SemaphoreType.DMA(shape)


def at_rows(ref, start, size):
    return ref.at[pl.ds(pl.multiple_of(start, size), size), :]


def greet(devices):
    barrier = pltpu.get_barrier_semaphore()
    for device in devices:
        pl.semaphore_signal(barrier, inc=1, device_id=device, device_id_type=MESH)
    pl.semaphore_wait(barrier, len(devices))


def swap_lanes(vectors):
    lanes = lax.broadcasted_iota(jnp.int32, vectors.shape, 1)
    width, half = vectors.shape[1], HEAD_DIM // 2
    first = lax.rem(lanes, HEAD_DIM) < half
    return jnp.where(first, pltpu.roll(vectors, width - half, 1), pltpu.roll(vectors, half, 1))


def front_kernel(
    ws, ctx, own_heads, group,
    x, gains, wq, wk, wv, gate, up, cot, cosines, sines,
    normed, w_all, q_out, k_out, v_out, pack, attn_in, gate_all, up_all, cot_all, gains_all,
    x_all, g_in, w_stage, raw, qkv_stage, pair, attn_stage, cos, sin,
    x_sem, g_sem, w_sem, wf_sem, ffn_sem, ff_sem, cot_sem, pair_sem, back_sem, own_sem,
):
    c, w = lax.axis_index("ctx"), lax.axis_index("ws")
    core = lax.rem(c, 2)
    sibling = (c + 1 - 2 * core, w)
    rows = x.shape[0]
    depth = wq.shape[0]
    half = depth // 2
    q_wide = group * HEAD_DIM
    wide = q_wide + 2 * HEAD_DIM
    pairs = ws * own_heads
    units = gate_all.shape[1]
    peer = [lax.rem(w + i, ws) for i in range(ws)]
    origin = [lax.rem(w + ws - i, ws) for i in range(ws)]

    def rope_copy(i):
        table, kept = ((cosines, cos), (sines, sin))[i]
        return pltpu.make_async_copy(at_rows(table, c * rows, rows), kept, own_sem.at[i])

    rope_copy(0).start()
    rope_copy(1).start()
    near = [(lax.rem(c + i, ctx), w) for i in range(1, ctx)]
    greet(near + [(c, peer[i]) for i in range(1, ws)])

    def send_gain(i):
        return remote(gains, g_in.at[w], g_sem.at[0, i], g_sem.at[1, i], (c, peer[i]))

    def send_x(i):
        return remote(x, x_all.at[w], x_sem.at[0, i], x_sem.at[1, i], (c, peer[i]))

    def send_w(i):
        return remote(
            at_rows(w_stage.at[peer[i]], core * half, half),
            at_rows(w_all.at[w], core * half, half),
            w_sem.at[0, i], w_sem.at[1, i], (c, peer[i]),
        )

    def pass_w(i):
        block = at_rows(w_all.at[origin[i]], core * half, half)
        return remote(block, block, wf_sem.at[0, i], wf_sem.at[1, i], sibling)

    def send_ffn(which, i):
        held, everyone = ((gate, gate_all), (up, up_all))[which]
        columns = pl.ds(pl.multiple_of(peer[i] * units, 128), units)
        return remote(
            held.at[pl.ds(pl.multiple_of(core * half, half), half), columns],
            at_rows(everyone, w * depth + core * half, half),
            ffn_sem.at[0, which, i], ffn_sem.at[1, which, i], (c, peer[i]),
        )

    def pass_ffn(which, i):
        block = at_rows((gate_all, up_all)[which], origin[i] * depth + core * half, half)
        return remote(block, block, ff_sem.at[0, which, i], ff_sem.at[1, which, i], sibling)

    def keep_ffn(which):
        held, everyone = ((gate, gate_all), (up, up_all))[which]
        columns = pl.ds(pl.multiple_of(w * units, 128), units)
        return pltpu.make_async_copy(
            held.at[:, columns], at_rows(everyone, w * depth, depth), own_sem.at[2 + which]
        )

    def send_cot(i):
        return remote(cot, cot_all.at[w], cot_sem.at[0, i], cot_sem.at[1, i], (c, peer[i]))

    def keep_cot():
        return pltpu.make_async_copy(cot, cot_all.at[w], own_sem.at[4])

    def send_pair(i):
        to = lax.rem(c + i, ctx)
        return remote(
            qkv_stage.at[lax.rem(to, pairs)], pair.at[c],
            pair_sem.at[0, i], pair_sem.at[1, i], (to, w),
        )

    first_back = c // pairs * pairs
    own_pair = lax.rem(c, pairs)

    def back_copy(to, i):
        return remote(
            attn_stage.at[to], attn_in.at[own_pair],
            back_sem.at[0, i], back_sem.at[1, i], (to, w),
        )

    for i in range(1, ws):
        send_gain(i).start()
    for i in range(1, ws):
        send_x(i).start()
    keep_ffn(0).start()
    keep_ffn(1).start()
    keep_cot().start()
    for d in range(ws):
        for j in range(own_heads):
            h = d * own_heads + j
            w_stage[d, :, j * wide : (j + 1) * wide] = jnp.concatenate(
                [
                    wq[:, h * q_wide : (h + 1) * q_wide],
                    wk[:, h * HEAD_DIM : (h + 1) * HEAD_DIM],
                    wv[:, h * HEAD_DIM : (h + 1) * HEAD_DIM],
                ],
                axis=1,
            )
    for i in range(1, ws):
        send_w(i).start()
    w_all[w] = w_stage[w]
    total_gain = gains[...]
    for i in range(1, ws):
        send_gain(i).wait_recv()
        total_gain = total_gain + g_in[origin[i]]
    gains_all[...] = total_gain
    gain = total_gain[0:1]

    def norm_block(index, block):
        wide_block = block.astype(F32)
        factor = lax.rsqrt(jnp.mean(wide_block * wide_block, axis=-1, keepdims=True) + EPSILON)
        normed[index] = (wide_block * factor * gain).astype(BF)

    norm_block(w, x[...])
    for i in range(1, ws):
        send_x(i).wait_recv()
        norm_block(origin[i], x_all[origin[i]])
    for i in range(1, ws):
        send_w(i).wait_recv()
        pass_w(i).start()
    for i in range(1, ws):
        pass_w(i).wait_recv()
    for i in range(1, ws):
        for which in range(2):
            send_ffn(which, i).start()
    for i in range(1, ws):
        send_cot(i).start()

    left = normed[...].reshape(ws * rows, normed.shape[2])
    step = 256 if raw.shape[1] % 256 == 0 else 128
    for n in range(0, raw.shape[1], step):
        right = w_all[:, :, n : n + step].reshape(ws * depth, step)
        raw[:, n : n + step] = jnp.dot(left, right, preferred_element_type=F32)
    rope_copy(0).wait()
    rope_copy(1).wait()
    for s in range(ws):
        for j in range(own_heads):
            block = raw[s * rows : (s + 1) * rows, j * wide : (j + 1) * wide]
            turned = block * cos[...] + swap_lanes(block) * sin[...]
            qkv_stage[s * own_heads + j] = turned.astype(BF)
    for i in range(1, ctx):
        send_pair(i).start()
    pair[c] = qkv_stage[own_pair]

    def split(index):
        block = pair[index]
        here = pl.ds(pl.multiple_of(index * rows, rows), rows)
        for g in range(group):
            q_out[g, here, :] = block[:, g * HEAD_DIM : (g + 1) * HEAD_DIM]
        k_out[here, :] = block[:, q_wide : q_wide + HEAD_DIM]
        v_out[here, :] = block[:, q_wide + HEAD_DIM :]

    split(c)
    for i in range(1, ctx):
        from_c = lax.rem(c + ctx - i, ctx)
        send_pair(i).wait_recv()
        split(from_c)

    length = ctx * rows
    span = min(256, length)
    lane = lax.broadcasted_iota(jnp.int32, (span, HEAD_DIM), 1)

    def attend(start, keys, diagonal):
        here = pl.ds(start, span)
        heads = []
        allowed = start + lax.broadcasted_iota(
            jnp.int32, (span, keys), 0
        ) >= lax.broadcasted_iota(jnp.int32, (span, keys), 1)
        for g in range(group):
            scores = lax.dot_general(
                q_out[g, here, :], k_out[0:keys, :], (((1,), (1,)), ((), ())),
                preferred_element_type=F32,
            ) * HEAD_DIM**-0.5
            scores = jnp.where(allowed, scores, MASK_FILL)
            top = jnp.max(scores, axis=1, keepdims=True)
            weights = jnp.exp(scores - top)
            total = jnp.sum(weights, axis=1, keepdims=True)
            mixed = jnp.dot(
                weights.astype(BF), v_out[0:keys, :], preferred_element_type=F32
            ) / total
            pack[g, here, 0:HEAD_DIM] = mixed
            pack[g, here, HEAD_DIM:128] = jnp.where(
                lane[:, : 128 - HEAD_DIM] == 0, top, total
            )
            heads.append(mixed)
        low = jnp.concatenate(heads, axis=1).astype(BF)
        for b in range(span // rows):
            attn_stage[start // rows + b] = low[b * rows : (b + 1) * rows]

    if length <= 1024:
        for start in range(0, length, span):
            attend(start, start + span, start)
    else:

        def attend_at(index, _):
            attend(pl.multiple_of(index * span, span), length, 0)
            return 0

        lax.fori_loop(0, length // span, attend_at, 0)
    for i in range(1, pairs):
        back_copy(first_back + lax.rem(own_pair + i, pairs), i).start()
    attn_in[own_pair] = attn_stage[c]

    for i in range(1, ws):
        for which in range(2):
            send_ffn(which, i).wait_recv()
            pass_ffn(which, i).start()
    for i in range(1, pairs):
        source = lax.rem(own_pair + pairs - i, pairs)
        arriving = remote(
            attn_stage.at[c], attn_in.at[source],
            back_sem.at[0, i], back_sem.at[1, i], (first_back + source, w),
        )
        arriving.wait_recv()
    for i in range(1, ws):
        for which in range(2):
            pass_ffn(which, i).wait_recv()
        send_cot(i).wait_recv()
    keep_ffn(0).wait()
    keep_ffn(1).wait()
    keep_cot().wait()
    for i in range(1, ws):
        send_gain(i).wait_send()
        send_x(i).wait_send()
        send_w(i).wait_send()
        pass_w(i).wait_send()
        send_cot(i).wait_send()
        for which in range(2):
            send_ffn(which, i).wait_send()
            pass_ffn(which, i).wait_send()
    for i in range(1, ctx):
        send_pair(i).wait_send()
    for i in range(1, pairs):
        back_copy(first_back + lax.rem(own_pair + i, pairs), i).wait_send()


def front(x, gains, wq, wk, wv, gate, up, cot, cosines, sines, ws, ctx, own_heads, group):
    rows, features = x.shape
    depth = wq.shape[0]
    q_wide = group * HEAD_DIM
    wide = q_wide + 2 * HEAD_DIM
    pairs = ws * own_heads
    length = ctx * rows
    units = gate.shape[1] // ws
    vmem, anywhere = pl.BlockSpec(memory_space=pltpu.VMEM), pl.BlockSpec(memory_space=pl.ANY)
    shape = jax.ShapeDtypeStruct
    return pl.pallas_call(
        functools.partial(front_kernel, ws, ctx, own_heads, group),
        out_shape=[
            shape((ws, rows, features), BF),
            shape((ws, depth, own_heads * wide), BF),
            shape((group, length, HEAD_DIM), BF),
            shape((length, HEAD_DIM), BF),
            shape((length, HEAD_DIM), BF),
            shape((group, length, 128), F32),
            shape((pairs, rows, q_wide), BF),
            shape((features, units), BF),
            shape((features, units), BF),
            shape((ws, rows, features), BF),
            shape(gains.shape, F32),
        ],
        in_specs=[vmem] * 5 + [anywhere] * 5,
        out_specs=[vmem] * 7 + [anywhere] * 3 + [vmem],
        scratch_shapes=[
            pltpu.VMEM((ws, rows, features), BF),
            pltpu.VMEM((ws,) + gains.shape, F32),
            pltpu.VMEM((ws, depth, own_heads * wide), BF),
            pltpu.VMEM((ws * rows, own_heads * wide), F32),
            pltpu.VMEM((pairs, rows, wide), BF),
            pltpu.VMEM((ctx, rows, wide), BF),
            pltpu.VMEM((ctx, rows, q_wide), BF),
            pltpu.VMEM((rows, wide), F32),
            pltpu.VMEM((rows, wide), F32),
            dma(2, ws), dma(2, ws), dma(2, ws), dma(2, ws), dma(2, 2, ws), dma(2, 2, ws),
            dma(2, ws), dma(2, ctx), dma(2, pairs), dma(5),
        ],
        compiler_params=pltpu.CompilerParams(
            collective_id=1, has_side_effects=True, vmem_limit_bytes=60 << 20
        ),
        name="front",
    )(x, gains, wq, wk, wv, gate, up, cot, cosines, sines)


def dot_bt(left, right):
    return lax.dot_general(left, right, (((1,), (1,)), ((), ())), preferred_element_type=F32)


def middle_kernel(
    ws, ctx, own_heads, group,
    x, attn, w_out, gains, gate_all, up_all, w_down_all, cot_all,
    output, grad_residual, gain_out, grad_pair, gw_gate, gw_up, gw_down, gw_out,
    gate, up, w_down, cot, sent, landed, normed, branch, grad_hidden, hidden, grad_gate, grad_up,
    turned, turned_hidden, keep, unit, pair_stage, gate_stage, up_stage, down_stage, out_stage,
    load_sem, save_sem, rs_sem, ag_sem, pair_sem,
):
    c, w = lax.axis_index("ctx"), lax.axis_index("ws")
    rows, features = x.shape
    q_wide = group * HEAD_DIM
    pairs = ws * own_heads
    units = gate.shape[1]
    total_rows = ws * rows
    tile = 256

    def load(i):
        return pltpu.make_async_copy(
            (gate_all, up_all, w_down_all, cot_all)[i], (gate, up, w_down, cot)[i], load_sem.at[i]
        )

    def save(i):
        return pltpu.make_async_copy(
            (gate_stage, up_stage, down_stage, out_stage)[i],
            (gw_gate, gw_up, gw_down, gw_out)[i], save_sem.at[i],
        )

    for i in (3, 2, 0, 1):
        load(i).start()
    near = [(lax.rem(c + i, ctx), w) for i in range(1, ctx)]
    greet(near + [(c, lax.rem(w + i, ws)) for i in range(1, ws)])

    def send_sum(turn, i):
        to = lax.rem(w + i, ws)
        return remote(
            sent.at[turn % 2, to], landed.at[turn % 2, w],
            rs_sem.at[0, turn, i], rs_sem.at[1, turn, i], (c, to),
        )

    def send_rows(turn, i):
        everyone = (normed, branch)[turn]
        return remote(
            everyone.at[w], everyone.at[w],
            ag_sem.at[0, turn, i], ag_sem.at[1, turn, i], (c, lax.rem(w + i, ws)),
        )

    def send_pair(i):
        to = lax.rem(c + i, ctx)
        return remote(
            pair_stage.at[lax.rem(to, pairs)], grad_pair.at[c],
            pair_sem.at[0, i], pair_sem.at[1, i], (to, w),
        )

    def landed_sum(turn):
        total = keep[...]
        for i in range(1, ws):
            send_sum(turn, i).wait_recv()
            total = total + landed[turn % 2, lax.rem(w + ws - i, ws)].astype(F32)
        return total

    def project(i, _):
        s = lax.rem(w + i, ws)
        part = jnp.zeros((rows, features), F32)
        for j in range(own_heads):
            part = part + jnp.dot(
                attn[s * own_heads + j], w_out[j * q_wide : (j + 1) * q_wide, :],
                preferred_element_type=F32,
            )

        @pl.when(i < ws)
        def _():
            sent[0, s] = part.astype(BF)
            send_sum(0, i).start()

        @pl.when(i == ws)
        def _():
            keep[...] = part

        return 0

    lax.fori_loop(1, ws + 1, project, 0)

    load(3).wait()
    load(2).wait()

    def hidden_back(n, _):
        here = pl.ds(pl.multiple_of(n * tile, tile), tile)
        grad_hidden[:, here] = dot_bt(cot[...].reshape(total_rows, features), w_down[here, :])
        return 0

    lax.fori_loop(0, units // tile, hidden_back, 0)
    load(0).wait()
    load(1).wait()

    residual = x[...].astype(F32) + landed_sum(0)
    gain = gains[1:2]
    factor = lax.rsqrt(jnp.mean(residual * residual, axis=-1, keepdims=True) + EPSILON)
    unit[...] = residual * factor
    normed[w] = (unit[...] * gain).astype(BF)
    for i in range(1, ws):
        send_rows(0, i).start()
    grad_residual[...] = residual

    def feed(i, _):
        s = lax.rem(w + ws - i, ws)
        here = pl.ds(pl.multiple_of(s * rows, rows), rows)

        @pl.when(i > 0)
        def _():
            send_rows(0, i).wait_recv()

        block = normed[s]

        def columns(n, _):
            cut = pl.ds(pl.multiple_of(n * tile, tile), tile)
            gate_proj = jnp.dot(block, gate[:, cut], preferred_element_type=F32)
            up_proj = jnp.dot(block, up[:, cut], preferred_element_type=F32)
            sigmoid = 1.0 / (1.0 + jnp.exp(-gate_proj))
            activation = gate_proj * sigmoid
            grad = grad_hidden[here, cut]
            hidden[here, cut] = (activation * up_proj).astype(BF)
            grad_up[here, cut] = (grad * activation).astype(BF)
            grad_gate[here, cut] = (
                grad * up_proj * sigmoid * (1.0 + gate_proj * (1.0 - sigmoid))
            ).astype(BF)
            return 0

        lax.fori_loop(0, units // tile, columns, 0)
        to = lax.rem(w + ws - i, ws)

        def back(n, _):
            cut = pl.ds(pl.multiple_of(n * tile, tile), tile)
            part = dot_bt(grad_gate[here, :], gate[cut, :]) + dot_bt(grad_up[here, :], up[cut, :])

            @pl.when(i > 0)
            def _():
                sent[1, to, :, cut] = part.astype(BF)

            @pl.when(i == 0)
            def _():
                keep[:, cut] = part

            return 0

        lax.fori_loop(0, features // tile, back, 0)

        @pl.when(i > 0)
        def _():
            send_sum(1, ws - i).start()

        return 0

    lax.fori_loop(0, ws, feed, 0)

    def turn(n, _):
        cut = pl.ds(pl.multiple_of(n * tile, tile), tile)
        turned[cut, :] = normed[:, :, cut].reshape(total_rows, tile).T
        return 0

    lax.fori_loop(0, features // tile, turn, 0)

    def turn_hidden(n, _):
        cut = pl.ds(pl.multiple_of(n * tile, tile), tile)
        turned_hidden[cut, :] = hidden[:, cut].T
        return 0

    lax.fori_loop(0, units // tile, turn_hidden, 0)

    def down_rows(n, _):
        cut = pl.ds(pl.multiple_of(n * tile, tile), tile)
        down_stage[cut, :] = jnp.dot(
            turned_hidden[cut, :], cot[...].reshape(total_rows, features),
            preferred_element_type=F32,
        ).astype(BF)
        return 0

    lax.fori_loop(0, units // tile, down_rows, 0)
    save(2).start()

    def ffn_rows(n, _):
        cut = pl.ds(pl.multiple_of(n * tile, tile), tile)
        gate_stage[cut, :] = jnp.dot(
            turned[cut, :], grad_gate[...], preferred_element_type=F32
        ).astype(BF)
        up_stage[cut, :] = jnp.dot(
            turned[cut, :], grad_up[...], preferred_element_type=F32
        ).astype(BF)
        return 0

    lax.fori_loop(0, features // tile, ffn_rows, 0)
    save(0).start()
    save(1).start()

    grad_normed = landed_sum(1)
    gain_out[...] = jnp.broadcast_to(
        jnp.sum(grad_normed * unit[...], axis=0, keepdims=True), gain_out.shape
    )
    grad = grad_normed * gain
    mean = jnp.mean(grad * unit[...], axis=-1, keepdims=True)
    residual = grad_residual[...]
    factor = lax.rsqrt(jnp.mean(residual * residual, axis=-1, keepdims=True) + EPSILON)
    back_grad = cot[w].astype(F32) + factor * (grad - unit[...] * mean)
    unit[...] = residual
    grad_residual[...] = back_grad
    branch[w] = back_grad.astype(BF)
    for i in range(1, ws):
        send_rows(1, i).start()

    for i in range(1, ws):
        send_sum(0, i).wait_send()

    def down_columns(n, _):
        cut = pl.ds(pl.multiple_of(n * tile, tile), tile)
        part = jnp.dot(hidden[...], w_down[:, cut], preferred_element_type=F32)
        sent[0, :, :, cut] = part.astype(BF).reshape(ws, rows, tile)
        keep[:, cut] = jnp.dot(
            hidden[pl.ds(pl.multiple_of(w * rows, rows), rows), :], w_down[:, cut],
            preferred_element_type=F32,
        )
        return 0

    lax.fori_loop(0, features // tile, down_columns, 0)

    for i in range(ws):
        s = lax.rem(w + ws - i, ws)
        if i:
            send_rows(1, i).wait_recv()
        grad_low = dot_bt(branch[s], w_out[...]).astype(BF)
        for j in range(own_heads):
            pair_stage[s * own_heads + j] = grad_low[:, j * q_wide : (j + 1) * q_wide]
    for i in range(1, ctx):
        send_pair(i).start()
    grad_pair[c] = pair_stage[lax.rem(c, pairs)]
    for i in range(1, ws):
        send_sum(2, i).start()

    for j in range(own_heads):
        side = jnp.concatenate([attn[s * own_heads + j] for s in range(ws)], axis=0)
        low_turned = side.T
        out_stage[j * q_wide : (j + 1) * q_wide, :] = jnp.dot(
            low_turned, branch[...].reshape(total_rows, features), preferred_element_type=F32
        ).astype(BF)
    save(3).start()

    for i in range(1, ctx):
        send_pair(i).wait_recv()
    output[...] = (unit[...] + landed_sum(2)).astype(BF)
    for i in range(4):
        save(i).wait()
    for i in range(1, ws):
        for t in range(1, 3):
            send_sum(t, i).wait_send()
        for t in range(2):
            send_rows(t, i).wait_send()
    for i in range(1, ctx):
        send_pair(i).wait_send()


def middle(x, attn, w_out, gains, gate, up, w_down, cot, ws, ctx, own_heads, group):
    rows, features = x.shape
    units = gate.shape[1]
    q_wide = group * HEAD_DIM
    pairs = ws * own_heads
    vmem, anywhere = pl.BlockSpec(memory_space=pltpu.VMEM), pl.BlockSpec(memory_space=pl.ANY)
    shape, held = jax.ShapeDtypeStruct, pltpu.VMEM
    total = ws * rows
    return pl.pallas_call(
        functools.partial(middle_kernel, ws, ctx, own_heads, group),
        out_shape=[
            shape((rows, features), BF),
            shape((rows, features), F32),
            shape((8, features), F32),
            shape((ctx, rows, q_wide), BF),
            shape((features, units), BF),
            shape((features, units), BF),
            shape((units, features), BF),
            shape(w_out.shape, BF),
        ],
        in_specs=[vmem] * 4 + [anywhere] * 4,
        out_specs=[vmem] * 4 + [anywhere] * 4,
        scratch_shapes=[
            held((features, units), BF),
            held((features, units), BF),
            held((units, features), BF),
            held((ws, rows, features), BF),
            held((2, ws, rows, features), BF),
            held((2, ws, rows, features), BF),
            held((ws, rows, features), BF),
            held((ws, rows, features), BF),
            held((total, units), F32),
            held((total, units), BF),
            held((total, units), BF),
            held((total, units), BF),
            held((features, total), BF),
            held((units, total), BF),
            held((rows, features), F32),
            held((rows, features), F32),
            held((pairs, rows, q_wide), BF),
            held((features, units), BF),
            held((features, units), BF),
            held((units, features), BF),
            held(w_out.shape, BF),
            dma(4), dma(4), dma(2, 3, ws), dma(2, 2, ws), dma(2, ctx),
        ],
        compiler_params=pltpu.CompilerParams(
            collective_id=2, has_side_effects=True, vmem_limit_bytes=62 << 20
        ),
        name="middle",
    )(x, attn, w_out, gains, gate, up, w_down, cot)


SKEW = 2


def back_kernel(
    ws, ctx, group, own_heads, moved, rows, ticks,
    x, gains, gain_in, grad_residual, q, k, v, pack, grad_pair, cosines, sines,
    normed_all, w_all, gw_down, gw_out, gw_gate, gw_up,
    grad_input, gain_out, *refs,
):
    count = len(moved)
    outs, refs = refs[:count], refs[count:]
    parts, refs = refs[:count], refs[count:]
    sib_buf, refs = refs[:count], refs[count:]
    fin, refs = refs[:count], refs[count:]
    acc, refs = refs[:count], refs[count:]
    red_send, red_recv, bc_send, bc_recv, core_send, core_recv = (
        refs[i * count : (i + 1) * count] for i in range(6)
    )
    (
        normed, w_qkv, turned, grad_q, grad_k, grad_v, key_turned, back_stage, grad_in, grad_rows,
        sent, landed, keep, own_gain, ws_gain, ctx_gain,
        sib_send, sib_recv, mv_send, mv_recv, loc_sem, load_sem, save_sem, pair_sem, rs_sem,
        gain_sem, wide_sem, cos, sin, rope_sem,
    ) = refs[6 * count :]
    c, w = lax.axis_index("ctx"), lax.axis_index("ws")
    core = lax.rem(c, 2)
    place, line = c // 2, ctx // 2
    sibling = (c + 1 - 2 * core, w)
    before, after = (c - 2, w), (c + 2, w)
    tokens, features = x.shape
    q_wide = group * HEAD_DIM
    wide = q_wide + 2 * HEAD_DIM
    pairs = ws * own_heads
    length = ctx * tokens
    depth = features // ws

    loads = (gw_down, gw_out, gw_gate, gw_up)

    def load(i):
        return pltpu.make_async_copy(loads[i], parts[i], load_sem.at[i])

    def load_more(i):
        return pltpu.make_async_copy(
            (normed_all, w_all)[i], (normed, w_qkv)[i], load_sem.at[4 + i]
        )

    for i in range(4):
        load(i).start()
    load_more(0).start()
    load_more(1).start()
    greet(
        [(lax.rem(c + i, ctx), w) for i in range(1, ctx)]
        + [(c, lax.rem(w + i, ws)) for i in range(1, ws)]
    )

    def across_cores(i):
        half = parts[i].at[:, 1 - core] if moved[i] else parts[i].at[1 - core]
        return remote(half, sib_buf[i], sib_send.at[i], sib_recv.at[i], sibling)

    own_columns = [
        pl.ds(pl.multiple_of(w * parts[i].shape[-1], 128), parts[i].shape[-1]) for i in range(count)
    ]

    def move_of(i, step):
        owner = lax.rem(w + step, ws)
        return remote(
            parts[i].at[owner, core], acc[i].at[:, own_columns[i]],
            mv_send.at[i, step], mv_recv.at[i, step], (c, owner),
        )

    def keep_of(i):
        return pltpu.make_async_copy(
            parts[i].at[w, core], acc[i].at[:, own_columns[i]], loc_sem.at[i]
        )

    def share(i):
        across_cores(i).wait_recv()
        for step in list(range(1, ws)) + [0]:
            owner = lax.rem(w + step, ws)
            total = parts[i][owner, core].astype(F32) + sib_buf[i][owner].astype(F32)
            parts[i][owner, core] = total.astype(BF)
            if step:
                move_of(i, step).start()
            else:
                keep_of(i).start()

    def settle(i):
        for step in range(1, ws):
            move_of(i, step).wait_recv()
        keep_of(i).wait()

    def chunk(ref, i, j):
        return ref.at[pl.ds(pl.multiple_of(j * rows[i], rows[i]), rows[i]), :]

    def running(i, j):
        return chunk(acc[i] if moved[i] else parts[i].at[core], i, j)

    def local(i, j):
        block = running(i, j)[...].astype(F32)
        if moved[i]:
            return block
        return block + chunk(sib_buf[i], i, j)[...].astype(F32)

    def up_line(i, j, odd):
        return remote(
            running(i, j), chunk(fin[i].at[core], i, j),
            red_send[i].at[j], red_recv[i].at[j], after if odd else before,
        )

    def down_line(i, j, odd):
        final = chunk(fin[i].at[core], i, j)
        return remote(
            final, final, bc_send[i].at[j], bc_recv[i].at[j], before if odd else after
        )

    def over(i, j, half):
        final = chunk(fin[i].at[half], i, j)
        return remote(final, final, core_send[i].at[j], core_recv[i].at[j], sibling)

    def ends(odd):
        low, high = place == 0, place == line - 1
        return (low, high) if odd else (high, low)

    def reduce_chunk(i, j, odd):
        start, end = ends(odd)

        @pl.when(start)
        def _():
            if not moved[i]:
                running(i, j)[...] = local(i, j).astype(BF)
            up_line(i, j, odd).start()

        @pl.when(jnp.logical_not(start))
        def _():
            up_line(i, j, odd).wait_recv()
            total = local(i, j) + chunk(fin[i].at[core], i, j)[...].astype(F32)
            total = total.astype(BF)

            @pl.when(jnp.logical_not(end))
            def _():
                running(i, j)[...] = total
                up_line(i, j, odd).start()

            @pl.when(end)
            def _():
                chunk(fin[i].at[core], i, j)[...] = total
                down_line(i, j, odd).start()

    def spread_chunk(i, j, odd):
        end, start = ends(odd)

        @pl.when(jnp.logical_not(start))
        def _():
            down_line(i, j, odd).wait_recv()

            @pl.when(jnp.logical_not(end))
            def _():
                down_line(i, j, odd).start()

        over(i, j, core).start()

    first, total_chunks = [], 0
    for i in range(count):
        first.append(total_chunks)
        total_chunks += fin[i].shape[1] // rows[i] // 2
    lasts = first[1:] + [total_chunks]
    hops = (line - 1 - place, place)

    def chain(t):
        for i in range(count):
            if moved[i]:

                @pl.when(t == max(first[i] - 8, 0))
                def _():
                    share(i)

                @pl.when(t == first[i])
                def _():
                    settle(i)

            else:

                @pl.when(t == first[i])
                def _():
                    across_cores(i).wait_recv()

        for odd in range(2):
            at = t - SKEW * hops[odd]
            back = t - SKEW * (2 * (line - 1) - hops[odd])
            for i in range(count):

                @pl.when((at >= first[i]) & (at < lasts[i]))
                def _():
                    reduce_chunk(i, 2 * (at - first[i]) + odd, odd)

                @pl.when((back >= first[i]) & (back < lasts[i]))
                def _():
                    spread_chunk(i, 2 * (back - first[i]) + odd, odd)

    first_back = c // pairs * pairs
    own_pair = lax.rem(c, pairs)
    span = min(256, length) if length <= 1024 else tokens

    def back_unit(g, start, low, keys):
        here, there = pl.ds(start, span), pl.ds(low, keys)
        query = q[g, here, :]
        grad = (
            grad_pair[pl.ds(start // tokens, span // tokens), :, g * HEAD_DIM : (g + 1) * HEAD_DIM]
        ).reshape(span, HEAD_DIM)
        kept = pack[g, here, :]
        kept_turned = kept.T
        top, total = kept_turned[HEAD_DIM : HEAD_DIM + 1], kept_turned[HEAD_DIM + 1 : HEAD_DIM + 2]
        grad_wide = grad.astype(F32)
        delta = jnp.sum(grad_wide.T * kept_turned[:HEAD_DIM], axis=0, keepdims=True)
        scaled = (grad_wide / kept[:, HEAD_DIM + 1 : HEAD_DIM + 2]).astype(BF)
        scores = dot_bt(k[there, :], query) * HEAD_DIM**-0.5
        allowed = start + lax.broadcasted_iota(
            jnp.int32, (keys, span), 1
        ) >= low + lax.broadcasted_iota(jnp.int32, (keys, span), 0)
        weights = jnp.exp(jnp.where(allowed, scores, MASK_FILL) - top)
        grad_probs = dot_bt(v[there, :], grad)
        grad_scores = (weights * (1.0 / total) * (grad_probs - delta)).astype(BF)
        grad_k[there, :] += jnp.dot(grad_scores, query, preferred_element_type=F32)
        grad_v[there, :] += jnp.dot(weights.astype(BF), scaled, preferred_element_type=F32)
        turned_grad = jnp.dot(
            key_turned[:, there], grad_scores, preferred_element_type=F32
        )
        if length <= 1024:
            grad_q[g, here, :] = turned_grad.T
        else:
            grad_q[g, here, :] += turned_grad.T

    def send_back(to, i):
        return remote(
            back_stage.at[to], grad_in.at[own_pair],
            pair_sem.at[0, i], pair_sem.at[1, i], (to, w),
        )

    def rope_copy(i, start):
        table, kept = ((cosines, cos), (sines, sin))[i]
        return pltpu.make_async_copy(table.at[pl.ds(start, span), :], kept, rope_sem.at[i])

    def finish_rows(start):
        here = pl.ds(start, span)
        rope_copy(0, start).wait()
        rope_copy(1, start).wait()
        scale = HEAD_DIM**-0.5
        block = jnp.concatenate(
            [grad_q[g, here, :] * scale for g in range(group)]
            + [grad_k[here, :] * scale, grad_v[here, :]],
            axis=1,
        )
        block = (block * cos[...] - swap_lanes(block) * sin[...]).astype(BF)
        for b in range(span // tokens):
            to = start // tokens + b
            back_stage[to] = block[b * tokens : (b + 1) * tokens]

    def send_rows_back(to):
        step = lax.rem(to - c + ctx, pairs)

        @pl.when((to // pairs == c // pairs) & (to != c))
        def _():
            send_back(to, step).start()

        @pl.when(to == c)
        def _():
            grad_in[own_pair] = back_stage[to]

    def prepare():
        grad_k[...] = jnp.zeros(grad_k.shape, F32)
        grad_v[...] = jnp.zeros(grad_v.shape, F32)
        key_turned[...] = k[...].T
        load_more(0).wait()
        load_more(1).wait()

    def turn_normed():
        def turn(n, _):
            cut = pl.ds(pl.multiple_of(n * 256, 256), 256)
            turned[cut, :] = normed[:, :, cut].reshape(ws * tokens, 256).T
            return 0

        lax.fori_loop(0, features // 256, turn, 0)

    def gather_back():
        for i in range(1, pairs):
            source = lax.rem(own_pair + pairs - i, pairs)
            arriving = remote(
                back_stage.at[c], grad_in.at[source],
                pair_sem.at[0, i], pair_sem.at[1, i], (first_back + source, w),
            )
            arriving.wait_recv()
        for s in range(ws):
            for j in range(own_heads):
                grad_rows[s * tokens : (s + 1) * tokens, j * wide : (j + 1) * wide] = grad_in[
                    s * own_heads + j
                ]

    def send_sum(i):
        to = lax.rem(w + i, ws)
        return remote(sent.at[to], landed.at[w], rs_sem.at[0, i], rs_sem.at[1, i], (c, to))

    def sum_rows():
        def one(i, _):
            s = lax.rem(w + i, ws)
            block = grad_rows[pl.ds(pl.multiple_of(s * tokens, tokens), tokens), :]
            for n in range(0, ws):
                part = dot_bt(block, w_qkv[n])

                @pl.when(i < ws)
                def _():
                    sent[s, :, n * depth : (n + 1) * depth] = part.astype(BF)

                @pl.when(i == ws)
                def _():
                    keep[:, n * depth : (n + 1) * depth] = part

            @pl.when(i < ws)
            def _():
                send_sum(i).start()

            return 0

        lax.fori_loop(1, ws + 1, one, 0)

    def weight_sums():
        half = depth // 2

        def one(o, _):
            for h in range(2):
                cut = pl.ds(pl.multiple_of(o * depth + h * half, half), half)
                parts[count - 1][o, h] = jnp.dot(
                    turned[cut, :], grad_rows[...], preferred_element_type=F32
                ).astype(BF)
            return 0

        lax.fori_loop(0, ws, one, 0)
        across_cores(count - 1).start()

    def send_gain(i):
        return remote(
            own_gain, ws_gain.at[w], gain_sem.at[0, i], gain_sem.at[1, i],
            (c, lax.rem(w + i, ws)),
        )

    def send_wide(i):
        return remote(
            ws_gain.at[w], ctx_gain.at[c], wide_sem.at[0, i], wide_sem.at[1, i],
            (lax.rem(c + i, ctx), w),
        )

    def finish_input():
        total = keep[...]
        for i in range(1, ws):
            send_sum(i).wait_recv()
            total = total + landed[lax.rem(w + ws - i, ws)].astype(F32)
        inputs = x[...].astype(F32)
        factor = lax.rsqrt(jnp.mean(inputs * inputs, axis=-1, keepdims=True) + EPSILON)
        unit = inputs * factor
        row = lax.broadcasted_iota(jnp.int32, own_gain.shape, 0)
        attn_gain = jnp.sum(total * unit, axis=0, keepdims=True)
        own_gain[...] = jnp.where(row == 0, attn_gain, gain_in[...])
        for i in range(1, ws):
            send_gain(i).start()
        grad = total * gains[0:1]
        mean = jnp.mean(grad * unit, axis=-1, keepdims=True)
        grad_input[...] = grad_residual[...] + factor * (grad - unit * mean)

    def widen_gain():
        total = own_gain[...]
        for i in range(1, ws):
            send_gain(i).wait_recv()
            total = total + ws_gain[lax.rem(w + ws - i, ws)]
        ws_gain[w] = total
        for i in range(1, ctx):
            send_wide(i).start()

    def finish_gain():
        total = ws_gain[w]
        for i in range(1, ctx):
            send_wide(i).wait_recv()
            total = total + ctx_gain[lax.rem(c + ctx - i, ctx)]
        gain_out[...] = total

    events = [[] for _ in range(ticks)]
    events[0].append(prepare)
    starts = list(range(0, length, span))[::-1]
    if length <= 1024:
        for n, start in enumerate(starts):

            def one_start(start=start):
                rope_copy(0, start).start()
                rope_copy(1, start).start()
                for g in range(group):
                    back_unit(g, start, 0, start + span)
                finish_rows(start)
                for b in range(span // tokens):
                    send_rows_back(start // tokens + b)

            events[min(n, ticks - 1)].append(one_start)
        at = min(len(starts), ticks - 1)
    else:

        def all_starts():
            grad_q[...] = jnp.zeros(grad_q.shape, F32)

            def one_start(n, _):
                start = pl.multiple_of(n * span, span)

                def one_block(m, _):
                    low = pl.multiple_of(m * 512, 512)

                    @pl.when(low < start + span)
                    def _():
                        for g in range(group):
                            back_unit(g, start, low, 512)

                    return 0

                lax.fori_loop(0, length // 512, one_block, 0)
                return 0

            lax.fori_loop(0, length // span, one_start, 0)

            def finish(n, _):
                start = pl.multiple_of(n * span, span)
                rope_copy(0, start).start()
                rope_copy(1, start).start()
                finish_rows(start)
                return 0

            lax.fori_loop(0, length // span, finish, 0)
            for to in range(ctx):
                send_rows_back(to)

        events[0].append(all_starts)
        at = 1
    events[at].append(turn_normed)
    events[at + 4].append(gather_back)
    events[at + 4].append(sum_rows)
    events[at + 4].append(weight_sums)
    events[at + 9].append(finish_input)
    events[at + 11].append(widen_gain)
    events[at + 14].append(finish_gain)

    for i in range(4):
        load(i).wait()
        across_cores(i).start()

    def tick(t, _):
        chain(t)
        for n, todo in enumerate(events):
            if todo:

                @pl.when(t == n)
                def _():
                    for event in todo:
                        event()

        return 0

    lax.fori_loop(0, ticks, tick, 0)

    for i in range(count):
        chunks = fin[i].shape[1] // rows[i]

        def finish_pair(p, _):
            for odd in range(2):
                j = 2 * p + odd
                _, reduce_end = ends(odd)
                spread_end, _ = ends(odd)

                @pl.when(jnp.logical_not(reduce_end))
                def _():
                    up_line(i, j, odd).wait_send()

                @pl.when(jnp.logical_not(spread_end))
                def _():
                    down_line(i, j, odd).wait_send()

                over(i, j, core).wait_send()
                over(i, j, 1 - core).wait_recv()
            return 0

        lax.fori_loop(0, chunks // 2, finish_pair, 0)
        pltpu.make_async_copy(fin[i], outs[i], save_sem.at[i]).start()
    for i in range(count):
        across_cores(i).wait_send()
        if moved[i]:
            for step in range(1, ws):
                move_of(i, step).wait_send()
    for i in range(1, ws):
        send_sum(i).wait_send()
        send_gain(i).wait_send()
    for i in range(1, ctx):
        send_wide(i).wait_send()
    for i in range(1, pairs):
        send_back(first_back + lax.rem(own_pair + i, pairs), i).wait_send()
    for i in range(count):
        pltpu.make_async_copy(fin[i], outs[i], save_sem.at[i]).wait()


def back(
    x, gains, gain_in, grad_residual, q, k, v, pack, grad_pair, cosines, sines,
    normed, w_all, gw_down, gw_out, gw_gate, gw_up, ws, ctx, own_heads,
):
    tokens, features = x.shape
    group, length, _ = q.shape
    q_wide = group * HEAD_DIM
    wide = q_wide + 2 * HEAD_DIM
    pairs = ws * own_heads
    span = min(256, length) if length <= 1024 else tokens
    depth = features // ws
    moved = (False, False, True, True, True)
    held = pltpu.VMEM
    widths = [gw_down.shape[1], gw_out.shape[1], gw_gate.shape[1], gw_up.shape[1], own_heads * wide]
    halves = [gw_down.shape[0] // 2, gw_out.shape[0] // 2] + [depth // 2] * 3
    rows = []
    parts, sib, fin, acc = [], [], [], []
    for is_moved, n, half, want in zip(moved, widths, halves, (32, 32, 16, 16, 16)):
        while half % (2 * want):
            want //= 2
        rows.append(want)
        lead = (ws,) if is_moved else ()
        parts.append(lead + (2, half, n))
        sib.append(held(lead + (half, n), BF))
        fin.append((2, half, ws * n if is_moved else n))
        acc.append(held((half, ws * n) if is_moved else (16, 128), BF))
    counts = [f[1] // r for f, r in zip(fin, rows)]
    ticks = sum(counts) // 2 + 2 * SKEW * (ctx // 2 - 1)
    k_count = len(parts)
    vmem, anywhere = pl.BlockSpec(memory_space=pltpu.VMEM), pl.BlockSpec(memory_space=pl.ANY)
    shape = jax.ShapeDtypeStruct
    results = pl.pallas_call(
        functools.partial(
            back_kernel, ws, ctx, group, own_heads, moved, tuple(rows), ticks
        ),
        out_shape=[shape((tokens, features), F32), shape(gains.shape, F32)]
        + [shape(f, BF) for f in fin],
        in_specs=[vmem] * 9 + [anywhere] * 8,
        out_specs=[vmem] * 2 + [anywhere] * k_count,
        scratch_shapes=[held(p, BF) for p in parts]
        + sib
        + [held(f, BF) for f in fin]
        + acc
        + [dma(n) for _ in range(6) for n in counts]
        + [
            held(normed.shape, BF),
            held(w_all.shape, BF),
            held((features, ws * tokens), BF),
            held((group, length, HEAD_DIM), F32),
            held((length, HEAD_DIM), F32),
            held((length, HEAD_DIM), F32),
            held((HEAD_DIM, length), BF),
            held((ctx, tokens, wide), BF),
            held((pairs, tokens, wide), BF),
            held((ws * tokens, own_heads * wide), BF),
            held((ws, tokens, features), BF),
            held((ws, tokens, features), BF),
            held((tokens, features), F32),
            held(gains.shape, F32),
            held((ws,) + gains.shape, F32),
            held((ctx,) + gains.shape, F32),
            dma(k_count), dma(k_count), dma(k_count, ws), dma(k_count, ws), dma(k_count),
            dma(6), dma(k_count), dma(2, pairs), dma(2, ws), dma(2, ws), dma(2, ctx),
            held((span, wide), F32), held((span, wide), F32), dma(2),
        ],
        compiler_params=pltpu.CompilerParams(
            collective_id=3, has_side_effects=True, vmem_limit_bytes=63 << 20
        ),
        name="back",
    )(
        x, gains, gain_in, grad_residual, q, k, v, pack, grad_pair, cosines, sines,
        normed, w_all,
        gw_down.reshape(parts[0]), gw_out.reshape(parts[1]),
        gw_gate.reshape(parts[2]), gw_up.reshape(parts[3]),
    )
    sums = [s.reshape(s.shape[0] * s.shape[1], s.shape[2]) for s in results[2:]]
    return results[0], results[1], sums


def tail_kernel(ws, group, *refs):
    low, refs = refs[:8], refs[8:]
    down, out, gate, up, qkv, output, grad_input, gain_sums = low
    (
        output_out, grad_input_out, attn_gain, g_query, g_key, g_value, g_out, ffn_gain, g_gate,
        g_up, g_down,
    ) = refs
    q_wide = group * HEAD_DIM
    wide = q_wide + 2 * HEAD_DIM
    output_out[...] = output[...]
    grad_input_out[...] = grad_input[...]
    g_down[...] = down[...].astype(F32)
    g_out[...] = out[...].astype(F32)
    g_gate[...] = gate[...].astype(F32)
    g_up[...] = up[...].astype(F32)
    heads = qkv.shape[1] // wide
    blocks = [qkv[:, h * wide : (h + 1) * wide].astype(F32) for h in range(heads)]
    g_query[...] = jnp.concatenate([b[:, :q_wide] for b in blocks], axis=1)
    g_key[...] = jnp.concatenate([b[:, q_wide : q_wide + HEAD_DIM] for b in blocks], axis=1)
    g_value[...] = jnp.concatenate([b[:, q_wide + HEAD_DIM :] for b in blocks], axis=1)
    w = lax.axis_index("ws")
    depth = attn_gain.shape[1]
    for i in range(ws):

        @pl.when(w == i)
        def _():
            here = gain_sums[:, i * depth : (i + 1) * depth]
            attn_gain[...] = here[0:1]
            ffn_gain[...] = here[1:2]


def tail(down, out, gate, up, qkv, output, grad_input, gain_sums, ws, group):
    depth = qkv.shape[0]
    steps = depth // 48
    features = out.shape[1]
    q_total = qkv.shape[1] * group // (group + 2)
    k_total = q_total // group
    shape = jax.ShapeDtypeStruct

    def split(rows, columns):
        return pl.BlockSpec((rows // steps, columns), lambda n: (n, 0))

    def whole(rows, columns):
        return pl.BlockSpec((rows, columns), lambda n: (0, 0))

    out_shape = [
        shape(output.shape, BF), shape(grad_input.shape, F32), shape((1, depth), F32),
        shape((depth, q_total), F32), shape((depth, k_total), F32), shape((depth, k_total), F32),
        shape(out.shape, F32), shape((1, depth), F32), shape(gate.shape, F32),
        shape(up.shape, F32), shape(down.shape, F32),
    ]
    return pl.pallas_call(
        functools.partial(tail_kernel, ws, group),
        grid=(steps,),
        out_shape=out_shape,
        in_specs=[split(*a.shape) for a in (down, out, gate, up, qkv, output, grad_input)]
        + [whole(*gain_sums.shape)],
        out_specs=[
            whole(*o.shape) if o.shape[0] == 1 else split(*o.shape) for o in out_shape
        ],
        compiler_params=pltpu.CompilerParams(vmem_limit_bytes=48 << 20),
        name="tail",
    )(down, out, gate, up, qkv, output, grad_input, gain_sums)


def body(
    hidden_in,
    attn_gain,
    w_query,
    key_weight,
    value_weight,
    w_out,
    ffn_gain,
    w_gate,
    w_up,
    w_down,
    cotangent,
):
    ws, ctx = lax.axis_size("ws"), lax.axis_size("ctx")
    local_len, local_seqs, features = hidden_in.shape
    row_count = local_len * local_seqs
    q_heads = w_query.shape[1] // HEAD_DIM
    kv_heads = key_weight.shape[1] // HEAD_DIM
    group = q_heads // kv_heads
    own_heads = kv_heads // ws
    wide = (group + 2) * HEAD_DIM
    q_wide = group * HEAD_DIM
    pairs = ws * local_seqs * own_heads
    copies = ctx // pairs
    depth = features // ws
    cosines, sines = rope_tables(ctx * local_len, group + 1, 1)
    gains = jnp.stack([attn_gain, ffn_gain]).astype(F32)
    gains = lax.dynamic_update_slice(
        jnp.zeros((8, features), F32), gains, (0, lax.axis_index("ws") * depth)
    )
    inputs = hidden_in.reshape(row_count, features)
    grad_low = cotangent.reshape(row_count, features)
    (
        normed_attn, w_qkv, q_pair, k_pair, v_pair, pack, attn_in, gate, up, grad_low_all, gains,
    ) = front(
        inputs, gains, w_query, key_weight, value_weight, w_gate, w_up, grad_low, cosines, sines,
        ws, ctx, own_heads, group,
    )
    (
        output, grad_residual, ffn_gain_sums, grad_pair, gw_gate, gw_up, gw_down, gw_out,
    ) = middle(
        inputs, attn_in, w_out, gains, gate, up, w_down, grad_low_all, ws, ctx, own_heads, group,
    )
    grad_input, gain_sums, (g_down, g_out, g_gate, g_up, g_qkv) = back(
        inputs, gains, ffn_gain_sums, grad_residual, q_pair, k_pair, v_pair, pack, grad_pair,
        cosines, sines, normed_attn, w_qkv, gw_down, gw_out, gw_gate, gw_up, ws, ctx, own_heads,
    )
    results = tail(
        g_down, g_out, g_gate, g_up, g_qkv, output, grad_input, gain_sums, ws, group
    )
    output, grad_input, attn_gain_sum, *middle_sums = results
    *middle_sums, ffn_gain_sum, g_gate, g_up, g_down = middle_sums
    return (
        output.reshape(hidden_in.shape),
        grad_input.reshape(hidden_in.shape),
        attn_gain_sum.reshape(depth),
        *middle_sums,
        ffn_gain_sum.reshape(depth),
        g_gate,
        g_up,
        g_down,
    )


def solution(mesh):
    tokens, rows, one = P("ctx", "ws", None), P("ws", None), P("ws")
    return jax.shard_map(
        body,
        mesh=mesh,
        in_specs=(tokens, one, rows, rows, rows, rows, one, rows, rows, rows, tokens),
        out_specs=(tokens, tokens, one, rows, rows, rows, rows, one, rows, rows, rows),
        check_vma=False,
    )
```

```python
import functools

import jax
import jax.numpy as jnp
import numpy as np
from jax import lax
from jax.experimental import pallas as pl
from jax.experimental.pallas import tpu as pltpu
from jax.sharding import PartitionSpec as P

HEAD_DIM = 96
EPSILON = 1e-05
ROPE_BASE = 100000.0
MASK_FILL = -1e30
BF = jnp.bfloat16
F32 = jnp.float32


def rope_tables(length, rotated_heads, plain_heads):
    half = HEAD_DIM // 2
    frequency = np.float32(ROPE_BASE) ** (-(np.arange(half, dtype=np.float32) * 2.0 / HEAD_DIM))
    angles = np.arange(length, dtype=np.float32)[:, None] * frequency[None, :].astype(np.float32)
    cosine, sine = np.cos(angles), np.sin(angles)
    plain = np.zeros((length, plain_heads * HEAD_DIM), np.float32)
    cosines = [cosine, cosine] * rotated_heads + [plain + 1.0]
    sines = [-sine, sine] * rotated_heads + [plain]
    return (
        jnp.asarray(np.concatenate(cosines, axis=-1), F32),
        jnp.asarray(np.concatenate(sines, axis=-1), F32),
    )


MESH = pl.DeviceIdType.MESH


def remote(src, dst, send_sem, recv_sem, device):
    return pltpu.make_async_remote_copy(
        src_ref=src, dst_ref=dst, send_sem=send_sem, recv_sem=recv_sem,
        device_id=device, device_id_type=MESH,
    )


def dma(*shape):
    return pltpu.SemaphoreType.DMA(shape)


def at_rows(ref, start, size):
    return ref.at[pl.ds(pl.multiple_of(start, size), size), :]


def greet(devices):
    barrier = pltpu.get_barrier_semaphore()
    for device in devices:
        pl.semaphore_signal(barrier, inc=1, device_id=device, device_id_type=MESH)
    pl.semaphore_wait(barrier, len(devices))


def swap_lanes(vectors):
    lanes = lax.broadcasted_iota(jnp.int32, vectors.shape, 1)
    width, half = vectors.shape[1], HEAD_DIM // 2
    first = lax.rem(lanes, HEAD_DIM) < half
    return jnp.where(first, pltpu.roll(vectors, width - half, 1), pltpu.roll(vectors, half, 1))


def front_kernel(
    ws, ctx, own_heads, group,
    x, gains, wq, wk, wv, gate, up, cot, cosines, sines,
    normed, w_all, q_out, k_out, v_out, pack, attn_in, gate_all, up_all, cot_all, gains_all,
    x_all, g_in, w_stage, raw, qkv_stage, pair, attn_stage, cos, sin,
    x_sem, g_sem, w_sem, wf_sem, ffn_sem, ff_sem, cot_sem, pair_sem, back_sem, own_sem,
):
    c, w = lax.axis_index("ctx"), lax.axis_index("ws")
    core = lax.rem(c, 2)
    sibling = (c + 1 - 2 * core, w)
    rows = x.shape[0]
    depth = wq.shape[0]
    half = depth // 2
    q_wide = group * HEAD_DIM
    wide = q_wide + 2 * HEAD_DIM
    pairs = ws * own_heads
    units = gate_all.shape[1]
    peer = [lax.rem(w + i, ws) for i in range(ws)]
    origin = [lax.rem(w + ws - i, ws) for i in range(ws)]

    def rope_copy(i):
        table, kept = ((cosines, cos), (sines, sin))[i]
        return pltpu.make_async_copy(at_rows(table, c * rows, rows), kept, own_sem.at[i])

    rope_copy(0).start()
    rope_copy(1).start()
    near = [(lax.rem(c + i, ctx), w) for i in range(1, ctx)]
    greet(near + [(c, peer[i]) for i in range(1, ws)])

    def send_gain(i):
        return remote(gains, g_in.at[w], g_sem.at[0, i], g_sem.at[1, i], (c, peer[i]))

    def send_x(i):
        return remote(x, x_all.at[w], x_sem.at[0, i], x_sem.at[1, i], (c, peer[i]))

    def send_w(i):
        return remote(
            at_rows(w_stage.at[peer[i]], core * half, half),
            at_rows(w_all.at[w], core * half, half),
            w_sem.at[0, i], w_sem.at[1, i], (c, peer[i]),
        )

    def pass_w(i):
        block = at_rows(w_all.at[origin[i]], core * half, half)
        return remote(block, block, wf_sem.at[0, i], wf_sem.at[1, i], sibling)

    def send_ffn(which, i):
        held, everyone = ((gate, gate_all), (up, up_all))[which]
        columns = pl.ds(pl.multiple_of(peer[i] * units, 128), units)
        return remote(
            held.at[pl.ds(pl.multiple_of(core * half, half), half), columns],
            at_rows(everyone, w * depth + core * half, half),
            ffn_sem.at[0, which, i], ffn_sem.at[1, which, i], (c, peer[i]),
        )

    def pass_ffn(which, i):
        block = at_rows((gate_all, up_all)[which], origin[i] * depth + core * half, half)
        return remote(block, block, ff_sem.at[0, which, i], ff_sem.at[1, which, i], sibling)

    def keep_ffn(which):
        held, everyone = ((gate, gate_all), (up, up_all))[which]
        columns = pl.ds(pl.multiple_of(w * units, 128), units)
        return pltpu.make_async_copy(
            held.at[:, columns], at_rows(everyone, w * depth, depth), own_sem.at[2 + which]
        )

    def send_cot(i):
        return remote(cot, cot_all.at[w], cot_sem.at[0, i], cot_sem.at[1, i], (c, peer[i]))

    def keep_cot():
        return pltpu.make_async_copy(cot, cot_all.at[w], own_sem.at[4])

    def send_pair(i):
        to = lax.rem(c + i, ctx)
        return remote(
            qkv_stage.at[lax.rem(to, pairs)], pair.at[c],
            pair_sem.at[0, i], pair_sem.at[1, i], (to, w),
        )

    first_back = c // pairs * pairs
    own_pair = lax.rem(c, pairs)

    def back_copy(to, i):
        return remote(
            attn_stage.at[to], attn_in.at[own_pair],
            back_sem.at[0, i], back_sem.at[1, i], (to, w),
        )

    for i in range(1, ws):
        send_gain(i).start()
    for i in range(1, ws):
        send_x(i).start()
    keep_ffn(0).start()
    keep_ffn(1).start()
    keep_cot().start()
    for d in range(ws):
        for j in range(own_heads):
            h = d * own_heads + j
            w_stage[d, :, j * wide : (j + 1) * wide] = jnp.concatenate(
                [
                    wq[:, h * q_wide : (h + 1) * q_wide],
                    wk[:, h * HEAD_DIM : (h + 1) * HEAD_DIM],
                    wv[:, h * HEAD_DIM : (h + 1) * HEAD_DIM],
                ],
                axis=1,
            )
    for i in range(1, ws):
        send_w(i).start()
    w_all[w] = w_stage[w]
    total_gain = gains[...]
    for i in range(1, ws):
        send_gain(i).wait_recv()
        total_gain = total_gain + g_in[origin[i]]
    gains_all[...] = total_gain
    gain = total_gain[0:1]

    def norm_block(index, block):
        wide_block = block.astype(F32)
        factor = lax.rsqrt(jnp.mean(wide_block * wide_block, axis=-1, keepdims=True) + EPSILON)
        normed[index] = (wide_block * factor * gain).astype(BF)

    norm_block(w, x[...])
    for i in range(1, ws):
        send_x(i).wait_recv()
        norm_block(origin[i], x_all[origin[i]])
    for i in range(1, ws):
        send_w(i).wait_recv()
        pass_w(i).start()
    for i in range(1, ws):
        pass_w(i).wait_recv()
    for i in range(1, ws):
        for which in range(2):
            send_ffn(which, i).start()
    for i in range(1, ws):
        send_cot(i).start()

    left = normed[...].reshape(ws * rows, normed.shape[2])
    step = 256 if raw.shape[1] % 256 == 0 else 128
    for n in range(0, raw.shape[1], step):
        right = w_all[:, :, n : n + step].reshape(ws * depth, step)
        raw[:, n : n + step] = jnp.dot(left, right, preferred_element_type=F32)
    rope_copy(0).wait()
    rope_copy(1).wait()
    for s in range(ws):
        for j in range(own_heads):
            block = raw[s * rows : (s + 1) * rows, j * wide : (j + 1) * wide]
            turned = block * cos[...] + swap_lanes(block) * sin[...]
            qkv_stage[s * own_heads + j] = turned.astype(BF)
    for i in range(1, ctx):
        send_pair(i).start()
    pair[c] = qkv_stage[own_pair]

    def split(index):
        block = pair[index]
        here = pl.ds(pl.multiple_of(index * rows, rows), rows)
        for g in range(group):
            q_out[g, here, :] = block[:, g * HEAD_DIM : (g + 1) * HEAD_DIM]
        k_out[here, :] = block[:, q_wide : q_wide + HEAD_DIM]
        v_out[here, :] = block[:, q_wide + HEAD_DIM :]

    split(c)
    for i in range(1, ctx):
        from_c = lax.rem(c + ctx - i, ctx)
        send_pair(i).wait_recv()
        split(from_c)

    length = ctx * rows
    span = min(256, length)
    lane = lax.broadcasted_iota(jnp.int32, (span, HEAD_DIM), 1)

    def attend(start, keys, diagonal):
        here = pl.ds(start, span)
        heads = []
        allowed = start + lax.broadcasted_iota(
            jnp.int32, (span, keys), 0
        ) >= lax.broadcasted_iota(jnp.int32, (span, keys), 1)
        for g in range(group):
            scores = lax.dot_general(
                q_out[g, here, :], k_out[0:keys, :], (((1,), (1,)), ((), ())),
                preferred_element_type=F32,
            ) * HEAD_DIM**-0.5
            scores = jnp.where(allowed, scores, MASK_FILL)
            top = jnp.max(scores, axis=1, keepdims=True)
            weights = jnp.exp(scores - top)
            total = jnp.sum(weights, axis=1, keepdims=True)
            mixed = jnp.dot(
                weights.astype(BF), v_out[0:keys, :], preferred_element_type=F32
            ) / total
            pack[g, here, 0:HEAD_DIM] = mixed
            pack[g, here, HEAD_DIM:128] = jnp.where(
                lane[:, : 128 - HEAD_DIM] == 0, top, total
            )
            heads.append(mixed)
        low = jnp.concatenate(heads, axis=1).astype(BF)
        for b in range(span // rows):
            attn_stage[start // rows + b] = low[b * rows : (b + 1) * rows]

    if length <= 1024:
        for start in range(0, length, span):
            attend(start, start + span, start)
    else:

        def attend_at(index, _):
            attend(pl.multiple_of(index * span, span), length, 0)
            return 0

        lax.fori_loop(0, length // span, attend_at, 0)
    for i in range(1, pairs):
        back_copy(first_back + lax.rem(own_pair + i, pairs), i).start()
    attn_in[own_pair] = attn_stage[c]

    for i in range(1, ws):
        for which in range(2):
            send_ffn(which, i).wait_recv()
            pass_ffn(which, i).start()
    for i in range(1, pairs):
        source = lax.rem(own_pair + pairs - i, pairs)
        arriving = remote(
            attn_stage.at[c], attn_in.at[source],
            back_sem.at[0, i], back_sem.at[1, i], (first_back + source, w),
        )
        arriving.wait_recv()
    for i in range(1, ws):
        for which in range(2):
            pass_ffn(which, i).wait_recv()
        send_cot(i).wait_recv()
    keep_ffn(0).wait()
    keep_ffn(1).wait()
    keep_cot().wait()
    for i in range(1, ws):
        send_gain(i).wait_send()
        send_x(i).wait_send()
        send_w(i).wait_send()
        pass_w(i).wait_send()
        send_cot(i).wait_send()
        for which in range(2):
            send_ffn(which, i).wait_send()
            pass_ffn(which, i).wait_send()
    for i in range(1, ctx):
        send_pair(i).wait_send()
    for i in range(1, pairs):
        back_copy(first_back + lax.rem(own_pair + i, pairs), i).wait_send()


def front(x, gains, wq, wk, wv, gate, up, cot, cosines, sines, ws, ctx, own_heads, group):
    rows, features = x.shape
    depth = wq.shape[0]
    q_wide = group * HEAD_DIM
    wide = q_wide + 2 * HEAD_DIM
    pairs = ws * own_heads
    length = ctx * rows
    units = gate.shape[1] // ws
    vmem, anywhere = pl.BlockSpec(memory_space=pltpu.VMEM), pl.BlockSpec(memory_space=pl.ANY)
    shape = jax.ShapeDtypeStruct
    return pl.pallas_call(
        functools.partial(front_kernel, ws, ctx, own_heads, group),
        out_shape=[
            shape((ws, rows, features), BF),
            shape((ws, depth, own_heads * wide), BF),
            shape((group, length, HEAD_DIM), BF),
            shape((length, HEAD_DIM), BF),
            shape((length, HEAD_DIM), BF),
            shape((group, length, 128), F32),
            shape((pairs, rows, q_wide), BF),
            shape((features, units), BF),
            shape((features, units), BF),
            shape((ws, rows, features), BF),
            shape(gains.shape, F32),
        ],
        in_specs=[vmem] * 5 + [anywhere] * 5,
        out_specs=[vmem] * 7 + [anywhere] * 3 + [vmem],
        scratch_shapes=[
            pltpu.VMEM((ws, rows, features), BF),
            pltpu.VMEM((ws,) + gains.shape, F32),
            pltpu.VMEM((ws, depth, own_heads * wide), BF),
            pltpu.VMEM((ws * rows, own_heads * wide), F32),
            pltpu.VMEM((pairs, rows, wide), BF),
            pltpu.VMEM((ctx, rows, wide), BF),
            pltpu.VMEM((ctx, rows, q_wide), BF),
            pltpu.VMEM((rows, wide), F32),
            pltpu.VMEM((rows, wide), F32),
            dma(2, ws), dma(2, ws), dma(2, ws), dma(2, ws), dma(2, 2, ws), dma(2, 2, ws),
            dma(2, ws), dma(2, ctx), dma(2, pairs), dma(5),
        ],
        compiler_params=pltpu.CompilerParams(
            collective_id=1, has_side_effects=True, vmem_limit_bytes=60 << 20
        ),
        name="front",
    )(x, gains, wq, wk, wv, gate, up, cot, cosines, sines)


def dot_bt(left, right):
    return lax.dot_general(left, right, (((1,), (1,)), ((), ())), preferred_element_type=F32)


def middle_kernel(
    ws, ctx, own_heads, group,
    x, attn, w_out, gains, gate_all, up_all, w_down_all, cot_all,
    residual_out, normed, hidden, grad_gate, grad_up, grad_sent, grad_keep, out_sent, out_keep,
    gate, up, w_down, cot, sent, landed, grad_hidden, keep, load_sem, rs_sem, ag_sem,
):
    c, w = lax.axis_index("ctx"), lax.axis_index("ws")
    rows, features = x.shape
    q_wide = group * HEAD_DIM
    units = gate.shape[1]
    total_rows = ws * rows
    tile = 256

    def load(i):
        return pltpu.make_async_copy(
            (gate_all, up_all, w_down_all, cot_all)[i], (gate, up, w_down, cot)[i], load_sem.at[i]
        )

    for i in (3, 2, 0, 1):
        load(i).start()
    greet([(c, lax.rem(w + i, ws)) for i in range(1, ws)])

    def send_sum(i):
        to = lax.rem(w + i, ws)
        return remote(sent.at[to], landed.at[w], rs_sem.at[0, i], rs_sem.at[1, i], (c, to))

    def send_rows(i):
        return remote(
            normed.at[w], normed.at[w], ag_sem.at[0, i], ag_sem.at[1, i],
            (c, lax.rem(w + i, ws)),
        )

    def project(i, _):
        s = lax.rem(w + i, ws)
        part = jnp.zeros((rows, features), F32)
        for j in range(own_heads):
            part = part + jnp.dot(
                attn[s * own_heads + j], w_out[j * q_wide : (j + 1) * q_wide, :],
                preferred_element_type=F32,
            )

        @pl.when(i < ws)
        def _():
            sent[s] = part.astype(BF)
            send_sum(i).start()

        @pl.when(i == ws)
        def _():
            keep[...] = part

        return 0

    lax.fori_loop(1, ws + 1, project, 0)

    load(3).wait()
    load(2).wait()

    def hidden_back(n, _):
        here = pl.ds(pl.multiple_of(n * tile, tile), tile)
        grad_hidden[:, here] = dot_bt(cot[...].reshape(total_rows, features), w_down[here, :])
        return 0

    lax.fori_loop(0, units // tile, hidden_back, 0)
    load(0).wait()
    load(1).wait()

    residual = x[...].astype(F32) + keep[...]
    for i in range(1, ws):
        send_sum(i).wait_recv()
        residual = residual + landed[lax.rem(w + ws - i, ws)].astype(F32)
    gain = gains[1:2]
    factor = lax.rsqrt(jnp.mean(residual * residual, axis=-1, keepdims=True) + EPSILON)
    normed[w] = (residual * factor * gain).astype(BF)
    for i in range(1, ws):
        send_rows(i).start()
    residual_out[...] = residual

    def feed(i, _):
        s = lax.rem(w + ws - i, ws)
        here = pl.ds(pl.multiple_of(s * rows, rows), rows)

        @pl.when(i > 0)
        def _():
            send_rows(i).wait_recv()

        block = normed[s]

        def columns(n, _):
            cut = pl.ds(pl.multiple_of(n * tile, tile), tile)
            gate_proj = jnp.dot(block, gate[:, cut], preferred_element_type=F32)
            up_proj = jnp.dot(block, up[:, cut], preferred_element_type=F32)
            sigmoid = 1.0 / (1.0 + jnp.exp(-gate_proj))
            activation = gate_proj * sigmoid
            grad = grad_hidden[here, cut]
            hidden[here, cut] = (activation * up_proj).astype(BF)
            grad_up[here, cut] = (grad * activation).astype(BF)
            grad_gate[here, cut] = (
                grad * up_proj * sigmoid * (1.0 + gate_proj * (1.0 - sigmoid))
            ).astype(BF)
            return 0

        lax.fori_loop(0, units // tile, columns, 0)
        to = lax.rem(w + ws - i, ws)

        def back(n, _):
            cut = pl.ds(pl.multiple_of(n * tile, tile), tile)
            part = dot_bt(grad_gate[here, :], gate[cut, :]) + dot_bt(grad_up[here, :], up[cut, :])

            @pl.when(i > 0)
            def _():
                grad_sent[to, :, cut] = part.astype(BF)

            @pl.when(i == 0)
            def _():
                grad_keep[:, cut] = part

            return 0

        lax.fori_loop(0, features // tile, back, 0)
        return 0

    lax.fori_loop(0, ws, feed, 0)

    def down_columns(n, _):
        cut = pl.ds(pl.multiple_of(n * tile, tile), tile)
        part = jnp.dot(hidden[...], w_down[:, cut], preferred_element_type=F32)
        out_sent[:, :, cut] = part.astype(BF).reshape(ws, rows, tile)
        own = hidden[pl.ds(pl.multiple_of(w * rows, rows), rows), :]
        out_keep[:, cut] = jnp.dot(own, w_down[:, cut], preferred_element_type=F32)
        return 0

    lax.fori_loop(0, features // tile, down_columns, 0)
    for i in range(1, ws):
        send_sum(i).wait_send()
        send_rows(i).wait_send()


def middle(x, attn, w_out, gains, gate, up, w_down, cot, ws, ctx, own_heads, group):
    rows, features = x.shape
    units = gate.shape[1]
    vmem, anywhere = pl.BlockSpec(memory_space=pltpu.VMEM), pl.BlockSpec(memory_space=pl.ANY)
    shape, held = jax.ShapeDtypeStruct, pltpu.VMEM
    total = ws * rows
    return pl.pallas_call(
        functools.partial(middle_kernel, ws, ctx, own_heads, group),
        out_shape=[
            shape((rows, features), F32),
            shape((ws, rows, features), BF),
            shape((total, units), BF),
            shape((total, units), BF),
            shape((total, units), BF),
            shape((ws, rows, features), BF),
            shape((rows, features), F32),
            shape((ws, rows, features), BF),
            shape((rows, features), F32),
        ],
        in_specs=[vmem] * 4 + [anywhere] * 4,
        out_specs=[vmem] * 9,
        scratch_shapes=[
            held((features, units), BF),
            held((features, units), BF),
            held((units, features), BF),
            held((ws, rows, features), BF),
            held((ws, rows, features), BF),
            held((ws, rows, features), BF),
            held((total, units), F32),
            held((rows, features), F32),
            dma(4), dma(2, ws), dma(2, ws),
        ],
        compiler_params=pltpu.CompilerParams(
            collective_id=2, has_side_effects=True, vmem_limit_bytes=60 << 20
        ),
        name="middle",
    )(x, attn, w_out, gains, gate, up, w_down, cot)


SKEW = 2
ROWS = (32, 48, 48, 32, 64)
TICK_NORM, TICK_ATTENDED, TICK_PAIRS, TICK_GATHER = 4, 9, 12, 4


def back_kernel(
    ws, ctx, group, own_heads, moved, rows, ticks,
    x, gains, cosines, sines, q_all, k_all, v_all, pack_all, attn_all, normed_all, w_qkv_all,
    w_out_all, cot_all, residual_all, ffn_all, hidden_all, gate_all, up_all, grad_sent, grad_keep,
    out_sent, out_keep,
    output, grad_input, gain_out, *refs,
):
    count = len(moved)
    outs, refs = refs[:count], refs[count:]
    parts, refs = refs[:count], refs[count:]
    sib_buf, refs = refs[:count], refs[count:]
    red_in, refs = refs[:count], refs[count:]
    red_send, red_recv, hand_send, hand_recv, bc_send, bc_recv, core_send, core_recv = (
        refs[i * count : (i + 1) * count] for i in range(8)
    )
    (
        q, k, v, pack, attn, normed, w_qkv, w_out, cot, residual, hidden, grad_gate, grad_up,
        own_part, turned, turned_hidden, branch, pair_stage, grad_pair, grad_residual,
        grad_q, grad_k, grad_v, key_turned, back_stage, grad_in, grad_rows,
        sent, landed, keep, own_gain, ws_gain, ctx_gain, cos, sin,
        sib_send, sib_recv, load_sem, ag_sem, to_pair_sem, pair_sem, rs_sem, gain_sem, wide_sem,
        rope_sem,
    ) = refs[8 * count :]
    c, w = lax.axis_index("ctx"), lax.axis_index("ws")
    core = lax.rem(c, 2)
    place, line = c // 2, ctx // 2
    sibling = (c + 1 - 2 * core, w)
    before, after = (c - 2, w), (c + 2, w)
    tokens, features = x.shape
    q_wide = group * HEAD_DIM
    wide = q_wide + 2 * HEAD_DIM
    pairs = ws * own_heads
    length = ctx * tokens
    depth = features // ws
    total_rows = ws * tokens
    units = hidden.shape[1]

    sources = (
        hidden_all, cot_all, ffn_all, gate_all, up_all, grad_keep, residual_all, w_out_all,
        attn_all, q_all, k_all, v_all, pack_all, w_qkv_all, normed_all, out_keep,
    )
    targets = (
        hidden, cot, normed, grad_gate, grad_up, own_part, residual, w_out,
        attn, q, k, v, pack, w_qkv, normed, own_part,
    )

    def load(i):
        return pltpu.make_async_copy(sources[i], targets[i], load_sem.at[i])

    for i in range(14):
        if length <= 1024 or i not in (9, 12):
            load(i).start()
    greet(
        [(lax.rem(c + i, ctx), w) for i in range(1, ctx)]
        + [(c, lax.rem(w + i, ws)) for i in range(1, ws)]
    )

    def send_sum(turn, i):
        to = lax.rem(w + i, ws)
        return remote(
            (grad_sent, out_sent, sent)[turn].at[to], landed.at[turn % 2, w],
            rs_sem.at[0, turn, i], rs_sem.at[1, turn, i], (c, to),
        )

    def landed_sum(turn, total):
        for i in range(1, ws):
            send_sum(turn, i).wait_recv()
            total = total + landed[turn % 2, lax.rem(w + ws - i, ws)].astype(F32)
        return total

    for i in range(1, ws):
        send_sum(0, i).start()

    def across_cores(i):
        half = parts[i].at[:, 1 - core] if moved[i] else parts[i].at[1 - core]
        return remote(half, sib_buf[i], sib_send.at[i], sib_recv.at[i], sibling)

    def spot(i, p, odd):
        if not moved[i]:
            return 2 * p + odd, None
        block = p // (ws // 2)
        return block, 2 * lax.rem(p, ws // 2) + lax.rem(block + odd, 2)

    def cut(i, block):
        return pl.ds(pl.multiple_of(block * rows[i], rows[i]), rows[i])

    def piece(i, p, odd, of):
        block, step = spot(i, p, odd)
        if not moved[i]:
            ref = parts[i].at[core] if of is parts else of[i]
            return ref.at[cut(i, block), :]
        owner = lax.rem(w + step, ws)
        ref = parts[i].at[owner, core] if of is parts else of[i].at[owner]
        return ref.at[cut(i, block), :]

    def final(i, p, odd, half, source):
        block, _ = spot(i, p, odd)
        if not moved[i]:
            return outs[i].at[half, cut(i, block), :]
        n = parts[i].shape[-1]
        columns = pl.ds(pl.multiple_of(source * n, 128), n)
        return outs[i].at[half, cut(i, block), columns]

    def source_of(i, p, odd):
        _, step = spot(i, p, odd)
        return None if step is None else lax.rem(w + ws - step, ws)

    def local(i, p, odd):
        here = piece(i, p, odd, parts)[...].astype(F32)
        return here + piece(i, p, odd, sib_buf)[...].astype(F32)

    def up_line(i, p, odd):
        e = 2 * p + odd
        return remote(
            piece(i, p, odd, parts), piece(i, p, odd, red_in),
            red_send[i].at[e], red_recv[i].at[e], after if odd else before,
        )

    def hand_over(i, p, odd):
        _, step = spot(i, p, odd)
        e = 2 * p + odd
        return remote(
            piece(i, p, odd, parts), final(i, p, odd, core, w),
            hand_send[i].at[e], hand_recv[i].at[e], (c, lax.rem(w + step, ws)),
        )

    def hand_here(i, p, odd):
        return pltpu.make_async_copy(
            piece(i, p, odd, parts), final(i, p, odd, core, w), hand_recv[i].at[2 * p + odd]
        )

    def down_line(i, p, odd):
        total = final(i, p, odd, core, source_of(i, p, odd))
        e = 2 * p + odd
        return remote(
            total, total, bc_send[i].at[e], bc_recv[i].at[e], before if odd else after
        )

    def over(i, p, odd, half):
        total = final(i, p, odd, half, source_of(i, p, odd))
        e = 2 * p + odd
        return remote(total, total, core_send[i].at[e], core_recv[i].at[e], sibling)

    def ends(odd):
        low, high = place == 0, place == line - 1
        return (low, high) if odd else (high, low)

    def either(i, p, odd, here, there):
        _, step = spot(i, p, odd)
        if step is None:
            here()
        else:
            pl.when(step == 0)(here)
            pl.when(step != 0)(there)

    def reduce_chunk(i, p, odd):
        start, end = ends(odd)

        @pl.when(start)
        def _():
            piece(i, p, odd, parts)[...] = local(i, p, odd).astype(BF)
            up_line(i, p, odd).start()

        @pl.when(jnp.logical_not(start))
        def _():
            up_line(i, p, odd).wait_recv()
            total = local(i, p, odd) + piece(i, p, odd, red_in)[...].astype(F32)
            piece(i, p, odd, parts)[...] = total.astype(BF)

            @pl.when(jnp.logical_not(end))
            def _():
                up_line(i, p, odd).start()

            @pl.when(end)
            def _():
                either(
                    i, p, odd,
                    lambda: hand_here(i, p, odd).start(), lambda: hand_over(i, p, odd).start(),
                )

    def spread_chunk(i, p, odd):
        end, start = ends(odd)

        @pl.when(start)
        def _():
            def arrived():
                total = final(i, p, odd, core, source_of(i, p, odd))
                e = 2 * p + odd
                remote(
                    total, total, hand_send[i].at[e], hand_recv[i].at[e], (c, lax.rem(w + 1, ws))
                ).wait_recv()

            either(i, p, odd, lambda: hand_here(i, p, odd).wait(), arrived)

        @pl.when(jnp.logical_not(start))
        def _():
            down_line(i, p, odd).wait_recv()

        @pl.when(jnp.logical_not(end))
        def _():
            down_line(i, p, odd).start()

        over(i, p, odd, core).start()

    counts = [red_send[i].shape[0] // 2 for i in range(count)]
    first, total_chunks = [], 0
    for i in range(count):
        first.append(total_chunks)
        total_chunks += counts[i]
    lasts = first[1:] + [total_chunks]
    hops = (line - 1 - place, place)

    def chain(t):
        for i in range(count):

            @pl.when(t == first[i])
            def _():
                across_cores(i).wait_recv()

        for odd in range(2):
            at = t - SKEW * hops[odd]
            down = t - SKEW * (2 * line - 1 - hops[odd])
            for i in range(count):

                @pl.when((at >= first[i]) & (at < lasts[i]))
                def _():
                    reduce_chunk(i, at - first[i], odd)

                @pl.when((down >= first[i]) & (down < lasts[i]))
                def _():
                    spread_chunk(i, down - first[i], odd)

    def down_weights():
        load(0).wait()
        load(1).wait()

        def turn(n, _):
            here = pl.ds(pl.multiple_of(n * 256, 256), 256)
            turned_hidden[here, :] = hidden[:, here].T
            return 0

        lax.fori_loop(0, units // 256, turn, 0)
        size = units // 4
        every = cot[...].reshape(total_rows, features)
        for h in range(2):
            for n in range(2):
                at = (2 * h + n) * size
                parts[0][h, n * size : (n + 1) * size, :] = jnp.dot(
                    turned_hidden[at : at + size, :], every, preferred_element_type=F32
                ).astype(BF)
        across_cores(0).start()

    def turn_rows():
        def turn(n, _):
            here = pl.ds(pl.multiple_of(n * 256, 256), 256)
            turned[here, :] = normed[:, :, here].reshape(total_rows, 256).T
            return 0

        lax.fori_loop(0, features // 256, turn, 0)

    def row_products(i, right):
        half = depth // 2

        def one(o, _):
            for h in range(2):
                here = pl.ds(pl.multiple_of(o * depth + h * half, half), half)
                parts[i][o, h] = jnp.dot(
                    turned[here, :], right[...], preferred_element_type=F32
                ).astype(BF)
            return 0

        lax.fori_loop(0, ws, one, 0)
        across_cores(i).start()

    def gate_weights():
        load(2).wait()
        load(3).wait()
        turn_rows()
        load(14).start()
        row_products(1, grad_gate)

    def up_weights():
        load(4).wait()
        row_products(2, grad_up)

    def send_rows(i):
        return remote(
            branch.at[w], branch.at[w], ag_sem.at[0, i], ag_sem.at[1, i],
            (c, lax.rem(w + i, ws)),
        )

    def ffn_norm_back():
        load(5).wait()
        load(6).wait()
        grad_normed = landed_sum(0, own_part[...])
        load(15).start()
        here = residual[...]
        factor = lax.rsqrt(jnp.mean(here * here, axis=-1, keepdims=True) + EPSILON)
        unit = here * factor
        own_gain[...] = jnp.broadcast_to(
            jnp.sum(grad_normed * unit, axis=0, keepdims=True), own_gain.shape
        )
        grad = grad_normed * gains[1:2]
        mean = jnp.mean(grad * unit, axis=-1, keepdims=True)
        back_grad = cot[w].astype(F32) + factor * (grad - unit * mean)
        grad_residual[...] = back_grad
        branch[w] = back_grad.astype(BF)
        for i in range(1, ws):
            send_rows(i).start()

    def send_pair(i):
        to = lax.rem(c + i, ctx)
        return remote(
            pair_stage.at[lax.rem(to, pairs)], grad_pair.at[c],
            to_pair_sem.at[0, i], to_pair_sem.at[1, i], (to, w),
        )

    def attended_back():
        load(7).wait()
        for i in range(ws):
            s = lax.rem(w + ws - i, ws)
            if i:
                send_rows(i).wait_recv()
            grad_low = dot_bt(branch[s], w_out[...]).astype(BF)
            for j in range(own_heads):
                pair_stage[s * own_heads + j] = grad_low[:, j * q_wide : (j + 1) * q_wide]
        for i in range(1, ctx):
            send_pair(i).start()
        grad_pair[c] = pair_stage[lax.rem(c, pairs)]
        for i in range(1, ws):
            send_sum(1, i).start()

    def out_weights():
        load(8).wait()
        half = own_heads * q_wide // 2
        for h in range(2):
            j, low = divmod(h * half, q_wide)
            side = jnp.concatenate([attn[s * own_heads + j] for s in range(ws)], axis=0)
            parts[3][h] = jnp.dot(
                side.T[low : low + half], branch[...].reshape(total_rows, features),
                preferred_element_type=F32,
            ).astype(BF)
        across_cores(3).start()

    def finish_output():
        load(15).wait()
        output[...] = (landed_sum(1, residual[...] + own_part[...])).astype(BF)

    first_back = c // pairs * pairs
    own_pair = lax.rem(c, pairs)
    span = min(256, length) if length <= 1024 else tokens

    def back_unit(g, start, low, keys):
        here, there = pl.ds(start, span), pl.ds(low, keys)
        query = q[g, here, :]
        grad = (
            grad_pair[pl.ds(start // tokens, span // tokens), :, g * HEAD_DIM : (g + 1) * HEAD_DIM]
        ).reshape(span, HEAD_DIM)
        kept = pack[g, here, :]
        kept_turned = kept.T
        top, total = kept_turned[HEAD_DIM : HEAD_DIM + 1], kept_turned[HEAD_DIM + 1 : HEAD_DIM + 2]
        grad_wide = grad.astype(F32)
        delta = jnp.sum(grad_wide.T * kept_turned[:HEAD_DIM], axis=0, keepdims=True)
        scaled = (grad_wide / kept[:, HEAD_DIM + 1 : HEAD_DIM + 2]).astype(BF)
        scores = dot_bt(k[there, :], query) * HEAD_DIM**-0.5
        allowed = start + lax.broadcasted_iota(
            jnp.int32, (keys, span), 1
        ) >= low + lax.broadcasted_iota(jnp.int32, (keys, span), 0)
        weights = jnp.exp(jnp.where(allowed, scores, MASK_FILL) - top)
        grad_probs = dot_bt(v[there, :], grad)
        grad_scores = (weights * (1.0 / total) * (grad_probs - delta)).astype(BF)
        grad_k[there, :] += jnp.dot(grad_scores, query, preferred_element_type=F32)
        grad_v[there, :] += jnp.dot(weights.astype(BF), scaled, preferred_element_type=F32)
        turned_grad = jnp.dot(
            key_turned[:, there], grad_scores, preferred_element_type=F32
        )
        if length <= 1024:
            grad_q[g, here, :] = turned_grad.T
        else:
            grad_q[g, here, :] += turned_grad.T

    def send_back(to, i):
        return remote(
            back_stage.at[to], grad_in.at[own_pair],
            pair_sem.at[0, i], pair_sem.at[1, i], (to, w),
        )

    def rope_copy(i, start):
        table, kept = ((cosines, cos), (sines, sin))[i]
        return pltpu.make_async_copy(table.at[pl.ds(start, span), :], kept, rope_sem.at[i])

    def finish_rows(start):
        here = pl.ds(start, span)
        rope_copy(0, start).wait()
        rope_copy(1, start).wait()
        scale = HEAD_DIM**-0.5
        block = jnp.concatenate(
            [grad_q[g, here, :] * scale for g in range(group)]
            + [grad_k[here, :] * scale, grad_v[here, :]],
            axis=1,
        )
        block = (block * cos[...] - swap_lanes(block) * sin[...]).astype(BF)
        for b in range(span // tokens):
            to = start // tokens + b
            back_stage[to] = block[b * tokens : (b + 1) * tokens]

    def send_rows_back(to):
        step = lax.rem(to - c + ctx, pairs)

        @pl.when((to // pairs == c // pairs) & (to != c))
        def _():
            send_back(to, step).start()

        @pl.when(to == c)
        def _():
            grad_in[own_pair] = back_stage[to]

    def prepare():
        for i in range(9, 13):
            load(i).wait()
        for i in range(1, ctx):
            send_pair(i).wait_recv()
        grad_k[...] = jnp.zeros(grad_k.shape, F32)
        grad_v[...] = jnp.zeros(grad_v.shape, F32)
        key_turned[...] = k[...].T

    def turn_normed():
        load(14).wait()
        turn_rows()

    def gather_back():
        for i in range(1, pairs):
            source = lax.rem(own_pair + pairs - i, pairs)
            arriving = remote(
                back_stage.at[c], grad_in.at[source],
                pair_sem.at[0, i], pair_sem.at[1, i], (first_back + source, w),
            )
            arriving.wait_recv()
        for s in range(ws):
            for j in range(own_heads):
                grad_rows[s * tokens : (s + 1) * tokens, j * wide : (j + 1) * wide] = grad_in[
                    s * own_heads + j
                ]

    def sum_rows():
        load(13).wait()

        def one(i, _):
            s = lax.rem(w + i, ws)
            block = grad_rows[pl.ds(pl.multiple_of(s * tokens, tokens), tokens), :]
            for n in range(0, ws):
                part = dot_bt(block, w_qkv[n])

                @pl.when(i < ws)
                def _():
                    sent[s, :, n * depth : (n + 1) * depth] = part.astype(BF)

                @pl.when(i == ws)
                def _():
                    keep[:, n * depth : (n + 1) * depth] = part

            @pl.when(i < ws)
            def _():
                send_sum(2, i).start()

            return 0

        lax.fori_loop(1, ws + 1, one, 0)

    def weight_sums():
        row_products(4, grad_rows)

    def send_gain(i):
        return remote(
            own_gain, ws_gain.at[w], gain_sem.at[0, i], gain_sem.at[1, i],
            (c, lax.rem(w + i, ws)),
        )

    def send_wide(i):
        return remote(
            ws_gain.at[w], ctx_gain.at[c], wide_sem.at[0, i], wide_sem.at[1, i],
            (lax.rem(c + i, ctx), w),
        )

    def finish_input():
        total = landed_sum(2, keep[...])
        inputs = x[...].astype(F32)
        factor = lax.rsqrt(jnp.mean(inputs * inputs, axis=-1, keepdims=True) + EPSILON)
        unit = inputs * factor
        row = lax.broadcasted_iota(jnp.int32, own_gain.shape, 0)
        attn_gain = jnp.sum(total * unit, axis=0, keepdims=True)
        own_gain[...] = jnp.where(row == 0, attn_gain, own_gain[...])
        for i in range(1, ws):
            send_gain(i).start()
        grad = total * gains[0:1]
        mean = jnp.mean(grad * unit, axis=-1, keepdims=True)
        grad_input[...] = grad_residual[...] + factor * (grad - unit * mean)

    def widen_gain():
        total = own_gain[...]
        for i in range(1, ws):
            send_gain(i).wait_recv()
            total = total + ws_gain[lax.rem(w + ws - i, ws)]
        ws_gain[w] = total
        for i in range(1, ctx):
            send_wide(i).start()

    def finish_gain():
        total = ws_gain[w]
        for i in range(1, ctx):
            send_wide(i).wait_recv()
            total = total + ctx_gain[lax.rem(c + ctx - i, ctx)]
        gain_out[...] = total

    events = [[] for _ in range(ticks)]

    def put(at, *todo):
        events[min(at, ticks - 1)].extend(todo)

    put(0, gate_weights)
    put(1, up_weights)
    put(TICK_NORM, ffn_norm_back)
    put(TICK_ATTENDED, attended_back, out_weights)
    put(TICK_PAIRS, prepare)
    starts = list(range(0, length, span))[::-1]
    if length <= 1024:
        for n, start in enumerate(starts):

            def one_start(start=start):
                rope_copy(0, start).start()
                rope_copy(1, start).start()
                for g in range(group):
                    back_unit(g, start, 0, start + span)
                finish_rows(start)
                for b in range(span // tokens):
                    send_rows_back(start // tokens + b)

            put(TICK_PAIRS + n, one_start)
        at = TICK_PAIRS + len(starts)
    else:

        def all_starts():
            grad_q[...] = jnp.zeros(grad_q.shape, F32)

            def one_start(n, _):
                start = pl.multiple_of(n * span, span)

                def one_block(m, _):
                    low = pl.multiple_of(m * 512, 512)

                    @pl.when(low < start + span)
                    def _():
                        for g in range(group):
                            back_unit(g, start, low, 512)

                    return 0

                lax.fori_loop(0, length // 512, one_block, 0)
                return 0

            lax.fori_loop(0, length // span, one_start, 0)

            def finish(n, _):
                start = pl.multiple_of(n * span, span)
                rope_copy(0, start).start()
                rope_copy(1, start).start()
                finish_rows(start)
                return 0

            lax.fori_loop(0, length // span, finish, 0)
            for to in range(ctx):
                send_rows_back(to)

        put(TICK_PAIRS, all_starts)
        at = TICK_PAIRS + 1
    put(at, turn_normed)
    put(at + 1, finish_output)
    put(at + TICK_GATHER, gather_back, weight_sums, sum_rows)
    put(at + TICK_GATHER + 5, finish_input)
    put(at + TICK_GATHER + 7, widen_gain)
    put(at + TICK_GATHER + 10, finish_gain)

    down_weights()

    def tick(t, _):
        chain(t)
        for n, todo in enumerate(events):
            if todo:

                @pl.when(t == n)
                def _():
                    for event in todo:
                        event()

        return 0

    lax.fori_loop(0, ticks, tick, 0)

    for i in range(count):

        def finish_pair(p, _):
            for odd in range(2):
                _, reduce_end = ends(odd)
                spread_end, _ = ends(odd)

                @pl.when(jnp.logical_not(reduce_end))
                def _():
                    up_line(i, p, odd).wait_send()

                if moved[i]:
                    _, step = spot(i, p, odd)

                    @pl.when(reduce_end & (step != 0))
                    def _():
                        hand_over(i, p, odd).wait_send()

                @pl.when(jnp.logical_not(spread_end))
                def _():
                    down_line(i, p, odd).wait_send()

                over(i, p, odd, core).wait_send()
                over(i, p, odd, 1 - core).wait_recv()
            return 0

        lax.fori_loop(0, counts[i], finish_pair, 0)
    for i in range(count):
        across_cores(i).wait_send()
    for i in range(1, ws):
        for turn in range(3):
            send_sum(turn, i).wait_send()
        send_rows(i).wait_send()
        send_gain(i).wait_send()
    for i in range(1, ctx):
        send_wide(i).wait_send()
        send_pair(i).wait_send()
    for i in range(1, pairs):
        send_back(first_back + lax.rem(own_pair + i, pairs), i).wait_send()


def back(
    x, gains, cosines, sines, q, k, v, pack, attn, normed, w_qkv, w_out, cot, residual, ffn,
    hidden, grad_gate, grad_up, grad_sent, grad_keep, out_sent, out_keep, ws, ctx, own_heads,
):
    tokens, features = x.shape
    group, length, _ = q.shape
    units = hidden.shape[1]
    q_wide = group * HEAD_DIM
    wide = q_wide + 2 * HEAD_DIM
    pairs = ws * own_heads
    span = min(256, length) if length <= 1024 else tokens
    kept = length if length <= 1024 else span
    depth = features // ws
    total_rows = ws * tokens
    moved = (False, True, True, False, True)
    held = pltpu.VMEM
    widths = [features, units, units, features, own_heads * wide]
    halves = [units // 2, depth // 2, depth // 2, own_heads * q_wide // 2, depth // 2]
    rows, parts, sib, red, outs, counts = [], [], [], [], [], []
    for is_moved, n, half, want in zip(moved, widths, halves, ROWS):
        while half % want or not is_moved and half % (2 * want):
            want -= 16
        rows.append(want)
        lead = (ws,) if is_moved else ()
        parts.append(held(lead + (2, half, n), BF))
        sib.append(held(lead + (half, n), BF))
        red.append(held(lead + (half, n), BF))
        outs.append((2, half, ws * n if is_moved else n))
        counts.append(half // want * (ws if is_moved else 1))
    ticks = sum(counts) // 2 + SKEW * (ctx - 1)
    k_count = len(parts)
    vmem, anywhere = pl.BlockSpec(memory_space=pltpu.VMEM), pl.BlockSpec(memory_space=pl.ANY)
    shape = jax.ShapeDtypeStruct
    results = pl.pallas_call(
        functools.partial(
            back_kernel, ws, ctx, group, own_heads, moved, tuple(rows), ticks
        ),
        out_shape=[
            shape((tokens, features), BF), shape((tokens, features), F32), shape(gains.shape, F32)
        ]
        + [shape(o, BF) for o in outs],
        in_specs=[vmem] * 2 + [anywhere] * 20,
        out_specs=[vmem] * 3 + [anywhere] * k_count,
        scratch_shapes=parts
        + sib
        + red
        + [dma(n) for _ in range(8) for n in counts]
        + [
            held((group, kept, HEAD_DIM), BF),
            held(k.shape, BF),
            held(v.shape, BF),
            held((group, kept, 128), F32),
            held(attn.shape, BF),
            held(normed.shape, BF),
            held(w_qkv.shape, BF),
            held(w_out.shape, BF),
            held(cot.shape, BF),
            held((tokens, features), F32),
            held((total_rows, units), BF),
            held((total_rows, units), BF),
            held((total_rows, units), BF),
            held((tokens, features), F32),
            held((features, total_rows), BF),
            held((units, total_rows), BF),
            held((ws, tokens, features), BF),
            held((pairs, tokens, q_wide), BF),
            held((ctx, tokens, q_wide), BF),
            held((tokens, features), F32),
            held((group, kept, HEAD_DIM), F32),
            held((length, HEAD_DIM), F32),
            held((length, HEAD_DIM), F32),
            held((HEAD_DIM, length), BF),
            held((ctx, tokens, wide), BF),
            held((pairs, tokens, wide), BF),
            held((total_rows, own_heads * wide), BF),
            held((ws, tokens, features), BF),
            held((2, ws, tokens, features), BF),
            held((tokens, features), F32),
            held(gains.shape, F32),
            held((ws,) + gains.shape, F32),
            held((ctx,) + gains.shape, F32),
            held((span, wide), F32),
            held((span, wide), F32),
            dma(k_count), dma(k_count), dma(16), dma(2, ws), dma(2, ctx), dma(2, pairs),
            dma(2, 3, ws), dma(2, ws), dma(2, ctx), dma(2),
        ],
        compiler_params=pltpu.CompilerParams(
            collective_id=3, has_side_effects=True, vmem_limit_bytes=63 << 20
        ),
        name="back",
    )(
        x, gains, cosines, sines, q, k, v, pack, attn, normed, w_qkv, w_out, cot, residual, ffn,
        hidden, grad_gate, grad_up, grad_sent, grad_keep, out_sent, out_keep,
    )
    sums = [s.reshape(s.shape[0] * s.shape[1], s.shape[2]) for s in results[3:]]
    return results[0], results[1], results[2], sums


def tail_kernel(ws, group, *refs):
    low, refs = refs[:8], refs[8:]
    down, out, gate, up, qkv, output, grad_input, gain_sums = low
    (
        output_out, grad_input_out, attn_gain, g_query, g_key, g_value, g_out, ffn_gain, g_gate,
        g_up, g_down,
    ) = refs
    q_wide = group * HEAD_DIM
    wide = q_wide + 2 * HEAD_DIM
    output_out[...] = output[...]
    grad_input_out[...] = grad_input[...]
    g_down[...] = down[...].astype(F32)
    g_out[...] = out[...].astype(F32)
    g_gate[...] = gate[...].astype(F32)
    g_up[...] = up[...].astype(F32)
    heads = qkv.shape[1] // wide
    blocks = [qkv[:, h * wide : (h + 1) * wide].astype(F32) for h in range(heads)]
    g_query[...] = jnp.concatenate([b[:, :q_wide] for b in blocks], axis=1)
    g_key[...] = jnp.concatenate([b[:, q_wide : q_wide + HEAD_DIM] for b in blocks], axis=1)
    g_value[...] = jnp.concatenate([b[:, q_wide + HEAD_DIM :] for b in blocks], axis=1)
    w = lax.axis_index("ws")
    depth = attn_gain.shape[1]
    for i in range(ws):

        @pl.when(w == i)
        def _():
            here = gain_sums[:, i * depth : (i + 1) * depth]
            attn_gain[...] = here[0:1]
            ffn_gain[...] = here[1:2]


def tail(down, out, gate, up, qkv, output, grad_input, gain_sums, ws, group):
    depth = qkv.shape[0]
    steps = depth // 48
    features = out.shape[1]
    q_total = qkv.shape[1] * group // (group + 2)
    k_total = q_total // group
    shape = jax.ShapeDtypeStruct

    def split(rows, columns):
        return pl.BlockSpec((rows // steps, columns), lambda n: (n, 0))

    def whole(rows, columns):
        return pl.BlockSpec((rows, columns), lambda n: (0, 0))

    out_shape = [
        shape(output.shape, BF), shape(grad_input.shape, F32), shape((1, depth), F32),
        shape((depth, q_total), F32), shape((depth, k_total), F32), shape((depth, k_total), F32),
        shape(out.shape, F32), shape((1, depth), F32), shape(gate.shape, F32),
        shape(up.shape, F32), shape(down.shape, F32),
    ]
    return pl.pallas_call(
        functools.partial(tail_kernel, ws, group),
        grid=(steps,),
        out_shape=out_shape,
        in_specs=[split(*a.shape) for a in (down, out, gate, up, qkv, output, grad_input)]
        + [whole(*gain_sums.shape)],
        out_specs=[
            whole(*o.shape) if o.shape[0] == 1 else split(*o.shape) for o in out_shape
        ],
        compiler_params=pltpu.CompilerParams(vmem_limit_bytes=48 << 20),
        name="tail",
    )(down, out, gate, up, qkv, output, grad_input, gain_sums)


def body(
    hidden_in,
    attn_gain,
    w_query,
    key_weight,
    value_weight,
    w_out,
    ffn_gain,
    w_gate,
    w_up,
    w_down,
    cotangent,
):
    ws, ctx = lax.axis_size("ws"), lax.axis_size("ctx")
    local_len, local_seqs, features = hidden_in.shape
    row_count = local_len * local_seqs
    q_heads = w_query.shape[1] // HEAD_DIM
    kv_heads = key_weight.shape[1] // HEAD_DIM
    group = q_heads // kv_heads
    own_heads = kv_heads // ws
    wide = (group + 2) * HEAD_DIM
    q_wide = group * HEAD_DIM
    pairs = ws * local_seqs * own_heads
    copies = ctx // pairs
    depth = features // ws
    cosines, sines = rope_tables(ctx * local_len, group + 1, 1)
    gains = jnp.stack([attn_gain, ffn_gain]).astype(F32)
    gains = lax.dynamic_update_slice(
        jnp.zeros((8, features), F32), gains, (0, lax.axis_index("ws") * depth)
    )
    inputs = hidden_in.reshape(row_count, features)
    grad_low = cotangent.reshape(row_count, features)
    (
        normed_attn, w_qkv, q_pair, k_pair, v_pair, pack, attn_in, gate, up, grad_low_all, gains,
    ) = front(
        inputs, gains, w_query, key_weight, value_weight, w_gate, w_up, grad_low, cosines, sines,
        ws, ctx, own_heads, group,
    )
    (
        residual, normed_ffn, hidden, grad_gate, grad_up, grad_sent, grad_keep, out_sent, out_keep,
    ) = middle(
        inputs, attn_in, w_out, gains, gate, up, w_down, grad_low_all, ws, ctx, own_heads, group,
    )
    output, grad_input, gain_sums, (g_down, g_gate, g_up, g_out, g_qkv) = back(
        inputs, gains, cosines, sines, q_pair, k_pair, v_pair, pack, attn_in, normed_attn, w_qkv,
        w_out, grad_low_all, residual, normed_ffn, hidden, grad_gate, grad_up, grad_sent,
        grad_keep, out_sent, out_keep, ws, ctx, own_heads,
    )
    results = tail(
        g_down, g_out, g_gate, g_up, g_qkv, output, grad_input, gain_sums, ws, group
    )
    output, grad_input, attn_gain_sum, *middle_sums = results
    *middle_sums, ffn_gain_sum, g_gate, g_up, g_down = middle_sums
    return (
        output.reshape(hidden_in.shape),
        grad_input.reshape(hidden_in.shape),
        attn_gain_sum.reshape(depth),
        *middle_sums,
        ffn_gain_sum.reshape(depth),
        g_gate,
        g_up,
        g_down,
    )


def solution(mesh):
    tokens, rows, one = P("ctx", "ws", None), P("ws", None), P("ws")
    return jax.shard_map(
        body,
        mesh=mesh,
        in_specs=(tokens, one, rows, rows, rows, rows, one, rows, rows, rows, tokens),
        out_specs=(tokens, tokens, one, rows, rows, rows, rows, one, rows, rows, rows),
        check_vma=False,
    )
```

```python
import functools

import jax
import jax.numpy as jnp
import numpy as np
from jax import lax
from jax.experimental import pallas as pl
from jax.experimental.pallas import tpu as pltpu
from jax.sharding import PartitionSpec as P

HEAD_DIM = 96
EPSILON = 1e-05
ROPE_BASE = 100000.0
MASK_FILL = -1e30
BF = jnp.bfloat16
F32 = jnp.float32


def rope_tables(length, rotated_heads, plain_heads):
    half = HEAD_DIM // 2
    frequency = np.float32(ROPE_BASE) ** (-(np.arange(half, dtype=np.float32) * 2.0 / HEAD_DIM))
    angles = np.arange(length, dtype=np.float32)[:, None] * frequency[None, :].astype(np.float32)
    cosine, sine = np.cos(angles), np.sin(angles)
    plain = np.zeros((length, plain_heads * HEAD_DIM), np.float32)
    cosines = [cosine, cosine] * rotated_heads + [plain + 1.0]
    sines = [-sine, sine] * rotated_heads + [plain]
    return (
        jnp.asarray(np.concatenate(cosines, axis=-1), F32),
        jnp.asarray(np.concatenate(sines, axis=-1), F32),
    )


MESH = pl.DeviceIdType.MESH


def remote(src, dst, send_sem, recv_sem, device):
    return pltpu.make_async_remote_copy(
        src_ref=src, dst_ref=dst, send_sem=send_sem, recv_sem=recv_sem,
        device_id=device, device_id_type=MESH,
    )


def dma(*shape):
    return pltpu.SemaphoreType.DMA(shape)


def at_rows(ref, start, size):
    return ref.at[pl.ds(pl.multiple_of(start, size), size), :]


def greet(devices):
    barrier = pltpu.get_barrier_semaphore()
    for device in devices:
        pl.semaphore_signal(barrier, inc=1, device_id=device, device_id_type=MESH)
    pl.semaphore_wait(barrier, len(devices))


def swap_lanes(vectors):
    lanes = lax.broadcasted_iota(jnp.int32, vectors.shape, 1)
    width, half = vectors.shape[1], HEAD_DIM // 2
    first = lax.rem(lanes, HEAD_DIM) < half
    return jnp.where(first, pltpu.roll(vectors, width - half, 1), pltpu.roll(vectors, half, 1))


class RowSpread:
    def __init__(self, own, everyone, send_sem, recv_sem, c, w, ws):
        self.own, self.everyone, self.ws = own, everyone, ws
        self.send_sem, self.recv_sem, self.c, self.w = send_sem, recv_sem, c, w
        self.half = own.shape[0] // 2
        self.square = ws == 4
        if self.square:
            self.beside = (w + 1 - 2 * lax.rem(w, 2), lax.rem(w + 2, 4))
            self.far = 3 - w

    def rows(self, ref, h):
        return ref.at[pl.ds(h * self.half, self.half), :]

    def direct(self, i):
        return remote(
            self.own, self.everyone.at[self.w], self.send_sem.at[i], self.recv_sem.at[i],
            (self.c, lax.rem(self.w + i, self.ws)),
        )

    def first(self, n, h):
        return remote(
            self.rows(self.own, h), self.rows(self.everyone.at[self.w], h),
            self.send_sem.at[2 * n + h], self.recv_sem.at[2 * n + h], (self.c, self.beside[n]),
        )

    def onward(self, n):
        block = self.rows(self.everyone.at[self.beside[n]], n)
        return remote(
            block, block, self.send_sem.at[4 + n], self.recv_sem.at[4 + n],
            (self.c, self.beside[1 - n]),
        )

    def start(self):
        if self.square:
            for h in range(2):
                for n in range(2):
                    self.first(n, n if h == 0 else 1 - n).start()
        else:
            for i in range(1, self.ws):
                self.direct(i).start()

    def block(self, i):
        if not self.square:
            return lax.rem(self.w + self.ws - i, self.ws)
        low, high = lax.rem(self.w + i, 2), lax.rem(self.w // 2 + i // 2, 2)
        return low + 2 * high

    def pass_on(self):
        if self.square:
            for n in range(2):
                self.first(n, n).wait_recv()
                self.onward(n).start()

    def wait_block(self, i):
        if not self.square:
            self.direct(i + 1).wait_recv()
        elif i < 2:
            self.first(i, 1 - i).wait_recv()
        else:
            self.onward(0).wait_recv()
            self.onward(1).wait_recv()

    def wait_sent(self):
        if self.square:
            for n in range(2):
                for h in range(2):
                    self.first(n, h).wait_send()
                self.onward(n).wait_send()
        else:
            for i in range(1, self.ws):
                self.direct(i).wait_send()


def dot_bt(left, right):
    return lax.dot_general(left, right, (((1,), (1,)), ((), ())), preferred_element_type=F32)


def feed_forward(
    ws, own_heads, group, c, w, wait_cot, wait_ffn,
    x, attn, w_out, gains, cot, gate, up, w_down,
    residual_out, normed, hidden, grad_gate, grad_up, grad_sent, grad_keep, out_sent, out_keep,
    sent, landed, grad_hidden, keep, rs_sem, ag_sem,
):
    rows, features = x.shape
    q_wide = group * HEAD_DIM
    units = gate.shape[1]
    total_rows = ws * rows
    tile = 256

    def send_sum(i):
        to = lax.rem(w + i, ws)
        return remote(sent.at[to], landed.at[w], rs_sem.at[0, i], rs_sem.at[1, i], (c, to))

    def project(i, _):
        s = lax.rem(w + i, ws)
        part = jnp.zeros((rows, features), F32)
        for j in range(own_heads):
            part = part + jnp.dot(
                attn[s * own_heads + j], w_out[j * q_wide : (j + 1) * q_wide, :],
                preferred_element_type=F32,
            )

        @pl.when(i < ws)
        def _():
            sent[s] = part.astype(BF)
            send_sum(i).start()

        @pl.when(i == ws)
        def _():
            keep[...] = part

        return 0

    lax.fori_loop(1, ws + 1, project, 0)

    wait_cot()

    def hidden_back(n, _):
        here = pl.ds(pl.multiple_of(n * tile, tile), tile)
        grad_hidden[:, here] = dot_bt(cot[...].reshape(total_rows, features), w_down[here, :])
        return 0

    lax.fori_loop(0, units // tile, hidden_back, 0)
    wait_ffn()

    residual = x[...].astype(F32) + keep[...]
    for i in range(1, ws):
        send_sum(i).wait_recv()
        residual = residual + landed[lax.rem(w + ws - i, ws)].astype(F32)
    gain = gains[1:2]
    factor = lax.rsqrt(jnp.mean(residual * residual, axis=-1, keepdims=True) + EPSILON)
    normed[w] = (residual * factor * gain).astype(BF)
    spread = RowSpread(normed.at[w], normed, ag_sem.at[0], ag_sem.at[1], c, w, ws)
    spread.start()
    residual_out[...] = residual

    def feed(i, _):
        s = spread.block(i)
        here = pl.ds(pl.multiple_of(s * rows, rows), rows)
        for n in range(1, ws):

            @pl.when(i == n)
            def _():
                if n == 1:
                    spread.pass_on()
                spread.wait_block(n - 1)

        block = normed[s]

        def columns(n, _):
            cut = pl.ds(pl.multiple_of(n * tile, tile), tile)
            gate_proj = jnp.dot(block, gate[:, cut], preferred_element_type=F32)
            up_proj = jnp.dot(block, up[:, cut], preferred_element_type=F32)
            sigmoid = 1.0 / (1.0 + jnp.exp(-gate_proj))
            activation = gate_proj * sigmoid
            grad = grad_hidden[here, cut]
            hidden[here, cut] = (activation * up_proj).astype(BF)
            grad_up[here, cut] = (grad * activation).astype(BF)
            grad_gate[here, cut] = (
                grad * up_proj * sigmoid * (1.0 + gate_proj * (1.0 - sigmoid))
            ).astype(BF)
            return 0

        lax.fori_loop(0, units // tile, columns, 0)

        def back(n, _):
            cut = pl.ds(pl.multiple_of(n * tile, tile), tile)
            part = dot_bt(grad_gate[here, :], gate[cut, :]) + dot_bt(grad_up[here, :], up[cut, :])

            @pl.when(i > 0)
            def _():
                grad_sent[s, :, cut] = part.astype(BF)

            @pl.when(i == 0)
            def _():
                grad_keep[:, cut] = part

            return 0

        lax.fori_loop(0, features // tile, back, 0)
        return 0

    lax.fori_loop(0, ws, feed, 0)

    def down_columns(n, _):
        cut = pl.ds(pl.multiple_of(n * tile, tile), tile)
        part = jnp.dot(hidden[...], w_down[:, cut], preferred_element_type=F32)
        out_sent[:, :, cut] = part.astype(BF).reshape(ws, rows, tile)
        own = hidden[pl.ds(pl.multiple_of(w * rows, rows), rows), :]
        out_keep[:, cut] = jnp.dot(own, w_down[:, cut], preferred_element_type=F32)
        return 0

    lax.fori_loop(0, features // tile, down_columns, 0)

    def wait_sent():
        for i in range(1, ws):
            send_sum(i).wait_send()
        spread.wait_sent()

    return wait_sent


def front_kernel(
    ws, ctx, own_heads, group,
    x, gains, wq, wk, wv, gate, up, cot, cosines, sines, w_out_all, w_down_all,
    normed_out, w_all_out, q_done, k_done, v_done, pack_done, attn_in, cot_all, gains_all,
    residual, normed_ffn, hidden, grad_gate, grad_up, grad_sent, grad_keep, out_sent, out_keep,
    normed, w_all, q_out, k_out, v_out, pack, gate_all, up_all, w_out, w_down,
    landed, grad_hidden, keep, rs_sem, ag_sem, load_sem, save_sem,
    x_all, g_in, w_stage, raw, qkv_stage, pair, attn_stage, cos, sin,
    x_sem, g_sem, w_sem, wf_sem, line_sem, ffn_sem, ff_sem, cot_sem, pair_sem, back_sem, own_sem,
):
    c, w = lax.axis_index("ctx"), lax.axis_index("ws")
    core = lax.rem(c, 2)
    sibling = (c + 1 - 2 * core, w)
    rows = x.shape[0]
    depth = wq.shape[0]
    half = depth // 2
    q_wide = group * HEAD_DIM
    wide = q_wide + 2 * HEAD_DIM
    pairs = ws * own_heads
    units = gate_all.shape[1]
    peer = [lax.rem(w + i, ws) for i in range(ws)]
    origin = [lax.rem(w + ws - i, ws) for i in range(ws)]

    def rope_copy(i):
        table, kept = ((cosines, cos), (sines, sin))[i]
        return pltpu.make_async_copy(at_rows(table, c * rows, rows), kept, own_sem.at[i])

    rope_copy(0).start()
    rope_copy(1).start()
    near = [(lax.rem(c + i, ctx), w) for i in range(1, ctx)]
    greet(near + [(c, peer[i]) for i in range(1, ws)])

    def send_gain(i):
        return remote(gains, g_in.at[w], g_sem.at[0, i], g_sem.at[1, i], (c, peer[i]))

    spread_x = RowSpread(x, x_all, x_sem.at[0], x_sem.at[1], c, w, ws)
    spread_cot = RowSpread(cot, cot_all, cot_sem.at[0], cot_sem.at[1], c, w, ws)
    line = ctx // 2
    place = c // 2
    shared = depth % (16 * ctx) == 0
    slice_rows = depth // ctx if shared else half
    slice_at = c * slice_rows if shared else core * half

    def send_w(i):
        return remote(
            at_rows(w_stage.at[peer[i]], slice_at, slice_rows),
            at_rows(w_all.at[w], slice_at, slice_rows),
            w_sem.at[0, i], w_sem.at[1, i], (c, peer[i]),
        )

    def line_w(i, z, towards):
        block = at_rows(w_all.at[origin[i]], (2 * z + core) * slice_rows, slice_rows)
        return remote(
            block, block, line_sem.at[0, towards, i, z], line_sem.at[1, 0, i, z],
            (c + 2 if towards else c - 2, w),
        )

    def pass_w(i, z, of):
        at = (2 * z + of) * slice_rows if shared else of * half
        block = at_rows(w_all.at[origin[i]], at, slice_rows)
        return remote(block, block, wf_sem.at[0, i, z], wf_sem.at[1, i, z], sibling)

    def on_line(act, hops):
        for h in hops:
            for side in range(2):
                z = place + h if side else place - h

                @pl.when((z >= 0) & (z < line))
                def _():
                    act(z, side)

    def start_w():
        for i in range(1, ws):
            send_w(i).wait_recv()
            pass_w(i, place if shared else 0, core).start()
            if shared:

                @pl.when(place > 0)
                def _():
                    line_w(i, place, 0).start()

                @pl.when(place < line - 1)
                def _():
                    line_w(i, place, 1).start()

    def arrive_w(z, side):
        for i in range(1, ws):
            line_w(i, z, side).wait_recv()

            @pl.when((place > 0) if side else (place < line - 1))
            def _():
                line_w(i, z, 1 - side).start()

            pass_w(i, z, core).start()

    def finish_w():
        for i in range(1, ws):
            for z in range(line if shared else 1):
                pass_w(i, z, 1 - core).wait_recv()

    def spread_w_sent():
        for i in range(1, ws):
            send_w(i).wait_send()
            for z in range(line if shared else 1):
                pass_w(i, z, core).wait_send()

            if shared:

                @pl.when(place > 0)
                def _():
                    line_w(i, place, 0).wait_send()

                @pl.when(place < line - 1)
                def _():
                    line_w(i, place, 1).wait_send()

        def left(z, side):
            for i in range(1, ws):

                @pl.when((place > 0) if side else (place < line - 1))
                def _():
                    line_w(i, z, 1 - side).wait_send()

        if shared:
            on_line(left, range(1, line))

    def send_ffn(which, i):
        held, everyone = ((gate, gate_all), (up, up_all))[which]
        columns = pl.ds(pl.multiple_of(peer[i] * units, 128), units)
        return remote(
            held.at[pl.ds(pl.multiple_of(core * half, half), half), columns],
            at_rows(everyone, w * depth + core * half, half),
            ffn_sem.at[0, which, i], ffn_sem.at[1, which, i], (c, peer[i]),
        )

    def pass_ffn(which, i):
        block = at_rows((gate_all, up_all)[which], origin[i] * depth + core * half, half)
        return remote(block, block, ff_sem.at[0, which, i], ff_sem.at[1, which, i], sibling)

    mine = pl.ds(pl.multiple_of(w * units, 128), units)
    own_rows = pl.ds(pl.multiple_of(w * depth, depth), depth)

    def load(i):
        source, to = (
            (gate.at[:, mine], gate_all.at[own_rows, :]),
            (up.at[:, mine], up_all.at[own_rows, :]),
            (w_down_all, w_down),
            (w_out_all, w_out),
            (cot, cot_all.at[w]),
        )[i]
        return pltpu.make_async_copy(source, to, load_sem.at[i])

    def save(i):
        source, to = (
            (normed, normed_out), (w_all, w_all_out), (q_out, q_done), (k_out, k_done),
            (v_out, v_done), (pack, pack_done),
        )[i]
        return pltpu.make_async_copy(source, to, save_sem.at[i])

    def send_pair(i):
        to = lax.rem(c + i, ctx)
        return remote(
            qkv_stage.at[lax.rem(to, pairs)], pair.at[c],
            pair_sem.at[0, i], pair_sem.at[1, i], (to, w),
        )

    first_back = c // pairs * pairs
    own_pair = lax.rem(c, pairs)

    def back_copy(to, i):
        return remote(
            attn_stage.at[to], attn_in.at[own_pair],
            back_sem.at[0, i], back_sem.at[1, i], (to, w),
        )

    for i in range(1, ws):
        send_gain(i).start()
    for d in range(ws):
        for j in range(own_heads):
            h = d * own_heads + j
            w_stage[d, :, j * wide : (j + 1) * wide] = jnp.concatenate(
                [
                    wq[:, h * q_wide : (h + 1) * q_wide],
                    wk[:, h * HEAD_DIM : (h + 1) * HEAD_DIM],
                    wv[:, h * HEAD_DIM : (h + 1) * HEAD_DIM],
                ],
                axis=1,
            )
    for i in range(1, ws):
        send_w(i).start()
    spread_x.start()
    w_all[w] = w_stage[w]
    for i in range(5):
        load(i).start()
    total_gain = gains[...]
    for i in range(1, ws):
        send_gain(i).wait_recv()
        total_gain = total_gain + g_in[origin[i]]
    gains_all[...] = total_gain
    gain = total_gain[0:1]

    def norm_block(index, block):
        wide_block = block.astype(F32)
        factor = lax.rsqrt(jnp.mean(wide_block * wide_block, axis=-1, keepdims=True) + EPSILON)
        normed[index] = (wide_block * factor * gain).astype(BF)

    norm_block(w, x[...])
    start_w()
    if shared:
        on_line(arrive_w, range(1, 2))
    spread_x.pass_on()
    for i in range(1, ws):
        for which in range(2):
            send_ffn(which, i).start()
    spread_cot.start()
    if shared:
        on_line(arrive_w, range(2, line))
    for i in range(1, ws):
        spread_x.wait_block(i - 1)
        norm_block(spread_x.block(i), x_all[spread_x.block(i)])
    finish_w()

    left = normed[...].reshape(ws * rows, normed.shape[2])
    step = 256 if raw.shape[1] % 256 == 0 else 128
    for n in range(0, raw.shape[1], step):
        right = w_all[:, :, n : n + step].reshape(ws * depth, step)
        raw[:, n : n + step] = jnp.dot(left, right, preferred_element_type=F32)
    rope_copy(0).wait()
    rope_copy(1).wait()
    for s in range(ws):
        for j in range(own_heads):
            block = raw[s * rows : (s + 1) * rows, j * wide : (j + 1) * wide]
            turned = block * cos[...] + swap_lanes(block) * sin[...]
            qkv_stage[s * own_heads + j] = turned.astype(BF)
    for i in range(1, ctx):
        send_pair(i).start()
    pair[c] = qkv_stage[own_pair]

    def split(index):
        block = pair[index]
        here = pl.ds(pl.multiple_of(index * rows, rows), rows)
        for g in range(group):
            q_out[g, here, :] = block[:, g * HEAD_DIM : (g + 1) * HEAD_DIM]
        k_out[here, :] = block[:, q_wide : q_wide + HEAD_DIM]
        v_out[here, :] = block[:, q_wide + HEAD_DIM :]

    split(c)
    for i in range(1, ctx):
        from_c = lax.rem(c + ctx - i, ctx)
        send_pair(i).wait_recv()
        split(from_c)

    length = ctx * rows
    span = min(256, length)
    lane = lax.broadcasted_iota(jnp.int32, (span, HEAD_DIM), 1)

    def attend(start, keys, diagonal):
        here = pl.ds(start, span)
        heads = []
        allowed = start + lax.broadcasted_iota(
            jnp.int32, (span, keys), 0
        ) >= lax.broadcasted_iota(jnp.int32, (span, keys), 1)
        for g in range(group):
            scores = lax.dot_general(
                q_out[g, here, :], k_out[0:keys, :], (((1,), (1,)), ((), ())),
                preferred_element_type=F32,
            ) * HEAD_DIM**-0.5
            scores = jnp.where(allowed, scores, MASK_FILL)
            top = jnp.max(scores, axis=1, keepdims=True)
            weights = jnp.exp(scores - top)
            total = jnp.sum(weights, axis=1, keepdims=True)
            mixed = jnp.dot(
                weights.astype(BF), v_out[0:keys, :], preferred_element_type=F32
            ) / total
            pack[g, here, 0:HEAD_DIM] = mixed
            pack[g, here, HEAD_DIM:128] = jnp.where(
                lane[:, : 128 - HEAD_DIM] == 0, top, total
            )
            heads.append(mixed)
        low = jnp.concatenate(heads, axis=1).astype(BF)
        for b in range(span // rows):
            attn_stage[start // rows + b] = low[b * rows : (b + 1) * rows]

    if length <= 1024:
        for start in range(0, length, span):
            attend(start, start + span, start)
    else:

        def attend_at(index, _):
            attend(pl.multiple_of(index * span, span), length, 0)
            return 0

        lax.fori_loop(0, length // span, attend_at, 0)
    for i in range(1, pairs):
        back_copy(first_back + lax.rem(own_pair + i, pairs), i).start()
    attn_in[own_pair] = attn_stage[c]
    spread_cot.pass_on()
    for i in range(6):
        save(i).start()
    for i in range(1, pairs):
        source = lax.rem(own_pair + pairs - i, pairs)
        arriving = remote(
            attn_stage.at[c], attn_in.at[source],
            back_sem.at[0, i], back_sem.at[1, i], (first_back + source, w),
        )
        arriving.wait_recv()
    load(3).wait()

    def wait_cot():
        for i in range(1, ws):
            for which in range(2):
                send_ffn(which, i).wait_recv()
                pass_ffn(which, i).start()
        load(4).wait()
        load(2).wait()
        for i in range(1, ws):
            spread_cot.wait_block(i - 1)

    def wait_ffn():
        load(0).wait()
        load(1).wait()
        for i in range(1, ws):
            for which in range(2):
                pass_ffn(which, i).wait_recv()

    spread_x.wait_sent()
    wait_sent = feed_forward(
        ws, own_heads, group, c, w, wait_cot, wait_ffn,
        x, attn_in, w_out, gains_all, cot_all, gate_all, up_all, w_down,
        residual, normed_ffn, hidden, grad_gate, grad_up, grad_sent, grad_keep, out_sent, out_keep,
        x_all, landed, grad_hidden, keep, rs_sem, ag_sem,
    )
    wait_sent()
    for i in range(6):
        save(i).wait()
    for i in range(1, ws):
        send_gain(i).wait_send()
        for which in range(2):
            send_ffn(which, i).wait_send()
            pass_ffn(which, i).wait_send()
    spread_w_sent()
    spread_cot.wait_sent()
    for i in range(1, ctx):
        send_pair(i).wait_send()
    for i in range(1, pairs):
        back_copy(first_back + lax.rem(own_pair + i, pairs), i).wait_send()


def front(
    x, gains, wq, wk, wv, gate, up, cot, cosines, sines, w_out, w_down, ws, ctx, own_heads, group
):
    rows, features = x.shape
    depth = wq.shape[0]
    q_wide = group * HEAD_DIM
    wide = q_wide + 2 * HEAD_DIM
    pairs = ws * own_heads
    length = ctx * rows
    units = gate.shape[1] // ws
    total = ws * rows
    vmem, anywhere = pl.BlockSpec(memory_space=pltpu.VMEM), pl.BlockSpec(memory_space=pl.ANY)
    shape = jax.ShapeDtypeStruct
    return pl.pallas_call(
        functools.partial(front_kernel, ws, ctx, own_heads, group),
        out_shape=[
            shape((ws, rows, features), BF),
            shape((ws, depth, own_heads * wide), BF),
            shape((group, length, HEAD_DIM), BF),
            shape((length, HEAD_DIM), BF),
            shape((length, HEAD_DIM), BF),
            shape((group, length, 128), F32),
            shape((pairs, rows, q_wide), BF),
            shape((ws, rows, features), BF),
            shape(gains.shape, F32),
            shape((rows, features), F32),
            shape((ws, rows, features), BF),
            shape((total, units), BF),
            shape((total, units), BF),
            shape((total, units), BF),
            shape((ws, rows, features), BF),
            shape((rows, features), F32),
            shape((ws, rows, features), BF),
            shape((rows, features), F32),
        ],
        in_specs=[vmem] * 5 + [anywhere] * 7,
        out_specs=[anywhere] * 6 + [vmem] * 12,
        scratch_shapes=[
            pltpu.VMEM((ws, rows, features), BF),
            pltpu.VMEM((ws, depth, own_heads * wide), BF),
            pltpu.VMEM((group, length, HEAD_DIM), BF),
            pltpu.VMEM((length, HEAD_DIM), BF),
            pltpu.VMEM((length, HEAD_DIM), BF),
            pltpu.VMEM((group, length, 128), F32),
            pltpu.VMEM((features, units), BF),
            pltpu.VMEM((features, units), BF),
            pltpu.VMEM(w_out.shape, BF),
            pltpu.VMEM((units, features), BF),
            pltpu.VMEM((ws, rows, features), BF),
            pltpu.VMEM((total, units), F32),
            pltpu.VMEM((rows, features), F32),
            dma(2, ws), dma(2, max(6, ws)), dma(5), dma(6),
            pltpu.VMEM((ws, rows, features), BF),
            pltpu.VMEM((ws,) + gains.shape, F32),
            pltpu.VMEM((ws, depth, own_heads * wide), BF),
            pltpu.VMEM((ws * rows, own_heads * wide), F32),
            pltpu.VMEM((pairs, rows, wide), BF),
            pltpu.VMEM((ctx, rows, wide), BF),
            pltpu.VMEM((ctx, rows, q_wide), BF),
            pltpu.VMEM((rows, wide), F32),
            pltpu.VMEM((rows, wide), F32),
            dma(2, max(6, ws)), dma(2, ws), dma(2, ws), dma(2, ws, ctx // 2),
            dma(2, 2, ws, ctx // 2), dma(2, 2, ws), dma(2, 2, ws), dma(2, max(6, ws)),
            dma(2, ctx), dma(2, pairs), dma(2),
        ],
        compiler_params=pltpu.CompilerParams(
            collective_id=1, has_side_effects=True, vmem_limit_bytes=63 << 20
        ),
        name="front",
    )(x, gains, wq, wk, wv, gate, up, cot, cosines, sines, w_out, w_down)


SKEW = 2
ROWS = (32, 48, 48, 32, 64)
TICK_NORM, TICK_ATTENDED, TICK_PAIRS, TICK_GATHER = 5, 11, 15, 6


def back_kernel(
    ws, ctx, group, own_heads, moved, rows, ticks,
    x, gains, cosines, sines, q_all, k_all, v_all, pack_all, attn_all, normed_all, w_qkv_all,
    w_out_all, cot_all, residual_all, ffn_all, hidden_all, gate_all, up_all, grad_sent, grad_keep,
    out_sent, out_keep,
    output, grad_input, gain_out, *refs,
):
    count = len(moved)
    outs, refs = refs[:count], refs[count:]
    parts, refs = refs[:count], refs[count:]
    sib_buf, refs = refs[:count], refs[count:]
    red_in, refs = refs[:count], refs[count:]
    red_send, red_recv, hand_send, hand_recv, bc_send, bc_recv, core_send, core_recv = (
        refs[i * count : (i + 1) * count] for i in range(8)
    )
    (
        q, k, v, pack, attn, normed, w_qkv, w_out, cot, residual, hidden, grad_gate, grad_up,
        own_part, turned, turned_hidden, branch, pair_stage, grad_pair, grad_residual,
        grad_q, grad_k, grad_v, key_turned, back_stage, grad_in, grad_rows,
        sent, landed, keep, own_gain, ws_gain, ctx_gain, cos, sin,
        sib_send, sib_recv, load_sem, ag_sem, to_pair_sem, pair_sem, rs_sem, gain_sem, wide_sem,
        rope_sem,
    ) = refs[8 * count :]
    c, w = lax.axis_index("ctx"), lax.axis_index("ws")
    core = lax.rem(c, 2)
    place, line = c // 2, ctx // 2
    sibling = (c + 1 - 2 * core, w)
    before, after = (c - 2, w), (c + 2, w)
    tokens, features = x.shape
    q_wide = group * HEAD_DIM
    wide = q_wide + 2 * HEAD_DIM
    pairs = ws * own_heads
    length = ctx * tokens
    depth = features // ws
    total_rows = ws * tokens
    units = hidden.shape[1]

    sources = (
        hidden_all, cot_all, ffn_all, gate_all, up_all, grad_keep, residual_all, w_out_all,
        attn_all, q_all, k_all, v_all, pack_all, w_qkv_all, normed_all, out_keep,
    )
    targets = (
        hidden, cot, normed, grad_gate, grad_up, own_part, residual, w_out,
        attn, q, k, v, pack, w_qkv, normed, own_part,
    )

    def load(i):
        return pltpu.make_async_copy(sources[i], targets[i], load_sem.at[i])

    for i in range(14):
        if length <= 1024 or i not in (9, 12):
            load(i).start()
    greet(
        [(lax.rem(c + i, ctx), w) for i in range(1, ctx)]
        + [(c, lax.rem(w + i, ws)) for i in range(1, ws)]
    )

    def send_sum(turn, i):
        to = lax.rem(w + i, ws)
        return remote(
            (grad_sent, out_sent, sent)[turn].at[to], landed.at[turn % 2, w],
            rs_sem.at[0, turn, i], rs_sem.at[1, turn, i], (c, to),
        )

    def landed_sum(turn, total):
        for i in range(1, ws):
            send_sum(turn, i).wait_recv()
            total = total + landed[turn % 2, lax.rem(w + ws - i, ws)].astype(F32)
        return total

    for i in range(1, ws):
        send_sum(0, i).start()

    def across_cores(i):
        half = parts[i].at[:, 1 - core] if moved[i] else parts[i].at[1 - core]
        return remote(half, sib_buf[i], sib_send.at[i], sib_recv.at[i], sibling)

    def spot(i, p, odd):
        if not moved[i]:
            return 2 * p + odd, None
        block = p // (ws // 2)
        return block, 2 * lax.rem(p, ws // 2) + lax.rem(block + odd, 2)

    def cut(i, block):
        return pl.ds(pl.multiple_of(block * rows[i], rows[i]), rows[i])

    def piece(i, p, odd, of):
        block, step = spot(i, p, odd)
        if not moved[i]:
            ref = parts[i].at[core] if of is parts else of[i]
            return ref.at[cut(i, block), :]
        owner = lax.rem(w + step, ws)
        ref = parts[i].at[owner, core] if of is parts else of[i].at[owner]
        return ref.at[cut(i, block), :]

    def final(i, p, odd, half, source):
        block, _ = spot(i, p, odd)
        if not moved[i]:
            return outs[i].at[half, cut(i, block), :]
        n = parts[i].shape[-1]
        columns = pl.ds(pl.multiple_of(source * n, 128), n)
        return outs[i].at[half, cut(i, block), columns]

    def source_of(i, p, odd):
        _, step = spot(i, p, odd)
        return None if step is None else lax.rem(w + ws - step, ws)

    def local(i, p, odd):
        here = piece(i, p, odd, parts)[...].astype(F32)
        return here + piece(i, p, odd, sib_buf)[...].astype(F32)

    def up_line(i, p, odd):
        e = 2 * p + odd
        return remote(
            piece(i, p, odd, parts), piece(i, p, odd, red_in),
            red_send[i].at[e], red_recv[i].at[e], after if odd else before,
        )

    def hand_over(i, p, odd):
        _, step = spot(i, p, odd)
        e = 2 * p + odd
        return remote(
            piece(i, p, odd, parts), final(i, p, odd, core, w),
            hand_send[i].at[e], hand_recv[i].at[e], (c, lax.rem(w + step, ws)),
        )

    def hand_here(i, p, odd):
        return pltpu.make_async_copy(
            piece(i, p, odd, parts), final(i, p, odd, core, w), hand_recv[i].at[2 * p + odd]
        )

    def down_line(i, p, odd):
        total = final(i, p, odd, core, source_of(i, p, odd))
        e = 2 * p + odd
        return remote(
            total, total, bc_send[i].at[e], bc_recv[i].at[e], before if odd else after
        )

    def over(i, p, odd, half):
        total = final(i, p, odd, half, source_of(i, p, odd))
        e = 2 * p + odd
        return remote(total, total, core_send[i].at[e], core_recv[i].at[e], sibling)

    def ends(odd):
        low, high = place == 0, place == line - 1
        return (low, high) if odd else (high, low)

    def either(i, p, odd, here, there):
        _, step = spot(i, p, odd)
        if step is None:
            here()
        else:
            pl.when(step == 0)(here)
            pl.when(step != 0)(there)

    def reduce_chunk(i, p, odd):
        start, end = ends(odd)

        @pl.when(start)
        def _():
            piece(i, p, odd, parts)[...] = local(i, p, odd).astype(BF)
            up_line(i, p, odd).start()

        @pl.when(jnp.logical_not(start))
        def _():
            up_line(i, p, odd).wait_recv()
            total = local(i, p, odd) + piece(i, p, odd, red_in)[...].astype(F32)
            piece(i, p, odd, parts)[...] = total.astype(BF)

            @pl.when(jnp.logical_not(end))
            def _():
                up_line(i, p, odd).start()

            @pl.when(end)
            def _():
                either(
                    i, p, odd,
                    lambda: hand_here(i, p, odd).start(), lambda: hand_over(i, p, odd).start(),
                )

    def spread_chunk(i, p, odd):
        end, start = ends(odd)

        @pl.when(start)
        def _():
            def arrived():
                total = final(i, p, odd, core, source_of(i, p, odd))
                e = 2 * p + odd
                remote(
                    total, total, hand_send[i].at[e], hand_recv[i].at[e], (c, lax.rem(w + 1, ws))
                ).wait_recv()

            either(i, p, odd, lambda: hand_here(i, p, odd).wait(), arrived)

        @pl.when(jnp.logical_not(start))
        def _():
            down_line(i, p, odd).wait_recv()

        @pl.when(jnp.logical_not(end))
        def _():
            down_line(i, p, odd).start()

        over(i, p, odd, core).start()

    counts = [red_send[i].shape[0] // 2 for i in range(count)]
    first, total_chunks = [], 0
    for i in range(count):
        first.append(total_chunks)
        total_chunks += counts[i]
    lasts = first[1:] + [total_chunks]
    hops = (line - 1 - place, place)

    def chain(t):
        for i in range(count):

            @pl.when(t == first[i])
            def _():
                across_cores(i).wait_recv()

        for odd in range(2):
            at = t - SKEW * hops[odd]
            down = t - SKEW * (2 * line - 1 - hops[odd])

            @pl.when((at >= 0) & (at < total_chunks))
            def _():
                for i in range(count):

                    @pl.when((at >= first[i]) & (at < lasts[i]))
                    def _():
                        reduce_chunk(i, at - first[i], odd)

            @pl.when((down >= 0) & (down < total_chunks))
            def _():
                for i in range(count):

                    @pl.when((down >= first[i]) & (down < lasts[i]))
                    def _():
                        spread_chunk(i, down - first[i], odd)

    def down_weights():
        load(0).wait()
        load(1).wait()

        def turn(n, _):
            here = pl.ds(pl.multiple_of(n * 256, 256), 256)
            turned_hidden[here, :] = hidden[:, here].T
            return 0

        lax.fori_loop(0, units // 256, turn, 0)
        size = units // 4
        every = cot[...].reshape(total_rows, features)
        for h in range(2):
            for n in range(2):
                at = (2 * h + n) * size
                parts[0][h, n * size : (n + 1) * size, :] = jnp.dot(
                    turned_hidden[at : at + size, :], every, preferred_element_type=F32
                ).astype(BF)
        across_cores(0).start()

    def turn_rows():
        def turn(n, _):
            here = pl.ds(pl.multiple_of(n * 256, 256), 256)
            turned[here, :] = normed[:, :, here].reshape(total_rows, 256).T
            return 0

        lax.fori_loop(0, features // 256, turn, 0)

    def row_products(i, right):
        half = depth // 2

        def one(o, _):
            for h in range(2):
                here = pl.ds(pl.multiple_of(o * depth + h * half, half), half)
                parts[i][o, h] = jnp.dot(
                    turned[here, :], right[...], preferred_element_type=F32
                ).astype(BF)
            return 0

        lax.fori_loop(0, ws, one, 0)
        across_cores(i).start()

    def gate_weights():
        load(2).wait()
        load(3).wait()
        turn_rows()
        load(14).start()
        row_products(1, grad_gate)

    def up_weights():
        load(4).wait()
        row_products(2, grad_up)

    def send_rows(i):
        return remote(
            branch.at[w], branch.at[w], ag_sem.at[0, i], ag_sem.at[1, i],
            (c, lax.rem(w + i, ws)),
        )

    def ffn_norm_back():
        load(5).wait()
        load(6).wait()
        grad_normed = landed_sum(0, own_part[...])
        load(15).start()
        here = residual[...]
        factor = lax.rsqrt(jnp.mean(here * here, axis=-1, keepdims=True) + EPSILON)
        unit = here * factor
        own_gain[...] = jnp.broadcast_to(
            jnp.sum(grad_normed * unit, axis=0, keepdims=True), own_gain.shape
        )
        grad = grad_normed * gains[1:2]
        mean = jnp.mean(grad * unit, axis=-1, keepdims=True)
        back_grad = cot[w].astype(F32) + factor * (grad - unit * mean)
        grad_residual[...] = back_grad
        branch[w] = back_grad.astype(BF)
        for i in range(1, ws):
            send_rows(i).start()

    def send_pair(i):
        to = lax.rem(c + i, ctx)
        return remote(
            pair_stage.at[lax.rem(to, pairs)], grad_pair.at[c],
            to_pair_sem.at[0, i], to_pair_sem.at[1, i], (to, w),
        )

    def attended_back():
        load(7).wait()
        for i in range(ws):
            s = lax.rem(w + ws - i, ws)
            if i:
                send_rows(i).wait_recv()
            grad_low = dot_bt(branch[s], w_out[...]).astype(BF)
            for j in range(own_heads):
                pair_stage[s * own_heads + j] = grad_low[:, j * q_wide : (j + 1) * q_wide]
        for i in range(1, ctx):
            send_pair(i).start()
        grad_pair[c] = pair_stage[lax.rem(c, pairs)]
        for i in range(1, ws):
            send_sum(1, i).start()

    def out_weights():
        load(8).wait()
        half = own_heads * q_wide // 2
        for h in range(2):
            j, low = divmod(h * half, q_wide)
            side = jnp.concatenate([attn[s * own_heads + j] for s in range(ws)], axis=0)
            parts[3][h] = jnp.dot(
                side.T[low : low + half], branch[...].reshape(total_rows, features),
                preferred_element_type=F32,
            ).astype(BF)
        across_cores(3).start()

    def finish_output():
        load(15).wait()
        output[...] = (landed_sum(1, residual[...] + own_part[...])).astype(BF)

    first_back = c // pairs * pairs
    own_pair = lax.rem(c, pairs)
    span = min(256, length) if length <= 1024 else tokens

    def back_unit(g, start, low, keys):
        here, there = pl.ds(start, span), pl.ds(low, keys)
        query = q[g, here, :]
        grad = (
            grad_pair[pl.ds(start // tokens, span // tokens), :, g * HEAD_DIM : (g + 1) * HEAD_DIM]
        ).reshape(span, HEAD_DIM)
        kept = pack[g, here, :]
        kept_turned = kept.T
        top, total = kept_turned[HEAD_DIM : HEAD_DIM + 1], kept_turned[HEAD_DIM + 1 : HEAD_DIM + 2]
        grad_wide = grad.astype(F32)
        delta = jnp.sum(grad_wide.T * kept_turned[:HEAD_DIM], axis=0, keepdims=True)
        scaled = (grad_wide / kept[:, HEAD_DIM + 1 : HEAD_DIM + 2]).astype(BF)
        scores = dot_bt(k[there, :], query) * HEAD_DIM**-0.5
        allowed = start + lax.broadcasted_iota(
            jnp.int32, (keys, span), 1
        ) >= low + lax.broadcasted_iota(jnp.int32, (keys, span), 0)
        weights = jnp.exp(jnp.where(allowed, scores, MASK_FILL) - top)
        grad_probs = dot_bt(v[there, :], grad)
        grad_scores = (weights * (1.0 / total) * (grad_probs - delta)).astype(BF)
        grad_k[there, :] += jnp.dot(grad_scores, query, preferred_element_type=F32)
        grad_v[there, :] += jnp.dot(weights.astype(BF), scaled, preferred_element_type=F32)
        turned_grad = jnp.dot(
            key_turned[:, there], grad_scores, preferred_element_type=F32
        )
        if length <= 1024:
            grad_q[g, here, :] = turned_grad.T
        else:
            grad_q[g, here, :] += turned_grad.T

    def send_back(to, i):
        return remote(
            back_stage.at[to], grad_in.at[own_pair],
            pair_sem.at[0, i], pair_sem.at[1, i], (to, w),
        )

    def rope_copy(i, start):
        table, kept = ((cosines, cos), (sines, sin))[i]
        return pltpu.make_async_copy(table.at[pl.ds(start, span), :], kept, rope_sem.at[i])

    def finish_rows(start):
        here = pl.ds(start, span)
        rope_copy(0, start).wait()
        rope_copy(1, start).wait()
        scale = HEAD_DIM**-0.5
        block = jnp.concatenate(
            [grad_q[g, here, :] * scale for g in range(group)]
            + [grad_k[here, :] * scale, grad_v[here, :]],
            axis=1,
        )
        block = (block * cos[...] - swap_lanes(block) * sin[...]).astype(BF)
        for b in range(span // tokens):
            to = start // tokens + b
            back_stage[to] = block[b * tokens : (b + 1) * tokens]

    def send_rows_back(to):
        step = lax.rem(to - c + ctx, pairs)

        @pl.when((to // pairs == c // pairs) & (to != c))
        def _():
            send_back(to, step).start()

        @pl.when(to == c)
        def _():
            grad_in[own_pair] = back_stage[to]

    def prepare():
        for i in range(9, 13):
            load(i).wait()
        for i in range(1, ctx):
            send_pair(i).wait_recv()
        grad_k[...] = jnp.zeros(grad_k.shape, F32)
        grad_v[...] = jnp.zeros(grad_v.shape, F32)
        key_turned[...] = k[...].T

    def turn_normed():
        load(14).wait()
        turn_rows()

    def gather_back():
        for i in range(1, pairs):
            source = lax.rem(own_pair + pairs - i, pairs)
            arriving = remote(
                back_stage.at[c], grad_in.at[source],
                pair_sem.at[0, i], pair_sem.at[1, i], (first_back + source, w),
            )
            arriving.wait_recv()
        for s in range(ws):
            for j in range(own_heads):
                grad_rows[s * tokens : (s + 1) * tokens, j * wide : (j + 1) * wide] = grad_in[
                    s * own_heads + j
                ]

    def sum_rows():
        load(13).wait()

        def one(i, _):
            s = lax.rem(w + i, ws)
            block = grad_rows[pl.ds(pl.multiple_of(s * tokens, tokens), tokens), :]
            for n in range(0, ws):
                part = dot_bt(block, w_qkv[n])

                @pl.when(i < ws)
                def _():
                    sent[s, :, n * depth : (n + 1) * depth] = part.astype(BF)

                @pl.when(i == ws)
                def _():
                    keep[:, n * depth : (n + 1) * depth] = part

            @pl.when(i < ws)
            def _():
                send_sum(2, i).start()

            return 0

        lax.fori_loop(1, ws + 1, one, 0)

    def weight_sums():
        row_products(4, grad_rows)

    def send_gain(i):
        return remote(
            own_gain, ws_gain.at[w], gain_sem.at[0, i], gain_sem.at[1, i],
            (c, lax.rem(w + i, ws)),
        )

    def send_wide(i):
        return remote(
            ws_gain.at[w], ctx_gain.at[c], wide_sem.at[0, i], wide_sem.at[1, i],
            (lax.rem(c + i, ctx), w),
        )

    def finish_input():
        total = landed_sum(2, keep[...])
        inputs = x[...].astype(F32)
        factor = lax.rsqrt(jnp.mean(inputs * inputs, axis=-1, keepdims=True) + EPSILON)
        unit = inputs * factor
        row = lax.broadcasted_iota(jnp.int32, own_gain.shape, 0)
        attn_gain = jnp.sum(total * unit, axis=0, keepdims=True)
        own_gain[...] = jnp.where(row == 0, attn_gain, own_gain[...])
        for i in range(1, ws):
            send_gain(i).start()
        grad = total * gains[0:1]
        mean = jnp.mean(grad * unit, axis=-1, keepdims=True)
        grad_input[...] = grad_residual[...] + factor * (grad - unit * mean)

    def widen_gain():
        total = own_gain[...]
        for i in range(1, ws):
            send_gain(i).wait_recv()
            total = total + ws_gain[lax.rem(w + ws - i, ws)]
        ws_gain[w] = total
        for i in range(1, ctx):
            send_wide(i).start()

    def finish_gain():
        total = ws_gain[w]
        for i in range(1, ctx):
            send_wide(i).wait_recv()
            total = total + ctx_gain[lax.rem(c + ctx - i, ctx)]
        gain_out[...] = total

    events = [[] for _ in range(ticks)]

    def put(at, *todo):
        events[min(at, ticks - 1)].extend(todo)

    put(0, gate_weights)
    put(1, up_weights)
    put(TICK_NORM, ffn_norm_back)
    put(TICK_ATTENDED, attended_back, out_weights)
    put(TICK_PAIRS, prepare)
    starts = list(range(0, length, span))[::-1]
    if length <= 1024:
        for n, start in enumerate(starts):

            def one_start(start=start):
                rope_copy(0, start).start()
                rope_copy(1, start).start()
                for g in range(group):
                    back_unit(g, start, 0, start + span)
                finish_rows(start)
                for b in range(span // tokens):
                    send_rows_back(start // tokens + b)

            put(TICK_PAIRS + n, one_start)
        at = TICK_PAIRS + len(starts)
    else:

        def all_starts():
            grad_q[...] = jnp.zeros(grad_q.shape, F32)

            def one_start(n, _):
                start = pl.multiple_of(n * span, span)

                def one_block(m, _):
                    low = pl.multiple_of(m * 512, 512)

                    @pl.when(low < start + span)
                    def _():
                        for g in range(group):
                            back_unit(g, start, low, 512)

                    return 0

                lax.fori_loop(0, length // 512, one_block, 0)
                return 0

            lax.fori_loop(0, length // span, one_start, 0)

            def finish(n, _):
                start = pl.multiple_of(n * span, span)
                rope_copy(0, start).start()
                rope_copy(1, start).start()
                finish_rows(start)
                return 0

            lax.fori_loop(0, length // span, finish, 0)
            for to in range(ctx):
                send_rows_back(to)

        put(TICK_PAIRS, all_starts)
        at = TICK_PAIRS + 1
    put(at, turn_normed)
    put(at + 1, finish_output)
    put(at + TICK_GATHER, gather_back, weight_sums, sum_rows)
    put(at + TICK_GATHER + 5, finish_input)
    put(at + TICK_GATHER + 7, widen_gain)
    put(at + TICK_GATHER + 10, finish_gain)

    down_weights()

    def tick(t, _):
        chain(t)
        for n, todo in enumerate(events):
            if todo:

                @pl.when(t == n)
                def _():
                    for event in todo:
                        event()

        return 0

    lax.fori_loop(0, ticks, tick, 0)

    for i in range(count):

        def finish_pair(p, _):
            for odd in range(2):
                _, reduce_end = ends(odd)
                spread_end, _ = ends(odd)

                @pl.when(jnp.logical_not(reduce_end))
                def _():
                    up_line(i, p, odd).wait_send()

                if moved[i]:
                    _, step = spot(i, p, odd)

                    @pl.when(reduce_end & (step != 0))
                    def _():
                        hand_over(i, p, odd).wait_send()

                @pl.when(jnp.logical_not(spread_end))
                def _():
                    down_line(i, p, odd).wait_send()

                over(i, p, odd, core).wait_send()
                over(i, p, odd, 1 - core).wait_recv()
            return 0

        lax.fori_loop(0, counts[i], finish_pair, 0)
    for i in range(count):
        across_cores(i).wait_send()
    for i in range(1, ws):
        for turn in range(3):
            send_sum(turn, i).wait_send()
        send_rows(i).wait_send()
        send_gain(i).wait_send()
    for i in range(1, ctx):
        send_wide(i).wait_send()
        send_pair(i).wait_send()
    for i in range(1, pairs):
        send_back(first_back + lax.rem(own_pair + i, pairs), i).wait_send()


def back(
    x, gains, cosines, sines, q, k, v, pack, attn, normed, w_qkv, w_out, cot, residual, ffn,
    hidden, grad_gate, grad_up, grad_sent, grad_keep, out_sent, out_keep, ws, ctx, own_heads,
):
    tokens, features = x.shape
    group, length, _ = q.shape
    units = hidden.shape[1]
    q_wide = group * HEAD_DIM
    wide = q_wide + 2 * HEAD_DIM
    pairs = ws * own_heads
    span = min(256, length) if length <= 1024 else tokens
    kept = length if length <= 1024 else span
    depth = features // ws
    total_rows = ws * tokens
    moved = (False, True, True, False, True)
    held = pltpu.VMEM
    widths = [features, units, units, features, own_heads * wide]
    halves = [units // 2, depth // 2, depth // 2, own_heads * q_wide // 2, depth // 2]
    rows, parts, sib, red, outs, counts = [], [], [], [], [], []
    for is_moved, n, half, want in zip(moved, widths, halves, ROWS):
        while half % want or not is_moved and half % (2 * want):
            want -= 16
        rows.append(want)
        lead = (ws,) if is_moved else ()
        parts.append(held(lead + (2, half, n), BF))
        sib.append(held(lead + (half, n), BF))
        red.append(held(lead + (half, n), BF))
        outs.append((2, half, ws * n if is_moved else n))
        counts.append(half // want * (ws if is_moved else 1))
    ticks = sum(counts) // 2 + SKEW * (ctx - 1)
    k_count = len(parts)
    vmem, anywhere = pl.BlockSpec(memory_space=pltpu.VMEM), pl.BlockSpec(memory_space=pl.ANY)
    shape = jax.ShapeDtypeStruct
    results = pl.pallas_call(
        functools.partial(
            back_kernel, ws, ctx, group, own_heads, moved, tuple(rows), ticks
        ),
        out_shape=[
            shape((tokens, features), BF), shape((tokens, features), F32), shape(gains.shape, F32)
        ]
        + [shape(o, BF) for o in outs],
        in_specs=[vmem] * 2 + [anywhere] * 20,
        out_specs=[vmem] * 3 + [anywhere] * k_count,
        scratch_shapes=parts
        + sib
        + red
        + [dma(n) for _ in range(8) for n in counts]
        + [
            held((group, kept, HEAD_DIM), BF),
            held(k.shape, BF),
            held(v.shape, BF),
            held((group, kept, 128), F32),
            held(attn.shape, BF),
            held(normed.shape, BF),
            held(w_qkv.shape, BF),
            held(w_out.shape, BF),
            held(cot.shape, BF),
            held((tokens, features), F32),
            held((total_rows, units), BF),
            held((total_rows, units), BF),
            held((total_rows, units), BF),
            held((tokens, features), F32),
            held((features, total_rows), BF),
            held((units, total_rows), BF),
            held((ws, tokens, features), BF),
            held((pairs, tokens, q_wide), BF),
            held((ctx, tokens, q_wide), BF),
            held((tokens, features), F32),
            held((group, kept, HEAD_DIM), F32),
            held((length, HEAD_DIM), F32),
            held((length, HEAD_DIM), F32),
            held((HEAD_DIM, length), BF),
            held((ctx, tokens, wide), BF),
            held((pairs, tokens, wide), BF),
            held((total_rows, own_heads * wide), BF),
            held((ws, tokens, features), BF),
            held((2, ws, tokens, features), BF),
            held((tokens, features), F32),
            held(gains.shape, F32),
            held((ws,) + gains.shape, F32),
            held((ctx,) + gains.shape, F32),
            held((span, wide), F32),
            held((span, wide), F32),
            dma(k_count), dma(k_count), dma(16), dma(2, ws), dma(2, ctx), dma(2, pairs),
            dma(2, 3, ws), dma(2, ws), dma(2, ctx), dma(2),
        ],
        compiler_params=pltpu.CompilerParams(
            collective_id=3, has_side_effects=True, vmem_limit_bytes=63 << 20
        ),
        name="back",
    )(
        x, gains, cosines, sines, q, k, v, pack, attn, normed, w_qkv, w_out, cot, residual, ffn,
        hidden, grad_gate, grad_up, grad_sent, grad_keep, out_sent, out_keep,
    )
    sums = [s.reshape(s.shape[0] * s.shape[1], s.shape[2]) for s in results[3:]]
    return results[0], results[1], results[2], sums


def tail_kernel(ws, group, *refs):
    low, refs = refs[:8], refs[8:]
    down, out, gate, up, qkv, output, grad_input, gain_sums = low
    (
        output_out, grad_input_out, attn_gain, g_query, g_key, g_value, g_out, ffn_gain, g_gate,
        g_up, g_down,
    ) = refs
    q_wide = group * HEAD_DIM
    wide = q_wide + 2 * HEAD_DIM
    output_out[...] = output[...]
    grad_input_out[...] = grad_input[...]
    g_down[...] = down[...].astype(F32)
    g_out[...] = out[...].astype(F32)
    g_gate[...] = gate[...].astype(F32)
    g_up[...] = up[...].astype(F32)
    heads = qkv.shape[1] // wide
    blocks = [qkv[:, h * wide : (h + 1) * wide].astype(F32) for h in range(heads)]
    g_query[...] = jnp.concatenate([b[:, :q_wide] for b in blocks], axis=1)
    g_key[...] = jnp.concatenate([b[:, q_wide : q_wide + HEAD_DIM] for b in blocks], axis=1)
    g_value[...] = jnp.concatenate([b[:, q_wide + HEAD_DIM :] for b in blocks], axis=1)
    w = lax.axis_index("ws")
    depth = attn_gain.shape[1]
    for i in range(ws):

        @pl.when(w == i)
        def _():
            here = gain_sums[:, i * depth : (i + 1) * depth]
            attn_gain[...] = here[0:1]
            ffn_gain[...] = here[1:2]


def tail(down, out, gate, up, qkv, output, grad_input, gain_sums, ws, group):
    depth = qkv.shape[0]
    steps = depth // 48
    features = out.shape[1]
    q_total = qkv.shape[1] * group // (group + 2)
    k_total = q_total // group
    shape = jax.ShapeDtypeStruct

    def split(rows, columns):
        return pl.BlockSpec((rows // steps, columns), lambda n: (n, 0))

    def whole(rows, columns):
        return pl.BlockSpec((rows, columns), lambda n: (0, 0))

    out_shape = [
        shape(output.shape, BF), shape(grad_input.shape, F32), shape((1, depth), F32),
        shape((depth, q_total), F32), shape((depth, k_total), F32), shape((depth, k_total), F32),
        shape(out.shape, F32), shape((1, depth), F32), shape(gate.shape, F32),
        shape(up.shape, F32), shape(down.shape, F32),
    ]
    return pl.pallas_call(
        functools.partial(tail_kernel, ws, group),
        grid=(steps,),
        out_shape=out_shape,
        in_specs=[split(*a.shape) for a in (down, out, gate, up, qkv, output, grad_input)]
        + [whole(*gain_sums.shape)],
        out_specs=[
            whole(*o.shape) if o.shape[0] == 1 else split(*o.shape) for o in out_shape
        ],
        compiler_params=pltpu.CompilerParams(vmem_limit_bytes=63 << 20),
        name="tail",
    )(down, out, gate, up, qkv, output, grad_input, gain_sums)


def body(
    hidden_in,
    attn_gain,
    w_query,
    key_weight,
    value_weight,
    w_out,
    ffn_gain,
    w_gate,
    w_up,
    w_down,
    cotangent,
):
    ws, ctx = lax.axis_size("ws"), lax.axis_size("ctx")
    local_len, local_seqs, features = hidden_in.shape
    row_count = local_len * local_seqs
    q_heads = w_query.shape[1] // HEAD_DIM
    kv_heads = key_weight.shape[1] // HEAD_DIM
    group = q_heads // kv_heads
    own_heads = kv_heads // ws
    wide = (group + 2) * HEAD_DIM
    q_wide = group * HEAD_DIM
    pairs = ws * local_seqs * own_heads
    copies = ctx // pairs
    depth = features // ws
    cosines, sines = rope_tables(ctx * local_len, group + 1, 1)
    gains = jnp.stack([attn_gain, ffn_gain]).astype(F32)
    gains = lax.dynamic_update_slice(
        jnp.zeros((8, features), F32), gains, (0, lax.axis_index("ws") * depth)
    )
    inputs = hidden_in.reshape(row_count, features)
    grad_low = cotangent.reshape(row_count, features)
    (
        normed_attn, w_qkv, q_pair, k_pair, v_pair, pack, attn_in, grad_low_all, gains,
        residual, normed_ffn, hidden, grad_gate, grad_up, grad_sent, grad_keep, out_sent, out_keep,
    ) = front(
        inputs, gains, w_query, key_weight, value_weight, w_gate, w_up, grad_low, cosines, sines,
        w_out, w_down, ws, ctx, own_heads, group,
    )
    output, grad_input, gain_sums, (g_down, g_gate, g_up, g_out, g_qkv) = back(
        inputs, gains, cosines, sines, q_pair, k_pair, v_pair, pack, attn_in, normed_attn, w_qkv,
        w_out, grad_low_all, residual, normed_ffn, hidden, grad_gate, grad_up, grad_sent,
        grad_keep, out_sent, out_keep, ws, ctx, own_heads,
    )
    results = tail(
        g_down, g_out, g_gate, g_up, g_qkv, output, grad_input, gain_sums, ws, group
    )
    output, grad_input, attn_gain_sum, *middle_sums = results
    *middle_sums, ffn_gain_sum, g_gate, g_up, g_down = middle_sums
    return (
        output.reshape(hidden_in.shape),
        grad_input.reshape(hidden_in.shape),
        attn_gain_sum.reshape(depth),
        *middle_sums,
        ffn_gain_sum.reshape(depth),
        g_gate,
        g_up,
        g_down,
    )


def solution(mesh):
    tokens, rows, one = P("ctx", "ws", None), P("ws", None), P("ws")
    return jax.shard_map(
        body,
        mesh=mesh,
        in_specs=(tokens, one, rows, rows, rows, rows, one, rows, rows, rows, tokens),
        out_specs=(tokens, tokens, one, rows, rows, rows, rows, one, rows, rows, rows),
        check_vma=False,
    )
```

```python
import functools

import jax
import jax.numpy as jnp
import numpy as np
from jax import lax
from jax.experimental import pallas as pl
from jax.experimental.pallas import tpu as pltpu
from jax.sharding import PartitionSpec as P

HEAD_DIM = 96
EPSILON = 1e-05
ROPE_BASE = 100000.0
MASK_FILL = -1e30
BF = jnp.bfloat16
F32 = jnp.float32


def rope_tables(length, rotated_heads, plain_heads):
    half = HEAD_DIM // 2
    frequency = np.float32(ROPE_BASE) ** (-(np.arange(half, dtype=np.float32) * 2.0 / HEAD_DIM))
    angles = np.arange(length, dtype=np.float32)[:, None] * frequency[None, :].astype(np.float32)
    cosine, sine = np.cos(angles), np.sin(angles)
    plain = np.zeros((length, plain_heads * HEAD_DIM), np.float32)
    cosines = [cosine, cosine] * rotated_heads + [plain + 1.0]
    sines = [-sine, sine] * rotated_heads + [plain]
    return (
        jnp.asarray(np.concatenate(cosines, axis=-1), F32),
        jnp.asarray(np.concatenate(sines, axis=-1), F32),
    )


MESH = pl.DeviceIdType.MESH


def remote(src, dst, send_sem, recv_sem, device):
    return pltpu.make_async_remote_copy(
        src_ref=src, dst_ref=dst, send_sem=send_sem, recv_sem=recv_sem,
        device_id=device, device_id_type=MESH,
    )


def dma(*shape):
    return pltpu.SemaphoreType.DMA(shape)


def at_rows(ref, start, size):
    return ref.at[pl.ds(pl.multiple_of(start, size), size), :]


def greet(devices):
    barrier = pltpu.get_barrier_semaphore()
    for device in devices:
        pl.semaphore_signal(barrier, inc=1, device_id=device, device_id_type=MESH)
    pl.semaphore_wait(barrier, len(devices))


def swap_lanes(vectors):
    lanes = lax.broadcasted_iota(jnp.int32, vectors.shape, 1)
    width, half = vectors.shape[1], HEAD_DIM // 2
    first = lax.rem(lanes, HEAD_DIM) < half
    return jnp.where(first, pltpu.roll(vectors, width - half, 1), pltpu.roll(vectors, half, 1))


class RowSpread:
    def __init__(self, own, everyone, send_sem, recv_sem, c, w, ws):
        self.own, self.everyone, self.ws = own, everyone, ws
        self.send_sem, self.recv_sem, self.c, self.w = send_sem, recv_sem, c, w
        self.half = own.shape[0] // 2
        self.square = ws == 4
        if self.square:
            self.beside = (w + 1 - 2 * lax.rem(w, 2), lax.rem(w + 2, 4))
            self.far = 3 - w

    def rows(self, ref, h):
        return ref.at[pl.ds(h * self.half, self.half), :]

    def direct(self, i):
        return remote(
            self.own, self.everyone.at[self.w], self.send_sem.at[i], self.recv_sem.at[i],
            (self.c, lax.rem(self.w + i, self.ws)),
        )

    def first(self, n, h):
        return remote(
            self.rows(self.own, h), self.rows(self.everyone.at[self.w], h),
            self.send_sem.at[2 * n + h], self.recv_sem.at[2 * n + h], (self.c, self.beside[n]),
        )

    def onward(self, n):
        block = self.rows(self.everyone.at[self.beside[n]], n)
        return remote(
            block, block, self.send_sem.at[4 + n], self.recv_sem.at[4 + n],
            (self.c, self.beside[1 - n]),
        )

    def start(self):
        if self.square:
            for h in range(2):
                for n in range(2):
                    self.first(n, n if h == 0 else 1 - n).start()
        else:
            for i in range(1, self.ws):
                self.direct(i).start()

    def block(self, i):
        if not self.square:
            return lax.rem(self.w + self.ws - i, self.ws)
        low, high = lax.rem(self.w + i, 2), lax.rem(self.w // 2 + i // 2, 2)
        return low + 2 * high

    def pass_on(self):
        if self.square:
            for n in range(2):
                self.first(n, n).wait_recv()
                self.onward(n).start()

    def wait_block(self, i):
        if not self.square:
            self.direct(i + 1).wait_recv()
        elif i < 2:
            self.first(i, 1 - i).wait_recv()
        else:
            self.onward(0).wait_recv()
            self.onward(1).wait_recv()

    def wait_sent(self):
        if self.square:
            for n in range(2):
                for h in range(2):
                    self.first(n, h).wait_send()
                self.onward(n).wait_send()
        else:
            for i in range(1, self.ws):
                self.direct(i).wait_send()


class RowSum:
    def __init__(self, sent, landed, relay, send_sem, recv_sem, c, w, ws):
        self.sent, self.landed, self.relay, self.ws = sent, landed, relay, ws
        self.send_sem, self.recv_sem, self.c, self.w = send_sem, recv_sem, c, w
        self.half = sent.shape[1] // 2
        self.square = ws == 4
        if self.square:
            self.beside = (w + 1 - 2 * lax.rem(w, 2), lax.rem(w + 2, 4))
            self.far = 3 - w

    def rows(self, ref, h):
        return ref.at[pl.ds(h * self.half, self.half), :]

    def owner(self, n):
        if not self.square:
            return lax.rem(self.w + n + 1, self.ws)
        i = jnp.where(n == 0, 3, jnp.where(n == 3, 0, n))
        low, high = lax.rem(self.w + i, 2), lax.rem(self.w // 2 + i // 2, 2)
        return low + 2 * high

    def direct(self, i):
        to = lax.rem(self.w + i, self.ws)
        return remote(
            self.sent.at[to], self.landed.at[self.w], self.send_sem.at[i], self.recv_sem.at[i],
            (self.c, to),
        )

    def corner(self, n):
        return remote(
            self.rows(self.sent.at[self.far], n), self.relay.at[n],
            self.send_sem.at[n], self.recv_sem.at[n], (self.c, self.beside[n]),
        )

    def near(self, n, h):
        return remote(
            self.rows(self.sent.at[self.beside[n]], h), self.rows(self.landed.at[n], h),
            self.send_sem.at[2 + 2 * n + h], self.recv_sem.at[2 + 2 * n + h],
            (self.c, self.beside[n]),
        )

    def start(self, n):
        if not self.square:
            for i in range(1, self.ws):

                @pl.when(n == i - 1)
                def _():
                    self.direct(i).start()

            return

        @pl.when(n == 0)
        def _():
            self.corner(0).start()
            self.corner(1).start()

        for i in range(2):

            @pl.when(n == i + 1)
            def _():
                self.near(i, i).start()

    def total(self, own):
        if not self.square:
            for i in range(1, self.ws):
                self.direct(i).wait_recv()
                own = own + self.landed[lax.rem(self.w + self.ws - i, self.ws)].astype(F32)
            return own
        for n in range(2):
            self.corner(n).wait_recv()
            mine = self.rows(self.sent.at[self.beside[1 - n]], n)
            mine[...] = (mine[...].astype(F32) + self.relay[n].astype(F32)).astype(BF)
            self.near(1 - n, n).start()
        for n in range(2):
            self.near(n, 0).wait_recv()
            self.near(n, 1).wait_recv()
            own = own + self.landed[n].astype(F32)
        return own

    def wait_sent(self):
        if not self.square:
            for i in range(1, self.ws):
                self.direct(i).wait_send()
            return
        for n in range(2):
            self.corner(n).wait_send()
            self.near(n, 0).wait_send()
            self.near(n, 1).wait_send()


def dot_bt(left, right):
    return lax.dot_general(left, right, (((1,), (1,)), ((), ())), preferred_element_type=F32)


def feed_forward(
    ws, own_heads, group, c, w, wait_cot, wait_ffn,
    x, attn, w_out, gains, cot, gate, up, w_down,
    residual_out, normed, hidden, grad_gate, grad_up, grad_sent, grad_keep, out_sent, out_keep,
    sent, landed, relay, grad_hidden, keep, rs_sem, ag_sem,
):
    rows, features = x.shape
    q_wide = group * HEAD_DIM
    units = gate.shape[1]
    total_rows = ws * rows
    tile = 256

    row_sum = RowSum(sent, landed, relay, rs_sem.at[0], rs_sem.at[1], c, w, ws)

    def project(n, _):
        s = row_sum.owner(n)
        part = jnp.zeros((rows, features), F32)
        for j in range(own_heads):
            part = part + jnp.dot(
                attn[s * own_heads + j], w_out[j * q_wide : (j + 1) * q_wide, :],
                preferred_element_type=F32,
            )

        @pl.when(n < ws - 1)
        def _():
            sent[s] = part.astype(BF)
            row_sum.start(n)

        @pl.when(n == ws - 1)
        def _():
            keep[...] = part

        return 0

    lax.fori_loop(0, ws, project, 0)

    wait_cot()

    def hidden_back(n, _):
        here = pl.ds(pl.multiple_of(n * tile, tile), tile)
        grad_hidden[:, here] = dot_bt(cot[...].reshape(total_rows, features), w_down[here, :])
        return 0

    lax.fori_loop(0, units // tile, hidden_back, 0)
    wait_ffn()

    residual = row_sum.total(x[...].astype(F32) + keep[...])
    gain = gains[1:2]
    factor = lax.rsqrt(jnp.mean(residual * residual, axis=-1, keepdims=True) + EPSILON)
    normed[w] = (residual * factor * gain).astype(BF)
    spread = RowSpread(normed.at[w], normed, ag_sem.at[0], ag_sem.at[1], c, w, ws)
    spread.start()
    residual_out[...] = residual

    def feed(i, _):
        s = spread.block(i)
        here = pl.ds(pl.multiple_of(s * rows, rows), rows)
        for n in range(1, ws):

            @pl.when(i == n)
            def _():
                if n == 1:
                    spread.pass_on()
                spread.wait_block(n - 1)

        block = normed[s]

        def columns(n, _):
            cut = pl.ds(pl.multiple_of(n * tile, tile), tile)
            gate_proj = jnp.dot(block, gate[:, cut], preferred_element_type=F32)
            up_proj = jnp.dot(block, up[:, cut], preferred_element_type=F32)
            sigmoid = 1.0 / (1.0 + jnp.exp(-gate_proj))
            activation = gate_proj * sigmoid
            grad = grad_hidden[here, cut]
            hidden[here, cut] = (activation * up_proj).astype(BF)
            grad_up[here, cut] = (grad * activation).astype(BF)
            grad_gate[here, cut] = (
                grad * up_proj * sigmoid * (1.0 + gate_proj * (1.0 - sigmoid))
            ).astype(BF)
            return 0

        lax.fori_loop(0, units // tile, columns, 0)

        def back(n, _):
            cut = pl.ds(pl.multiple_of(n * tile, tile), tile)
            part = dot_bt(grad_gate[here, :], gate[cut, :]) + dot_bt(grad_up[here, :], up[cut, :])

            @pl.when(i > 0)
            def _():
                grad_sent[s, :, cut] = part.astype(BF)

            @pl.when(i == 0)
            def _():
                grad_keep[:, cut] = part

            return 0

        lax.fori_loop(0, features // tile, back, 0)
        return 0

    lax.fori_loop(0, ws, feed, 0)

    def down_columns(n, _):
        cut = pl.ds(pl.multiple_of(n * tile, tile), tile)
        part = jnp.dot(hidden[...], w_down[:, cut], preferred_element_type=F32)
        out_sent[:, :, cut] = part.astype(BF).reshape(ws, rows, tile)
        own = hidden[pl.ds(pl.multiple_of(w * rows, rows), rows), :]
        out_keep[:, cut] = jnp.dot(own, w_down[:, cut], preferred_element_type=F32)
        return 0

    lax.fori_loop(0, features // tile, down_columns, 0)

    def wait_sent():
        row_sum.wait_sent()
        spread.wait_sent()

    return wait_sent


def front_kernel(
    ws, ctx, own_heads, group,
    x, gains, wq, wk, wv, gate, up, cot, cosines, sines, w_out_all, w_down_all,
    normed_out, w_all_out, q_done, k_done, v_done, pack_done, attn_in, cot_all, gains_all,
    residual, normed_ffn, hidden, grad_gate, grad_up, grad_sent, grad_keep, out_sent, out_keep,
    normed, w_all, q_out, k_out, v_out, pack, gate_all, up_all, w_out, w_down,
    landed, relay, grad_hidden, keep, rs_sem, ag_sem, load_sem, save_sem,
    x_all, g_in, w_stage, raw, qkv_stage, pair, attn_stage, cos, sin,
    x_sem, g_sem, w_sem, wf_sem, line_sem, ffn_sem, ff_sem, cot_sem, pair_sem, back_sem, own_sem,
):
    c, w = lax.axis_index("ctx"), lax.axis_index("ws")
    core = lax.rem(c, 2)
    sibling = (c + 1 - 2 * core, w)
    rows = x.shape[0]
    depth = wq.shape[0]
    half = depth // 2
    q_wide = group * HEAD_DIM
    wide = q_wide + 2 * HEAD_DIM
    pairs = ws * own_heads
    units = gate_all.shape[1]
    peer = [lax.rem(w + i, ws) for i in range(ws)]
    origin = [lax.rem(w + ws - i, ws) for i in range(ws)]

    def rope_copy(i):
        table, kept = ((cosines, cos), (sines, sin))[i]
        return pltpu.make_async_copy(at_rows(table, c * rows, rows), kept, own_sem.at[i])

    rope_copy(0).start()
    rope_copy(1).start()
    near = [(lax.rem(c + i, ctx), w) for i in range(1, ctx)]
    greet(near + [(c, peer[i]) for i in range(1, ws)])

    def send_gain(i):
        return remote(gains, g_in.at[w], g_sem.at[0, i], g_sem.at[1, i], (c, peer[i]))

    spread_x = RowSpread(x, x_all, x_sem.at[0], x_sem.at[1], c, w, ws)
    spread_cot = RowSpread(cot, cot_all, cot_sem.at[0], cot_sem.at[1], c, w, ws)
    line = ctx // 2
    place = c // 2
    shared = depth % (16 * ctx) == 0
    slice_rows = depth // ctx if shared else half
    slice_at = c * slice_rows if shared else core * half

    def send_w(i):
        return remote(
            at_rows(w_stage.at[peer[i]], slice_at, slice_rows),
            at_rows(w_all.at[w], slice_at, slice_rows),
            w_sem.at[0, i], w_sem.at[1, i], (c, peer[i]),
        )

    def line_w(i, z, towards):
        block = at_rows(w_all.at[origin[i]], (2 * z + core) * slice_rows, slice_rows)
        return remote(
            block, block, line_sem.at[0, towards, i, z], line_sem.at[1, 0, i, z],
            (c + 2 if towards else c - 2, w),
        )

    def pass_w(i, z, of):
        at = (2 * z + of) * slice_rows if shared else of * half
        block = at_rows(w_all.at[origin[i]], at, slice_rows)
        return remote(block, block, wf_sem.at[0, i, z], wf_sem.at[1, i, z], sibling)

    def on_line(act, hops):
        for h in hops:
            for side in range(2):
                z = place + h if side else place - h

                @pl.when((z >= 0) & (z < line))
                def _():
                    act(z, side)

    def start_w():
        for i in range(1, ws):
            send_w(i).wait_recv()
            pass_w(i, place if shared else 0, core).start()
            if shared:

                @pl.when(place > 0)
                def _():
                    line_w(i, place, 0).start()

                @pl.when(place < line - 1)
                def _():
                    line_w(i, place, 1).start()

    def arrive_w(z, side):
        for i in range(1, ws):
            line_w(i, z, side).wait_recv()

            @pl.when((place > 0) if side else (place < line - 1))
            def _():
                line_w(i, z, 1 - side).start()

            pass_w(i, z, core).start()

    def finish_w():
        for i in range(1, ws):
            for z in range(line if shared else 1):
                pass_w(i, z, 1 - core).wait_recv()

    def spread_w_sent():
        for i in range(1, ws):
            send_w(i).wait_send()
            for z in range(line if shared else 1):
                pass_w(i, z, core).wait_send()

            if shared:

                @pl.when(place > 0)
                def _():
                    line_w(i, place, 0).wait_send()

                @pl.when(place < line - 1)
                def _():
                    line_w(i, place, 1).wait_send()

        def left(z, side):
            for i in range(1, ws):

                @pl.when((place > 0) if side else (place < line - 1))
                def _():
                    line_w(i, z, 1 - side).wait_send()

        if shared:
            on_line(left, range(1, line))

    def send_ffn(which, i):
        held, everyone = ((gate, gate_all), (up, up_all))[which]
        columns = pl.ds(pl.multiple_of(peer[i] * units, 128), units)
        return remote(
            held.at[pl.ds(pl.multiple_of(core * half, half), half), columns],
            at_rows(everyone, w * depth + core * half, half),
            ffn_sem.at[0, which, i], ffn_sem.at[1, which, i], (c, peer[i]),
        )

    def pass_ffn(which, i):
        block = at_rows((gate_all, up_all)[which], origin[i] * depth + core * half, half)
        return remote(block, block, ff_sem.at[0, which, i], ff_sem.at[1, which, i], sibling)

    mine = pl.ds(pl.multiple_of(w * units, 128), units)
    own_rows = pl.ds(pl.multiple_of(w * depth, depth), depth)

    def load(i):
        source, to = (
            (gate.at[:, mine], gate_all.at[own_rows, :]),
            (up.at[:, mine], up_all.at[own_rows, :]),
            (w_down_all, w_down),
            (w_out_all, w_out),
            (cot, cot_all.at[w]),
        )[i]
        return pltpu.make_async_copy(source, to, load_sem.at[i])

    def save(i):
        source, to = (
            (normed, normed_out), (w_all, w_all_out), (q_out, q_done), (k_out, k_done),
            (v_out, v_done), (pack, pack_done),
        )[i]
        return pltpu.make_async_copy(source, to, save_sem.at[i])

    def send_pair(i):
        to = lax.rem(c + i, ctx)
        return remote(
            qkv_stage.at[lax.rem(to, pairs)], pair.at[c],
            pair_sem.at[0, i], pair_sem.at[1, i], (to, w),
        )

    first_back = c // pairs * pairs
    own_pair = lax.rem(c, pairs)

    def back_copy(to, i):
        return remote(
            attn_stage.at[to], attn_in.at[own_pair],
            back_sem.at[0, i], back_sem.at[1, i], (to, w),
        )

    for i in range(1, ws):
        send_gain(i).start()
    for d in range(ws):
        for j in range(own_heads):
            h = d * own_heads + j
            w_stage[d, :, j * wide : (j + 1) * wide] = jnp.concatenate(
                [
                    wq[:, h * q_wide : (h + 1) * q_wide],
                    wk[:, h * HEAD_DIM : (h + 1) * HEAD_DIM],
                    wv[:, h * HEAD_DIM : (h + 1) * HEAD_DIM],
                ],
                axis=1,
            )
    for i in range(1, ws):
        send_w(i).start()
    spread_x.start()
    w_all[w] = w_stage[w]
    for i in range(5):
        load(i).start()
    total_gain = gains[...]
    for i in range(1, ws):
        send_gain(i).wait_recv()
        total_gain = total_gain + g_in[origin[i]]
    gains_all[...] = total_gain
    gain = total_gain[0:1]

    def norm_block(index, block):
        wide_block = block.astype(F32)
        factor = lax.rsqrt(jnp.mean(wide_block * wide_block, axis=-1, keepdims=True) + EPSILON)
        normed[index] = (wide_block * factor * gain).astype(BF)

    norm_block(w, x[...])
    start_w()
    if shared:
        on_line(arrive_w, range(1, 2))
    spread_x.pass_on()
    for i in range(1, ws):
        for which in range(2):
            send_ffn(which, i).start()
    spread_cot.start()
    if shared:
        on_line(arrive_w, range(2, line))
    for i in range(1, ws):
        spread_x.wait_block(i - 1)
        norm_block(spread_x.block(i), x_all[spread_x.block(i)])
    finish_w()

    left = normed[...].reshape(ws * rows, normed.shape[2])
    step = 256 if raw.shape[1] % 256 == 0 else 128
    for n in range(0, raw.shape[1], step):
        right = w_all[:, :, n : n + step].reshape(ws * depth, step)
        raw[:, n : n + step] = jnp.dot(left, right, preferred_element_type=F32)
    rope_copy(0).wait()
    rope_copy(1).wait()
    for s in range(ws):
        for j in range(own_heads):
            block = raw[s * rows : (s + 1) * rows, j * wide : (j + 1) * wide]
            turned = block * cos[...] + swap_lanes(block) * sin[...]
            qkv_stage[s * own_heads + j] = turned.astype(BF)
    for i in range(1, ctx):
        send_pair(i).start()
    pair[c] = qkv_stage[own_pair]

    def split(index):
        block = pair[index]
        here = pl.ds(pl.multiple_of(index * rows, rows), rows)
        for g in range(group):
            q_out[g, here, :] = block[:, g * HEAD_DIM : (g + 1) * HEAD_DIM]
        k_out[here, :] = block[:, q_wide : q_wide + HEAD_DIM]
        v_out[here, :] = block[:, q_wide + HEAD_DIM :]

    split(c)
    for i in range(1, ctx):
        from_c = lax.rem(c + ctx - i, ctx)
        send_pair(i).wait_recv()
        split(from_c)

    length = ctx * rows
    span = min(256, length)
    lane = lax.broadcasted_iota(jnp.int32, (span, HEAD_DIM), 1)

    def attend(start, keys, diagonal):
        here = pl.ds(start, span)
        heads = []
        allowed = start + lax.broadcasted_iota(
            jnp.int32, (span, keys), 0
        ) >= lax.broadcasted_iota(jnp.int32, (span, keys), 1)
        for g in range(group):
            scores = lax.dot_general(
                q_out[g, here, :], k_out[0:keys, :], (((1,), (1,)), ((), ())),
                preferred_element_type=F32,
            ) * HEAD_DIM**-0.5
            scores = jnp.where(allowed, scores, MASK_FILL)
            top = jnp.max(scores, axis=1, keepdims=True)
            weights = jnp.exp(scores - top)
            total = jnp.sum(weights, axis=1, keepdims=True)
            mixed = jnp.dot(
                weights.astype(BF), v_out[0:keys, :], preferred_element_type=F32
            ) / total
            pack[g, here, 0:HEAD_DIM] = mixed
            pack[g, here, HEAD_DIM:128] = jnp.where(
                lane[:, : 128 - HEAD_DIM] == 0, top, total
            )
            heads.append(mixed)
        low = jnp.concatenate(heads, axis=1).astype(BF)
        for b in range(span // rows):
            attn_stage[start // rows + b] = low[b * rows : (b + 1) * rows]

    if length <= 1024:
        for start in range(0, length, span):
            attend(start, start + span, start)
    else:

        def attend_at(index, _):
            attend(pl.multiple_of(index * span, span), length, 0)
            return 0

        lax.fori_loop(0, length // span, attend_at, 0)
    for i in range(1, pairs):
        back_copy(first_back + lax.rem(own_pair + i, pairs), i).start()
    attn_in[own_pair] = attn_stage[c]
    spread_cot.pass_on()
    for i in range(6):
        save(i).start()
    for i in range(1, pairs):
        source = lax.rem(own_pair + pairs - i, pairs)
        arriving = remote(
            attn_stage.at[c], attn_in.at[source],
            back_sem.at[0, i], back_sem.at[1, i], (first_back + source, w),
        )
        arriving.wait_recv()
    load(3).wait()

    def wait_cot():
        for i in range(1, ws):
            for which in range(2):
                send_ffn(which, i).wait_recv()
                pass_ffn(which, i).start()
        load(4).wait()
        load(2).wait()
        for i in range(1, ws):
            spread_cot.wait_block(i - 1)

    def wait_ffn():
        load(0).wait()
        load(1).wait()
        for i in range(1, ws):
            for which in range(2):
                pass_ffn(which, i).wait_recv()

    spread_x.wait_sent()
    wait_sent = feed_forward(
        ws, own_heads, group, c, w, wait_cot, wait_ffn,
        x, attn_in, w_out, gains_all, cot_all, gate_all, up_all, w_down,
        residual, normed_ffn, hidden, grad_gate, grad_up, grad_sent, grad_keep, out_sent, out_keep,
        x_all, landed, relay, grad_hidden, keep, rs_sem, ag_sem,
    )
    wait_sent()
    for i in range(6):
        save(i).wait()
    for i in range(1, ws):
        send_gain(i).wait_send()
        for which in range(2):
            send_ffn(which, i).wait_send()
            pass_ffn(which, i).wait_send()
    spread_w_sent()
    spread_cot.wait_sent()
    for i in range(1, ctx):
        send_pair(i).wait_send()
    for i in range(1, pairs):
        back_copy(first_back + lax.rem(own_pair + i, pairs), i).wait_send()


def front(
    x, gains, wq, wk, wv, gate, up, cot, cosines, sines, w_out, w_down, ws, ctx, own_heads, group
):
    rows, features = x.shape
    depth = wq.shape[0]
    q_wide = group * HEAD_DIM
    wide = q_wide + 2 * HEAD_DIM
    pairs = ws * own_heads
    length = ctx * rows
    units = gate.shape[1] // ws
    total = ws * rows
    vmem, anywhere = pl.BlockSpec(memory_space=pltpu.VMEM), pl.BlockSpec(memory_space=pl.ANY)
    shape = jax.ShapeDtypeStruct
    return pl.pallas_call(
        functools.partial(front_kernel, ws, ctx, own_heads, group),
        out_shape=[
            shape((ws, rows, features), BF),
            shape((ws, depth, own_heads * wide), BF),
            shape((group, length, HEAD_DIM), BF),
            shape((length, HEAD_DIM), BF),
            shape((length, HEAD_DIM), BF),
            shape((group, length, 128), F32),
            shape((pairs, rows, q_wide), BF),
            shape((ws, rows, features), BF),
            shape(gains.shape, F32),
            shape((rows, features), F32),
            shape((ws, rows, features), BF),
            shape((total, units), BF),
            shape((total, units), BF),
            shape((total, units), BF),
            shape((ws, rows, features), BF),
            shape((rows, features), F32),
            shape((ws, rows, features), BF),
            shape((rows, features), F32),
        ],
        in_specs=[vmem] * 5 + [anywhere] * 7,
        out_specs=[anywhere] * 6 + [vmem] * 12,
        scratch_shapes=[
            pltpu.VMEM((ws, rows, features), BF),
            pltpu.VMEM((ws, depth, own_heads * wide), BF),
            pltpu.VMEM((group, length, HEAD_DIM), BF),
            pltpu.VMEM((length, HEAD_DIM), BF),
            pltpu.VMEM((length, HEAD_DIM), BF),
            pltpu.VMEM((group, length, 128), F32),
            pltpu.VMEM((features, units), BF),
            pltpu.VMEM((features, units), BF),
            pltpu.VMEM(w_out.shape, BF),
            pltpu.VMEM((units, features), BF),
            pltpu.VMEM((ws, rows, features), BF),
            pltpu.VMEM((2, rows // 2, features), BF),
            pltpu.VMEM((total, units), F32),
            pltpu.VMEM((rows, features), F32),
            dma(2, max(6, ws)), dma(2, max(6, ws)), dma(5), dma(6),
            pltpu.VMEM((ws, rows, features), BF),
            pltpu.VMEM((ws,) + gains.shape, F32),
            pltpu.VMEM((ws, depth, own_heads * wide), BF),
            pltpu.VMEM((ws * rows, own_heads * wide), F32),
            pltpu.VMEM((pairs, rows, wide), BF),
            pltpu.VMEM((ctx, rows, wide), BF),
            pltpu.VMEM((ctx, rows, q_wide), BF),
            pltpu.VMEM((rows, wide), F32),
            pltpu.VMEM((rows, wide), F32),
            dma(2, max(6, ws)), dma(2, ws), dma(2, ws), dma(2, ws, ctx // 2),
            dma(2, 2, ws, ctx // 2), dma(2, 2, ws), dma(2, 2, ws), dma(2, max(6, ws)),
            dma(2, ctx), dma(2, pairs), dma(2),
        ],
        compiler_params=pltpu.CompilerParams(
            collective_id=1, has_side_effects=True, vmem_limit_bytes=63 << 20
        ),
        name="front",
    )(x, gains, wq, wk, wv, gate, up, cot, cosines, sines, w_out, w_down)


SKEW = 2
ROWS = (32, 48, 48, 32, 64)
TICK_NORM, TICK_ATTENDED, TICK_PAIRS, TICK_GATHER = 6, 12, 16, 6
UNITS_PER_TICK = 2


def back_kernel(
    ws, ctx, group, own_heads, moved, rows, ticks,
    x, gains, cosines, sines, q_all, k_all, v_all, pack_all, attn_all, normed_all, w_qkv_all,
    w_out_all, cot_all, residual_all, ffn_all, hidden_all, gate_all, up_all, grad_sent, grad_keep,
    out_sent, out_keep,
    output, grad_input, gain_out, *refs,
):
    count = len(moved)
    outs, refs = refs[:count], refs[count:]
    parts, refs = refs[:count], refs[count:]
    sib_buf, refs = refs[:count], refs[count:]
    red_in, refs = refs[:count], refs[count:]
    red_send, red_recv, hand_send, hand_recv, bc_send, bc_recv, core_send, core_recv = (
        refs[i * count : (i + 1) * count] for i in range(8)
    )
    (
        q, k, v, pack, attn, normed, w_qkv, w_out, cot, residual, hidden, grad_gate, grad_up,
        own_part, turned, turned_hidden, branch, pair_stage, grad_pair, grad_residual,
        grad_q, grad_k, grad_v, key_turned, back_stage, grad_in, grad_rows,
        landed, keep, own_gain, ws_gain, ctx_gain, cos, sin,
        sib_send, sib_recv, load_sem, ag_sem, to_pair_sem, pair_sem, rs_sem, gain_sem, wide_sem,
        rope_sem,
    ) = refs[8 * count :]
    c, w = lax.axis_index("ctx"), lax.axis_index("ws")
    core = lax.rem(c, 2)
    place, line = c // 2, ctx // 2
    sibling = (c + 1 - 2 * core, w)
    before, after = (c - 2, w), (c + 2, w)
    tokens, features = x.shape
    q_wide = group * HEAD_DIM
    wide = q_wide + 2 * HEAD_DIM
    pairs = ws * own_heads
    length = ctx * tokens
    depth = features // ws
    total_rows = ws * tokens
    units = hidden.shape[1]

    sources = (
        hidden_all, cot_all, ffn_all, gate_all, up_all, grad_keep, residual_all, w_out_all,
        attn_all, q_all, k_all, v_all, pack_all, w_qkv_all, normed_all, out_keep,
    )
    targets = (
        hidden, cot, normed, grad_gate, grad_up, own_part, residual, w_out,
        attn, q, k, v, pack, w_qkv, normed, own_part,
    )

    def load(i):
        return pltpu.make_async_copy(sources[i], targets[i], load_sem.at[i])

    for i in range(14):
        if length <= 1024 or i not in (9, 12):
            load(i).start()
    greet(
        [(lax.rem(c + i, ctx), w) for i in range(1, ctx)]
        + [(c, lax.rem(w + i, ws)) for i in range(1, ws)]
    )

    def send_sum(turn, i):
        to = lax.rem(w + i, ws)
        return remote(
            (grad_sent, out_sent, cot)[turn].at[to], landed.at[turn % 2, w],
            rs_sem.at[0, turn, i], rs_sem.at[1, turn, i], (c, to),
        )

    def landed_sum(turn, total):
        for i in range(1, ws):
            send_sum(turn, i).wait_recv()
            total = total + landed[turn % 2, lax.rem(w + ws - i, ws)].astype(F32)
        return total

    for i in range(1, ws):
        send_sum(0, i).start()

    def across_cores(i):
        half = parts[i].at[:, 1 - core] if moved[i] else parts[i].at[1 - core]
        return remote(half, sib_buf[i], sib_send.at[i], sib_recv.at[i], sibling)

    def spot(i, p, odd):
        if not moved[i]:
            return 2 * p + odd, None
        block = p // (ws // 2)
        return block, 2 * lax.rem(p, ws // 2) + lax.rem(block + odd, 2)

    def cut(i, block):
        return pl.ds(pl.multiple_of(block * rows[i], rows[i]), rows[i])

    def piece(i, p, odd, of):
        block, step = spot(i, p, odd)
        if not moved[i]:
            ref = parts[i].at[core] if of is parts else of[i]
            return ref.at[cut(i, block), :]
        owner = lax.rem(w + step, ws)
        ref = parts[i].at[owner, core] if of is parts else of[i].at[owner]
        return ref.at[cut(i, block), :]

    def final(i, p, odd, half, source):
        block, _ = spot(i, p, odd)
        if not moved[i]:
            return outs[i].at[half, cut(i, block), :]
        n = parts[i].shape[-1]
        columns = pl.ds(pl.multiple_of(source * n, 128), n)
        return outs[i].at[half, cut(i, block), columns]

    def source_of(i, p, odd):
        _, step = spot(i, p, odd)
        return None if step is None else lax.rem(w + ws - step, ws)

    def local(i, p, odd):
        here = piece(i, p, odd, parts)[...].astype(F32)
        return here + piece(i, p, odd, sib_buf)[...].astype(F32)

    def up_line(i, p, odd):
        e = 2 * p + odd
        return remote(
            piece(i, p, odd, parts), piece(i, p, odd, red_in),
            red_send[i].at[e], red_recv[i].at[e], after if odd else before,
        )

    def hand_over(i, p, odd):
        _, step = spot(i, p, odd)
        e = 2 * p + odd
        return remote(
            piece(i, p, odd, parts), final(i, p, odd, core, w),
            hand_send[i].at[e], hand_recv[i].at[e], (c, lax.rem(w + step, ws)),
        )

    def hand_here(i, p, odd):
        return pltpu.make_async_copy(
            piece(i, p, odd, parts), final(i, p, odd, core, w), hand_recv[i].at[2 * p + odd]
        )

    def down_line(i, p, odd):
        total = final(i, p, odd, core, source_of(i, p, odd))
        e = 2 * p + odd
        return remote(
            total, total, bc_send[i].at[e], bc_recv[i].at[e], before if odd else after
        )

    def over(i, p, odd, half):
        total = final(i, p, odd, half, source_of(i, p, odd))
        e = 2 * p + odd
        return remote(total, total, core_send[i].at[e], core_recv[i].at[e], sibling)

    def ends(odd):
        low, high = place == 0, place == line - 1
        return (low, high) if odd else (high, low)

    def either(i, p, odd, here, there):
        _, step = spot(i, p, odd)
        if step is None:
            here()
        else:
            pl.when(step == 0)(here)
            pl.when(step != 0)(there)

    def reduce_chunk(i, p, odd):
        start, end = ends(odd)

        @pl.when(start)
        def _():
            piece(i, p, odd, parts)[...] = local(i, p, odd).astype(BF)
            up_line(i, p, odd).start()

        @pl.when(jnp.logical_not(start))
        def _():
            up_line(i, p, odd).wait_recv()
            total = local(i, p, odd) + piece(i, p, odd, red_in)[...].astype(F32)
            piece(i, p, odd, parts)[...] = total.astype(BF)

            @pl.when(jnp.logical_not(end))
            def _():
                up_line(i, p, odd).start()

            @pl.when(end)
            def _():
                either(
                    i, p, odd,
                    lambda: hand_here(i, p, odd).start(), lambda: hand_over(i, p, odd).start(),
                )

    def spread_chunk(i, p, odd):
        end, start = ends(odd)

        @pl.when(start)
        def _():
            def arrived():
                total = final(i, p, odd, core, source_of(i, p, odd))
                e = 2 * p + odd
                remote(
                    total, total, hand_send[i].at[e], hand_recv[i].at[e], (c, lax.rem(w + 1, ws))
                ).wait_recv()

            either(i, p, odd, lambda: hand_here(i, p, odd).wait(), arrived)

        @pl.when(jnp.logical_not(start))
        def _():
            down_line(i, p, odd).wait_recv()

        @pl.when(jnp.logical_not(end))
        def _():
            down_line(i, p, odd).start()

        over(i, p, odd, core).start()

    counts = [red_send[i].shape[0] // 2 for i in range(count)]
    first, total_chunks = [], 0
    for i in range(count):
        first.append(total_chunks)
        total_chunks += counts[i]
    lasts = first[1:] + [total_chunks]
    hops = (line - 1 - place, place)

    def chain(t):
        for i in range(count):

            @pl.when(t == first[i])
            def _():
                across_cores(i).wait_recv()

        for odd in range(2):
            at = t - SKEW * hops[odd]
            down = t - SKEW * (2 * line - 1 - hops[odd])

            @pl.when((at >= 0) & (at < total_chunks))
            def _():
                for i in range(count):

                    @pl.when((at >= first[i]) & (at < lasts[i]))
                    def _():
                        reduce_chunk(i, at - first[i], odd)

            @pl.when((down >= 0) & (down < total_chunks))
            def _():
                for i in range(count):

                    @pl.when((down >= first[i]) & (down < lasts[i]))
                    def _():
                        spread_chunk(i, down - first[i], odd)

    def down_weights():
        load(0).wait()
        load(1).wait()

        def turn(n, _):
            here = pl.ds(pl.multiple_of(n * 256, 256), 256)
            turned_hidden[here, :] = hidden[:, here].T
            return 0

        lax.fori_loop(0, units // 256, turn, 0)
        size = units // 4
        every = cot[...].reshape(total_rows, features)
        for side in range(2):
            h = core if side else 1 - core
            for n in range(2):
                at = pl.multiple_of((2 * h + n) * size, size)
                parts[0][h, n * size : (n + 1) * size, :] = jnp.dot(
                    turned_hidden[pl.ds(at, size), :], every, preferred_element_type=F32
                ).astype(BF)
            if side == 0:
                across_cores(0).start()

    def turn_rows():
        def turn(n, _):
            here = pl.ds(pl.multiple_of(n * 256, 256), 256)
            turned[here, :] = normed[:, :, here].reshape(total_rows, 256).T
            return 0

        lax.fori_loop(0, features // 256, turn, 0)

    def row_products(i, right):
        half = depth // 2

        def one(n, _):
            o = lax.rem(n, ws)
            h = jnp.where(n < ws, 1 - core, core)
            here = pl.ds(pl.multiple_of(o * depth + h * half, half), half)
            parts[i][o, h] = jnp.dot(
                turned[here, :], right[...], preferred_element_type=F32
            ).astype(BF)

            @pl.when(n == ws - 1)
            def _():
                across_cores(i).start()

            return 0

        lax.fori_loop(0, 2 * ws, one, 0)

    def gate_weights():
        load(2).wait()
        load(3).wait()
        turn_rows()
        load(14).start()
        row_products(1, grad_gate)

    def up_weights():
        load(4).wait()
        row_products(2, grad_up)

    def send_rows(i):
        return remote(
            branch.at[w], branch.at[w], ag_sem.at[0, i], ag_sem.at[1, i],
            (c, lax.rem(w + i, ws)),
        )

    def ffn_norm_back():
        load(5).wait()
        load(6).wait()
        grad_normed = landed_sum(0, own_part[...])
        load(15).start()
        here = residual[...]
        factor = lax.rsqrt(jnp.mean(here * here, axis=-1, keepdims=True) + EPSILON)
        unit = here * factor
        own_gain[...] = jnp.broadcast_to(
            jnp.sum(grad_normed * unit, axis=0, keepdims=True), own_gain.shape
        )
        grad = grad_normed * gains[1:2]
        mean = jnp.mean(grad * unit, axis=-1, keepdims=True)
        back_grad = cot[w].astype(F32) + factor * (grad - unit * mean)
        grad_residual[...] = back_grad
        branch[w] = back_grad.astype(BF)
        for i in range(1, ws):
            send_rows(i).start()

    def send_pair(i):
        to = lax.rem(c + i, ctx)
        return remote(
            pair_stage.at[lax.rem(to, pairs)], grad_pair.at[c],
            to_pair_sem.at[0, i], to_pair_sem.at[1, i], (to, w),
        )

    def attended_back():
        load(7).wait()
        for i in range(ws):
            s = lax.rem(w + ws - i, ws)
            if i:
                send_rows(i).wait_recv()
            grad_low = dot_bt(branch[s], w_out[...]).astype(BF)
            for j in range(own_heads):
                pair_stage[s * own_heads + j] = grad_low[:, j * q_wide : (j + 1) * q_wide]
        for i in range(1, ctx):
            send_pair(i).start()
        grad_pair[c] = pair_stage[lax.rem(c, pairs)]
        for i in range(1, ws):
            send_sum(1, i).start()

    def out_weights():
        load(8).wait()
        half = own_heads * q_wide // 2
        for h in range(2):
            j, low = divmod(h * half, q_wide)
            side = jnp.concatenate([attn[s * own_heads + j] for s in range(ws)], axis=0)
            parts[3][h] = jnp.dot(
                side.T[low : low + half], branch[...].reshape(total_rows, features),
                preferred_element_type=F32,
            ).astype(BF)
        across_cores(3).start()

    def finish_output():
        load(15).wait()
        output[...] = (landed_sum(1, residual[...] + own_part[...])).astype(BF)

    first_back = c // pairs * pairs
    own_pair = lax.rem(c, pairs)
    span = min(256, length) if length <= 1024 else tokens

    def back_unit(g, start, low, keys):
        here, there = pl.ds(start, span), pl.ds(low, keys)
        query = q[g, here, :]
        grad = (
            grad_pair[pl.ds(start // tokens, span // tokens), :, g * HEAD_DIM : (g + 1) * HEAD_DIM]
        ).reshape(span, HEAD_DIM)
        kept = pack[g, here, :]
        kept_turned = kept.T
        top, total = kept_turned[HEAD_DIM : HEAD_DIM + 1], kept_turned[HEAD_DIM + 1 : HEAD_DIM + 2]
        grad_wide = grad.astype(F32)
        delta = jnp.sum(grad_wide.T * kept_turned[:HEAD_DIM], axis=0, keepdims=True)
        scaled = (grad_wide / kept[:, HEAD_DIM + 1 : HEAD_DIM + 2]).astype(BF)
        scores = dot_bt(k[there, :], query) * HEAD_DIM**-0.5
        allowed = start + lax.broadcasted_iota(
            jnp.int32, (keys, span), 1
        ) >= low + lax.broadcasted_iota(jnp.int32, (keys, span), 0)
        weights = jnp.exp(jnp.where(allowed, scores, MASK_FILL) - top)
        grad_probs = dot_bt(v[there, :], grad)
        grad_scores = (weights * (1.0 / total) * (grad_probs - delta)).astype(BF)
        grad_k[there, :] += jnp.dot(grad_scores, query, preferred_element_type=F32)
        grad_v[there, :] += jnp.dot(weights.astype(BF), scaled, preferred_element_type=F32)
        turned_grad = jnp.dot(
            key_turned[:, there], grad_scores, preferred_element_type=F32
        )
        if length <= 1024:
            grad_q[g, here, :] = turned_grad.T
        else:
            grad_q[g, here, :] += turned_grad.T

    def send_back(to, i):
        return remote(
            back_stage.at[to], grad_in.at[own_pair],
            pair_sem.at[0, i], pair_sem.at[1, i], (to, w),
        )

    def rope_copy(i, start):
        table, kept = ((cosines, cos), (sines, sin))[i]
        return pltpu.make_async_copy(table.at[pl.ds(start, span), :], kept, rope_sem.at[i])

    def finish_rows(start):
        here = pl.ds(start, span)
        rope_copy(0, start).wait()
        rope_copy(1, start).wait()
        scale = HEAD_DIM**-0.5
        block = jnp.concatenate(
            [grad_q[g, here, :] * scale for g in range(group)]
            + [grad_k[here, :] * scale, grad_v[here, :]],
            axis=1,
        )
        block = (block * cos[...] - swap_lanes(block) * sin[...]).astype(BF)
        for b in range(span // tokens):
            to = start // tokens + b
            back_stage[to] = block[b * tokens : (b + 1) * tokens]

    def send_rows_back(to):
        step = lax.rem(to - c + ctx, pairs)

        @pl.when((to // pairs == c // pairs) & (to != c))
        def _():
            send_back(to, step).start()

        @pl.when(to == c)
        def _():
            grad_in[own_pair] = back_stage[to]

    def prepare():
        for i in range(9, 13):
            load(i).wait()
        for i in range(1, ctx):
            send_pair(i).wait_recv()
        grad_k[...] = jnp.zeros(grad_k.shape, F32)
        grad_v[...] = jnp.zeros(grad_v.shape, F32)
        key_turned[...] = k[...].T

    def turn_normed():
        load(14).wait()
        turn_rows()

    def gather_back():
        for i in range(1, pairs):
            source = lax.rem(own_pair + pairs - i, pairs)
            arriving = remote(
                back_stage.at[c], grad_in.at[source],
                pair_sem.at[0, i], pair_sem.at[1, i], (first_back + source, w),
            )
            arriving.wait_recv()
        for s in range(ws):
            for j in range(own_heads):
                grad_rows[s * tokens : (s + 1) * tokens, j * wide : (j + 1) * wide] = grad_in[
                    s * own_heads + j
                ]

    def sum_rows():
        load(13).wait()

        def one(i, _):
            s = lax.rem(w + i, ws)
            block = grad_rows[pl.ds(pl.multiple_of(s * tokens, tokens), tokens), :]
            for n in range(0, ws):
                part = dot_bt(block, w_qkv[n])

                @pl.when(i < ws)
                def _():
                    cot[s, :, n * depth : (n + 1) * depth] = part.astype(BF)

                @pl.when(i == ws)
                def _():
                    keep[:, n * depth : (n + 1) * depth] = part

            @pl.when(i < ws)
            def _():
                send_sum(2, i).start()

            return 0

        lax.fori_loop(1, ws + 1, one, 0)

    def weight_sums():
        row_products(4, grad_rows)

    def send_gain(i):
        return remote(
            own_gain, ws_gain.at[w], gain_sem.at[0, i], gain_sem.at[1, i],
            (c, lax.rem(w + i, ws)),
        )

    def send_wide(i):
        return remote(
            ws_gain.at[w], ctx_gain.at[c], wide_sem.at[0, i], wide_sem.at[1, i],
            (lax.rem(c + i, ctx), w),
        )

    def finish_input():
        total = landed_sum(2, keep[...])
        inputs = x[...].astype(F32)
        factor = lax.rsqrt(jnp.mean(inputs * inputs, axis=-1, keepdims=True) + EPSILON)
        unit = inputs * factor
        row = lax.broadcasted_iota(jnp.int32, own_gain.shape, 0)
        attn_gain = jnp.sum(total * unit, axis=0, keepdims=True)
        own_gain[...] = jnp.where(row == 0, attn_gain, own_gain[...])
        for i in range(1, ws):
            send_gain(i).start()
        grad = total * gains[0:1]
        mean = jnp.mean(grad * unit, axis=-1, keepdims=True)
        grad_input[...] = grad_residual[...] + factor * (grad - unit * mean)

    def widen_gain():
        total = own_gain[...]
        for i in range(1, ws):
            send_gain(i).wait_recv()
            total = total + ws_gain[lax.rem(w + ws - i, ws)]
        ws_gain[w] = total
        for i in range(1, ctx):
            send_wide(i).start()

    def finish_gain():
        total = ws_gain[w]
        for i in range(1, ctx):
            send_wide(i).wait_recv()
            total = total + ctx_gain[lax.rem(c + ctx - i, ctx)]
        gain_out[...] = total

    events = [[] for _ in range(ticks)]

    def put(at, *todo):
        events[min(at, ticks - 1)].extend(todo)

    put(0, gate_weights)
    put(1, up_weights)
    put(TICK_NORM, ffn_norm_back)
    put(TICK_ATTENDED, attended_back, out_weights)
    put(TICK_PAIRS, prepare)
    starts = list(range(0, length, span))[::-1]
    if length <= 1024:
        for n, start in enumerate(starts):

            def one_head(g, start=start):
                if g == 0:
                    rope_copy(0, start).start()
                    rope_copy(1, start).start()
                back_unit(g, start, 0, start + span)
                if g == group - 1:
                    finish_rows(start)
                    for b in range(span // tokens):
                        send_rows_back(start // tokens + b)

            for g in range(group):
                put(
                    TICK_PAIRS + (n * group + g) // UNITS_PER_TICK,
                    functools.partial(one_head, g, start),
                )
        at = TICK_PAIRS + -(-len(starts) * group // UNITS_PER_TICK)
    else:

        def all_starts():
            grad_q[...] = jnp.zeros(grad_q.shape, F32)

            def one_start(n, _):
                start = pl.multiple_of(n * span, span)

                def one_block(m, _):
                    low = pl.multiple_of(m * 512, 512)

                    @pl.when(low < start + span)
                    def _():
                        for g in range(group):
                            back_unit(g, start, low, 512)

                    return 0

                lax.fori_loop(0, length // 512, one_block, 0)
                return 0

            lax.fori_loop(0, length // span, one_start, 0)

            def finish(n, _):
                start = pl.multiple_of(n * span, span)
                rope_copy(0, start).start()
                rope_copy(1, start).start()
                finish_rows(start)
                return 0

            lax.fori_loop(0, length // span, finish, 0)
            for to in range(ctx):
                send_rows_back(to)

        put(TICK_PAIRS, all_starts)
        at = TICK_PAIRS + 1
    put(at, turn_normed)
    put(at + 1, finish_output)
    put(at + TICK_GATHER, gather_back, weight_sums, sum_rows)
    put(at + TICK_GATHER + 5, finish_input)
    put(at + TICK_GATHER + 7, widen_gain)
    put(at + TICK_GATHER + 10, finish_gain)

    down_weights()

    def tick(t, _):
        chain(t)
        for n, todo in enumerate(events):
            if todo:

                @pl.when(t == n)
                def _():
                    for event in todo:
                        event()

        return 0

    lax.fori_loop(0, ticks, tick, 0)

    for i in range(count):

        def finish_pair(p, _):
            for odd in range(2):
                _, reduce_end = ends(odd)
                spread_end, _ = ends(odd)

                @pl.when(jnp.logical_not(reduce_end))
                def _():
                    up_line(i, p, odd).wait_send()

                if moved[i]:
                    _, step = spot(i, p, odd)

                    @pl.when(reduce_end & (step != 0))
                    def _():
                        hand_over(i, p, odd).wait_send()

                @pl.when(jnp.logical_not(spread_end))
                def _():
                    down_line(i, p, odd).wait_send()

                over(i, p, odd, core).wait_send()
                over(i, p, odd, 1 - core).wait_recv()
            return 0

        lax.fori_loop(0, counts[i], finish_pair, 0)
    for i in range(count):
        across_cores(i).wait_send()
    for i in range(1, ws):
        for turn in range(3):
            send_sum(turn, i).wait_send()
        send_rows(i).wait_send()
        send_gain(i).wait_send()
    for i in range(1, ctx):
        send_wide(i).wait_send()
        send_pair(i).wait_send()
    for i in range(1, pairs):
        send_back(first_back + lax.rem(own_pair + i, pairs), i).wait_send()


def back(
    x, gains, cosines, sines, q, k, v, pack, attn, normed, w_qkv, w_out, cot, residual, ffn,
    hidden, grad_gate, grad_up, grad_sent, grad_keep, out_sent, out_keep, ws, ctx, own_heads,
):
    tokens, features = x.shape
    group, length, _ = q.shape
    units = hidden.shape[1]
    q_wide = group * HEAD_DIM
    wide = q_wide + 2 * HEAD_DIM
    pairs = ws * own_heads
    span = min(256, length) if length <= 1024 else tokens
    kept = length if length <= 1024 else span
    depth = features // ws
    total_rows = ws * tokens
    moved = (False, True, True, False, True)
    held = pltpu.VMEM
    widths = [features, units, units, features, own_heads * wide]
    halves = [units // 2, depth // 2, depth // 2, own_heads * q_wide // 2, depth // 2]
    rows, parts, sib, red, outs, counts = [], [], [], [], [], []
    for is_moved, n, half, want in zip(moved, widths, halves, ROWS):
        while half % want or not is_moved and half % (2 * want):
            want -= 16
        rows.append(want)
        lead = (ws,) if is_moved else ()
        parts.append(held(lead + (2, half, n), BF))
        sib.append(held(lead + (half, n), BF))
        red.append(held(lead + (half, n), BF))
        outs.append((2, half, ws * n if is_moved else n))
        counts.append(half // want * (ws if is_moved else 1))
    ticks = sum(counts) // 2 + SKEW * (ctx - 1)
    k_count = len(parts)
    vmem, anywhere = pl.BlockSpec(memory_space=pltpu.VMEM), pl.BlockSpec(memory_space=pl.ANY)
    shape = jax.ShapeDtypeStruct
    results = pl.pallas_call(
        functools.partial(
            back_kernel, ws, ctx, group, own_heads, moved, tuple(rows), ticks
        ),
        out_shape=[
            shape((tokens, features), BF), shape((tokens, features), F32), shape(gains.shape, F32)
        ]
        + [shape(o, BF) for o in outs],
        in_specs=[vmem] * 2 + [anywhere] * 20,
        out_specs=[vmem] * 3 + [anywhere] * k_count,
        scratch_shapes=parts
        + sib
        + red
        + [dma(n) for _ in range(8) for n in counts]
        + [
            held((group, kept, HEAD_DIM), BF),
            held(k.shape, BF),
            held(v.shape, BF),
            held((group, kept, 128), F32),
            held(attn.shape, BF),
            held(normed.shape, BF),
            held(w_qkv.shape, BF),
            held(w_out.shape, BF),
            held(cot.shape, BF),
            held((tokens, features), F32),
            held((total_rows, units), BF),
            held((total_rows, units), BF),
            held((total_rows, units), BF),
            held((tokens, features), F32),
            held((features, total_rows), BF),
            held((units, total_rows), BF),
            held((ws, tokens, features), BF),
            held((pairs, tokens, q_wide), BF),
            held((ctx, tokens, q_wide), BF),
            held((tokens, features), F32),
            held((group, kept, HEAD_DIM), F32),
            held((length, HEAD_DIM), F32),
            held((length, HEAD_DIM), F32),
            held((HEAD_DIM, length), BF),
            held((ctx, tokens, wide), BF),
            held((pairs, tokens, wide), BF),
            held((total_rows, own_heads * wide), BF),
            held((2, ws, tokens, features), BF),
            held((tokens, features), F32),
            held(gains.shape, F32),
            held((ws,) + gains.shape, F32),
            held((ctx,) + gains.shape, F32),
            held((span, wide), F32),
            held((span, wide), F32),
            dma(k_count), dma(k_count), dma(16), dma(2, ws), dma(2, ctx), dma(2, pairs),
            dma(2, 3, ws), dma(2, ws), dma(2, ctx), dma(2),
        ],
        compiler_params=pltpu.CompilerParams(
            collective_id=3, has_side_effects=True, vmem_limit_bytes=63 << 20
        ),
        name="back",
    )(
        x, gains, cosines, sines, q, k, v, pack, attn, normed, w_qkv, w_out, cot, residual, ffn,
        hidden, grad_gate, grad_up, grad_sent, grad_keep, out_sent, out_keep,
    )
    sums = [s.reshape(s.shape[0] * s.shape[1], s.shape[2]) for s in results[3:]]
    return results[0], results[1], results[2], sums


def tail_kernel(ws, group, *refs):
    low, refs = refs[:8], refs[8:]
    down, out, gate, up, qkv, output, grad_input, gain_sums = low
    (
        output_out, grad_input_out, attn_gain, g_query, g_key, g_value, g_out, ffn_gain, g_gate,
        g_up, g_down,
    ) = refs
    q_wide = group * HEAD_DIM
    wide = q_wide + 2 * HEAD_DIM
    output_out[...] = output[...].reshape(output_out.shape)
    grad_input_out[...] = grad_input[...].reshape(grad_input_out.shape)
    g_down[...] = down[...].astype(F32)
    g_out[...] = out[...].astype(F32)
    g_gate[...] = gate[...].astype(F32)
    g_up[...] = up[...].astype(F32)
    heads = qkv.shape[1] // wide
    blocks = [qkv[:, h * wide : (h + 1) * wide].astype(F32) for h in range(heads)]
    g_query[...] = jnp.concatenate([b[:, :q_wide] for b in blocks], axis=1)
    g_key[...] = jnp.concatenate([b[:, q_wide : q_wide + HEAD_DIM] for b in blocks], axis=1)
    g_value[...] = jnp.concatenate([b[:, q_wide + HEAD_DIM :] for b in blocks], axis=1)
    w = lax.axis_index("ws")
    depth = attn_gain.shape[0]
    for i in range(ws):

        @pl.when(w == i)
        def _():
            here = gain_sums[:, i * depth : (i + 1) * depth]
            attn_gain[...] = here[0]
            ffn_gain[...] = here[1]


def tail(down, out, gate, up, qkv, output, grad_input, gain_sums, token_shape, ws, group):
    depth = qkv.shape[0]
    steps = depth // 96
    features = out.shape[1]
    q_total = qkv.shape[1] * group // (group + 2)
    k_total = q_total // group
    shape = jax.ShapeDtypeStruct

    def split(rows, *rest):
        return pl.BlockSpec((rows // steps,) + rest, lambda n: (n,) + (0,) * len(rest))

    def whole(*dims):
        return pl.BlockSpec(dims, lambda n: (0,) * len(dims))

    out_shape = [
        shape(token_shape, BF), shape(token_shape, F32), shape((depth,), F32),
        shape((depth, q_total), F32), shape((depth, k_total), F32), shape((depth, k_total), F32),
        shape(out.shape, F32), shape((depth,), F32), shape(gate.shape, F32),
        shape(up.shape, F32), shape(down.shape, F32),
    ]
    return pl.pallas_call(
        functools.partial(tail_kernel, ws, group),
        grid=(steps,),
        out_shape=out_shape,
        in_specs=[split(*a.shape) for a in (down, out, gate, up, qkv, output, grad_input)]
        + [whole(*gain_sums.shape)],
        out_specs=[
            whole(*o.shape) if len(o.shape) == 1 else split(*o.shape) for o in out_shape
        ],
        compiler_params=pltpu.CompilerParams(vmem_limit_bytes=63 << 20),
        name="tail",
    )(down, out, gate, up, qkv, output, grad_input, gain_sums)


def body(
    hidden_in,
    attn_gain,
    w_query,
    key_weight,
    value_weight,
    w_out,
    ffn_gain,
    w_gate,
    w_up,
    w_down,
    cotangent,
):
    ws, ctx = lax.axis_size("ws"), lax.axis_size("ctx")
    local_len, local_seqs, features = hidden_in.shape
    row_count = local_len * local_seqs
    q_heads = w_query.shape[1] // HEAD_DIM
    kv_heads = key_weight.shape[1] // HEAD_DIM
    group = q_heads // kv_heads
    own_heads = kv_heads // ws
    wide = (group + 2) * HEAD_DIM
    q_wide = group * HEAD_DIM
    pairs = ws * local_seqs * own_heads
    copies = ctx // pairs
    depth = features // ws
    cosines, sines = rope_tables(ctx * local_len, group + 1, 1)
    gains = jnp.stack([attn_gain, ffn_gain]).astype(F32)
    gains = lax.dynamic_update_slice(
        jnp.zeros((8, features), F32), gains, (0, lax.axis_index("ws") * depth)
    )
    inputs = hidden_in.reshape(row_count, features)
    grad_low = cotangent.reshape(row_count, features)
    (
        normed_attn, w_qkv, q_pair, k_pair, v_pair, pack, attn_in, grad_low_all, gains,
        residual, normed_ffn, hidden, grad_gate, grad_up, grad_sent, grad_keep, out_sent, out_keep,
    ) = front(
        inputs, gains, w_query, key_weight, value_weight, w_gate, w_up, grad_low, cosines, sines,
        w_out, w_down, ws, ctx, own_heads, group,
    )
    output, grad_input, gain_sums, (g_down, g_gate, g_up, g_out, g_qkv) = back(
        inputs, gains, cosines, sines, q_pair, k_pair, v_pair, pack, attn_in, normed_attn, w_qkv,
        w_out, grad_low_all, residual, normed_ffn, hidden, grad_gate, grad_up, grad_sent,
        grad_keep, out_sent, out_keep, ws, ctx, own_heads,
    )
    results = tail(
        g_down, g_out, g_gate, g_up, g_qkv, output, grad_input, gain_sums, hidden_in.shape, ws, group
    )
    output, grad_input, attn_gain_sum, *middle_sums = results
    *middle_sums, ffn_gain_sum, g_gate, g_up, g_down = middle_sums
    return (
        output,
        grad_input,
        attn_gain_sum,
        *middle_sums,
        ffn_gain_sum,
        g_gate,
        g_up,
        g_down,
    )


def solution(mesh):
    tokens, rows, one = P("ctx", "ws", None), P("ws", None), P("ws")
    return jax.shard_map(
        body,
        mesh=mesh,
        in_specs=(tokens, one, rows, rows, rows, rows, one, rows, rows, rows, tokens),
        out_specs=(tokens, tokens, one, rows, rows, rows, rows, one, rows, rows, rows),
        check_vma=False,
    )
```

```python
import functools

import jax
import jax.numpy as jnp
import numpy as np
from jax import lax
from jax.experimental import pallas as pl
from jax.experimental.pallas import tpu as pltpu
from jax.sharding import PartitionSpec as P

HEAD_DIM = 96
EPSILON = 1e-05
ROPE_BASE = 100000.0
MASK_FILL = -1e30
BF = jnp.bfloat16
F32 = jnp.float32


def rope_tables(length, rotated_heads, plain_heads):
    half = HEAD_DIM // 2
    frequency = np.float32(ROPE_BASE) ** (-(np.arange(half, dtype=np.float32) * 2.0 / HEAD_DIM))
    angles = np.arange(length, dtype=np.float32)[:, None] * frequency[None, :].astype(np.float32)
    cosine, sine = np.cos(angles), np.sin(angles)
    plain = np.zeros((length, plain_heads * HEAD_DIM), np.float32)
    cosines = [cosine, cosine] * rotated_heads + [plain + 1.0]
    sines = [-sine, sine] * rotated_heads + [plain]
    return (
        jnp.asarray(np.concatenate(cosines, axis=-1), F32),
        jnp.asarray(np.concatenate(sines, axis=-1), F32),
    )


MESH = pl.DeviceIdType.MESH


def remote(src, dst, send_sem, recv_sem, device):
    return pltpu.make_async_remote_copy(
        src_ref=src, dst_ref=dst, send_sem=send_sem, recv_sem=recv_sem,
        device_id=device, device_id_type=MESH,
    )


def dma(*shape):
    return pltpu.SemaphoreType.DMA(shape)


def at_rows(ref, start, size):
    return ref.at[pl.ds(pl.multiple_of(start, size), size), :]


def greet(devices):
    barrier = pltpu.get_barrier_semaphore()
    for device in devices:
        pl.semaphore_signal(barrier, inc=1, device_id=device, device_id_type=MESH)
    pl.semaphore_wait(barrier, len(devices))


def swap_lanes(vectors):
    lanes = lax.broadcasted_iota(jnp.int32, vectors.shape, 1)
    width, half = vectors.shape[1], HEAD_DIM // 2
    first = lax.rem(lanes, HEAD_DIM) < half
    return jnp.where(first, pltpu.roll(vectors, width - half, 1), pltpu.roll(vectors, half, 1))


class RowSpread:
    def __init__(self, own, everyone, send_sem, recv_sem, c, w, ws):
        self.own, self.everyone, self.ws = own, everyone, ws
        self.send_sem, self.recv_sem, self.c, self.w = send_sem, recv_sem, c, w
        self.half = own.shape[0] // 2
        self.square = ws == 4
        if self.square:
            self.beside = (w + 1 - 2 * lax.rem(w, 2), lax.rem(w + 2, 4))
            self.far = 3 - w

    def rows(self, ref, h):
        return ref.at[pl.ds(h * self.half, self.half), :]

    def direct(self, i):
        return remote(
            self.own, self.everyone.at[self.w], self.send_sem.at[i], self.recv_sem.at[i],
            (self.c, lax.rem(self.w + i, self.ws)),
        )

    def first(self, n, h):
        return remote(
            self.rows(self.own, h), self.rows(self.everyone.at[self.w], h),
            self.send_sem.at[2 * n + h], self.recv_sem.at[2 * n + h], (self.c, self.beside[n]),
        )

    def onward(self, n):
        block = self.rows(self.everyone.at[self.beside[n]], n)
        return remote(
            block, block, self.send_sem.at[4 + n], self.recv_sem.at[4 + n],
            (self.c, self.beside[1 - n]),
        )

    def start(self):
        if self.square:
            for h in range(2):
                for n in range(2):
                    self.first(n, n if h == 0 else 1 - n).start()
        else:
            for i in range(1, self.ws):
                self.direct(i).start()

    def block(self, i):
        if not self.square:
            return lax.rem(self.w + self.ws - i, self.ws)
        low, high = lax.rem(self.w + i, 2), lax.rem(self.w // 2 + i // 2, 2)
        return low + 2 * high

    def pass_on(self):
        if self.square:
            for n in range(2):
                self.first(n, n).wait_recv()
                self.onward(n).start()

    def wait_block(self, i):
        if not self.square:
            self.direct(i + 1).wait_recv()
        elif i < 2:
            self.first(i, 1 - i).wait_recv()
        else:
            self.onward(0).wait_recv()
            self.onward(1).wait_recv()

    def wait_sent(self):
        if self.square:
            for n in range(2):
                for h in range(2):
                    self.first(n, h).wait_send()
                self.onward(n).wait_send()
        else:
            for i in range(1, self.ws):
                self.direct(i).wait_send()


class LineSlices:
    def __init__(self, ws, line, place, c, w, fetch, block, pass_sem, line_sem):
        self.ws, self.line, self.place, self.c, self.w = ws, line, place, c, w
        self.fetch, self.block, self.pass_sem, self.line_sem = fetch, block, pass_sem, line_sem
        self.core = lax.rem(c, 2)

    def along(self, i, z, right):
        slice_ref = self.block(i, z, self.core)
        return remote(
            slice_ref, slice_ref, self.line_sem.at[0, right, i, z], self.line_sem.at[1, 0, i, z],
            (self.c + 2 if right else self.c - 2, self.w),
        )

    def across(self, i, z, core):
        slice_ref = self.block(i, z, core)
        return remote(
            slice_ref, slice_ref, self.pass_sem.at[0, i, z], self.pass_sem.at[1, i, z],
            (self.c + 1 - 2 * self.core, self.w),
        )

    def neighbours(self, act):
        if self.line > 1:
            for right in range(2):

                @pl.when((self.place < self.line - 1) if right else (self.place > 0))
                def _():
                    act(right)

    def from_chips(self, hops, act):
        for h in hops:
            for right in range(2):
                z = self.place + h if right else self.place - h

                @pl.when((z >= 0) & (z < self.line))
                def _():
                    act(z, right)

    def start(self):
        for i in range(1, self.ws):
            self.fetch(i).wait_recv()
            self.across(i, self.place, self.core).start()
            self.neighbours(lambda right: self.along(i, self.place, right).start())

    def arrive(self, hops):
        def one(z, right):
            for i in range(1, self.ws):
                self.along(i, z, right).wait_recv()

                @pl.when((self.place > 0) if right else (self.place < self.line - 1))
                def _():
                    self.along(i, z, 1 - right).start()

                self.across(i, z, self.core).start()

        self.from_chips(hops, one)

    def finish(self):
        for i in range(1, self.ws):
            for z in range(self.line):
                self.across(i, z, 1 - self.core).wait_recv()

    def wait_sent(self):
        for i in range(1, self.ws):
            self.fetch(i).wait_send()
            for z in range(self.line):
                self.across(i, z, self.core).wait_send()
            self.neighbours(lambda right: self.along(i, self.place, right).wait_send())

        def one(z, right):
            for i in range(1, self.ws):

                @pl.when((self.place > 0) if right else (self.place < self.line - 1))
                def _():
                    self.along(i, z, 1 - right).wait_send()

        self.from_chips(range(1, self.line), one)


class RowSum:
    def __init__(self, sent, landed, relay, send_sem, recv_sem, c, w, ws):
        self.sent, self.landed, self.relay, self.ws = sent, landed, relay, ws
        self.send_sem, self.recv_sem, self.c, self.w = send_sem, recv_sem, c, w
        self.half = sent.shape[1] // 2
        self.square = ws == 4
        if self.square:
            self.beside = (w + 1 - 2 * lax.rem(w, 2), lax.rem(w + 2, 4))
            self.far = 3 - w

    def rows(self, ref, h):
        return ref.at[pl.ds(h * self.half, self.half), :]

    def owner(self, n):
        if not self.square:
            return lax.rem(self.w + n + 1, self.ws)
        i = jnp.where(n == 0, 3, jnp.where(n == 3, 0, n))
        low, high = lax.rem(self.w + i, 2), lax.rem(self.w // 2 + i // 2, 2)
        return low + 2 * high

    def direct(self, i):
        to = lax.rem(self.w + i, self.ws)
        return remote(
            self.sent.at[to], self.landed.at[self.w], self.send_sem.at[i], self.recv_sem.at[i],
            (self.c, to),
        )

    def corner(self, n):
        return remote(
            self.rows(self.sent.at[self.far], n), self.relay.at[n],
            self.send_sem.at[n], self.recv_sem.at[n], (self.c, self.beside[n]),
        )

    def near(self, n, h):
        return remote(
            self.rows(self.sent.at[self.beside[n]], h), self.rows(self.landed.at[n], h),
            self.send_sem.at[2 + 2 * n + h], self.recv_sem.at[2 + 2 * n + h],
            (self.c, self.beside[n]),
        )

    def start(self, n):
        if not self.square:
            for i in range(1, self.ws):

                @pl.when(n == i - 1)
                def _():
                    self.direct(i).start()

            return

        @pl.when(n == 0)
        def _():
            self.corner(0).start()
            self.corner(1).start()

        for i in range(2):

            @pl.when(n == i + 1)
            def _():
                self.near(i, i).start()

    def total(self, own):
        if not self.square:
            for i in range(1, self.ws):
                self.direct(i).wait_recv()
                own = own + self.landed[lax.rem(self.w + self.ws - i, self.ws)].astype(F32)
            return own
        for n in range(2):
            self.corner(n).wait_recv()
            mine = self.rows(self.sent.at[self.beside[1 - n]], n)
            mine[...] = (mine[...].astype(F32) + self.relay[n].astype(F32)).astype(BF)
            self.near(1 - n, n).start()
        for n in range(2):
            self.near(n, 0).wait_recv()
            self.near(n, 1).wait_recv()
            own = own + self.landed[n].astype(F32)
        return own

    def wait_sent(self):
        if not self.square:
            for i in range(1, self.ws):
                self.direct(i).wait_send()
            return
        for n in range(2):
            self.corner(n).wait_send()
            self.near(n, 0).wait_send()
            self.near(n, 1).wait_send()


def dot_bt(left, right):
    return lax.dot_general(left, right, (((1,), (1,)), ((), ())), preferred_element_type=F32)


def feed_forward(
    ws, own_heads, group, c, w, wait_cot, more_ffn, wait_ffn,
    x, attn, w_out, gains, cot, gate, up, w_down,
    residual_out, normed, hidden, grad_gate, grad_up, grad_sent, grad_keep, out_sent, out_keep,
    sent, landed, relay, grad_hidden, keep, rs_sem, ag_sem,
):
    rows, features = x.shape
    q_wide = group * HEAD_DIM
    units = gate.shape[1]
    total_rows = ws * rows
    tile = 256

    row_sum = RowSum(sent, landed, relay, rs_sem.at[0], rs_sem.at[1], c, w, ws)

    def project(n, _):
        s = row_sum.owner(n)
        part = jnp.zeros((rows, features), F32)
        for j in range(own_heads):
            part = part + jnp.dot(
                attn[s * own_heads + j], w_out[j * q_wide : (j + 1) * q_wide, :],
                preferred_element_type=F32,
            )

        @pl.when(n < ws - 1)
        def _():
            sent[s] = part.astype(BF)
            row_sum.start(n)

        @pl.when(n == ws - 1)
        def _():
            keep[...] = part

        return 0

    lax.fori_loop(0, ws, project, 0)

    wait_cot()

    def hidden_back(n, _):
        here = pl.ds(pl.multiple_of(n * tile, tile), tile)
        grad_hidden[:, here] = dot_bt(cot[...].reshape(total_rows, features), w_down[here, :])
        return 0

    lax.fori_loop(0, units // tile, hidden_back, 0)
    more_ffn()

    residual = row_sum.total(x[...].astype(F32) + keep[...])
    gain = gains[1:2]
    factor = lax.rsqrt(jnp.mean(residual * residual, axis=-1, keepdims=True) + EPSILON)
    normed[w] = (residual * factor * gain).astype(BF)
    spread = RowSpread(normed.at[w], normed, ag_sem.at[0], ag_sem.at[1], c, w, ws)
    spread.start()
    residual_out[...] = residual
    wait_ffn()

    def feed(i, _):
        s = spread.block(i)
        here = pl.ds(pl.multiple_of(s * rows, rows), rows)
        for n in range(1, ws):

            @pl.when(i == n)
            def _():
                if n == 1:
                    spread.pass_on()
                spread.wait_block(n - 1)

        block = normed[s]

        def columns(n, _):
            cut = pl.ds(pl.multiple_of(n * tile, tile), tile)
            gate_proj = jnp.dot(block, gate[:, cut], preferred_element_type=F32)
            up_proj = jnp.dot(block, up[:, cut], preferred_element_type=F32)
            sigmoid = 1.0 / (1.0 + jnp.exp(-gate_proj))
            activation = gate_proj * sigmoid
            grad = grad_hidden[here, cut]
            hidden[here, cut] = (activation * up_proj).astype(BF)
            grad_up[here, cut] = (grad * activation).astype(BF)
            grad_gate[here, cut] = (
                grad * up_proj * sigmoid * (1.0 + gate_proj * (1.0 - sigmoid))
            ).astype(BF)
            return 0

        lax.fori_loop(0, units // tile, columns, 0)

        def back(n, _):
            cut = pl.ds(pl.multiple_of(n * tile, tile), tile)
            part = dot_bt(grad_gate[here, :], gate[cut, :]) + dot_bt(grad_up[here, :], up[cut, :])

            @pl.when(i > 0)
            def _():
                grad_sent[s, :, cut] = part.astype(BF)

            @pl.when(i == 0)
            def _():
                grad_keep[:, cut] = part

            return 0

        lax.fori_loop(0, features // tile, back, 0)
        return 0

    lax.fori_loop(0, ws, feed, 0)

    def down_columns(n, _):
        cut = pl.ds(pl.multiple_of(n * tile, tile), tile)
        part = jnp.dot(hidden[...], w_down[:, cut], preferred_element_type=F32)
        out_sent[:, :, cut] = part.astype(BF).reshape(ws, rows, tile)
        own = hidden[pl.ds(pl.multiple_of(w * rows, rows), rows), :]
        out_keep[:, cut] = jnp.dot(own, w_down[:, cut], preferred_element_type=F32)
        return 0

    lax.fori_loop(0, features // tile, down_columns, 0)

    def wait_sent():
        row_sum.wait_sent()
        spread.wait_sent()

    return wait_sent


def front_kernel(
    ws, ctx, own_heads, group,
    x, gains, wq, wk, wv, gate, up, cot, cosines, sines, w_out_all, w_down_all,
    normed_out, w_all_out, q_done, k_done, v_done, pack_done, attn_in, cot_all, gains_all,
    residual, normed_ffn, hidden, grad_gate, grad_up, grad_sent, grad_keep, out_sent, out_keep,
    normed, w_all, q_out, k_out, v_out, pack, gate_all, up_all, w_out, w_down,
    landed, relay, grad_hidden, keep, rs_sem, ag_sem, load_sem, save_sem,
    x_all, g_in, w_stage, raw, qkv_stage, pair, attn_stage, cos, sin,
    x_sem, g_sem, w_sem, wf_sem, lw_sem, line_sem, ffn_sem, ff_sem, fu_sem, cot_sem, pair_sem, back_sem, own_sem,
):
    c, w = lax.axis_index("ctx"), lax.axis_index("ws")
    core = lax.rem(c, 2)
    sibling = (c + 1 - 2 * core, w)
    rows = x.shape[0]
    depth = wq.shape[0]
    half = depth // 2
    q_wide = group * HEAD_DIM
    wide = q_wide + 2 * HEAD_DIM
    pairs = ws * own_heads
    units = gate_all.shape[1]
    peer = [lax.rem(w + i, ws) for i in range(ws)]
    origin = [lax.rem(w + ws - i, ws) for i in range(ws)]

    def rope_copy(i):
        table, kept = ((cosines, cos), (sines, sin))[i]
        return pltpu.make_async_copy(at_rows(table, c * rows, rows), kept, own_sem.at[i])

    rope_copy(0).start()
    rope_copy(1).start()
    near = [(lax.rem(c + i, ctx), w) for i in range(1, ctx)]
    greet(near + [(c, peer[i]) for i in range(1, ws)])

    def send_gain(i):
        return remote(gains, g_in.at[w], g_sem.at[0, i], g_sem.at[1, i], (c, peer[i]))

    spread_x = RowSpread(x, x_all, x_sem.at[0], x_sem.at[1], c, w, ws)
    spread_cot = RowSpread(cot, cot_all, cot_sem.at[0], cot_sem.at[1], c, w, ws)
    shared = depth % (16 * ctx) == 0

    def sliced(along_line, fetch, block, sem, send_sem, recv_sem):
        size = depth // ctx if along_line else half
        own = c * size if along_line else core * size

        def start(i):
            source, to = fetch(i, own, size)
            return remote(source, to, send_sem.at[i], recv_sem.at[i], (c, peer[i]))

        return LineSlices(
            ws, ctx // 2 if along_line else 1, c // 2 if along_line else 0, c, w, start,
            lambda i, z, of: block(i, (2 * z + of) * size, size), *sem,
        )

    def ffn_slices(which, along_line):
        held, everyone = ((gate, gate_all), (up, up_all))[which]

        def fetch(i, first, size):
            columns = pl.ds(pl.multiple_of(peer[i] * units, 128), units)
            source = held.at[pl.ds(pl.multiple_of(first, size), size), columns]
            return source, at_rows(everyone, w * depth + first, size)

        return sliced(
            along_line, fetch,
            lambda i, first, size: at_rows(everyone, origin[i] * depth + first, size),
            ((ff_sem, line_sem), (fu_sem, line_sem))[which],
            ffn_sem.at[0, which], ffn_sem.at[1, which],
        )

    slices_w = sliced(
        shared,
        lambda i, first, size: (
            at_rows(w_stage.at[peer[i]], first, size), at_rows(w_all.at[w], first, size)
        ),
        lambda i, first, size: at_rows(w_all.at[origin[i]], first, size),
        (wf_sem, lw_sem), w_sem.at[0], w_sem.at[1],
    )
    slices_gate = ffn_slices(0, shared)
    slices_up = ffn_slices(1, False)

    mine = pl.ds(pl.multiple_of(w * units, 128), units)
    own_rows = pl.ds(pl.multiple_of(w * depth, depth), depth)

    def load(i):
        source, to = (
            (gate.at[:, mine], gate_all.at[own_rows, :]),
            (up.at[:, mine], up_all.at[own_rows, :]),
            (w_down_all, w_down),
            (w_out_all, w_out),
            (cot, cot_all.at[w]),
        )[i]
        return pltpu.make_async_copy(source, to, load_sem.at[i])

    def save(i):
        source, to = (
            (normed, normed_out), (w_all, w_all_out), (q_out, q_done), (k_out, k_done),
            (v_out, v_done), (pack, pack_done),
        )[i]
        return pltpu.make_async_copy(source, to, save_sem.at[i])

    def send_pair(i):
        to = lax.rem(c + i, ctx)
        return remote(
            qkv_stage.at[lax.rem(to, pairs)], pair.at[c],
            pair_sem.at[0, i], pair_sem.at[1, i], (to, w),
        )

    first_back = c // pairs * pairs
    own_pair = lax.rem(c, pairs)

    def back_copy(to, i):
        return remote(
            attn_stage.at[to], attn_in.at[own_pair],
            back_sem.at[0, i], back_sem.at[1, i], (to, w),
        )

    for i in range(1, ws):
        send_gain(i).start()
    for d in range(ws):
        for j in range(own_heads):
            h = d * own_heads + j
            w_stage[d, :, j * wide : (j + 1) * wide] = jnp.concatenate(
                [
                    wq[:, h * q_wide : (h + 1) * q_wide],
                    wk[:, h * HEAD_DIM : (h + 1) * HEAD_DIM],
                    wv[:, h * HEAD_DIM : (h + 1) * HEAD_DIM],
                ],
                axis=1,
            )
    for i in range(1, ws):
        slices_w.fetch(i).start()
    spread_x.start()
    w_all[w] = w_stage[w]
    for i in range(5):
        load(i).start()
    total_gain = gains[...]
    for i in range(1, ws):
        send_gain(i).wait_recv()
        total_gain = total_gain + g_in[origin[i]]
    gains_all[...] = total_gain
    gain = total_gain[0:1]

    def norm_block(index, block):
        wide_block = block.astype(F32)
        factor = lax.rsqrt(jnp.mean(wide_block * wide_block, axis=-1, keepdims=True) + EPSILON)
        normed[index] = (wide_block * factor * gain).astype(BF)

    norm_block(w, x[...])
    slices_w.start()
    slices_w.arrive(range(1, slices_w.line)[:1])
    spread_x.pass_on()
    for i in range(1, ws):
        slices_gate.fetch(i).start()
    for i in range(1, ws):
        slices_up.fetch(i).start()
    spread_cot.start()
    slices_w.arrive(range(2, slices_w.line))
    for i in range(1, ws):
        spread_x.wait_block(i - 1)
        norm_block(spread_x.block(i), x_all[spread_x.block(i)])
    slices_w.finish()

    left = normed[...].reshape(ws * rows, normed.shape[2])
    step = 256 if raw.shape[1] % 256 == 0 else 128
    for n in range(0, raw.shape[1], step):
        right = w_all[:, :, n : n + step].reshape(ws * depth, step)
        raw[:, n : n + step] = jnp.dot(left, right, preferred_element_type=F32)
    rope_copy(0).wait()
    rope_copy(1).wait()
    for s in range(ws):
        for j in range(own_heads):
            block = raw[s * rows : (s + 1) * rows, j * wide : (j + 1) * wide]
            turned = block * cos[...] + swap_lanes(block) * sin[...]
            qkv_stage[s * own_heads + j] = turned.astype(BF)
    for i in range(1, ctx):
        send_pair(i).start()
    pair[c] = qkv_stage[own_pair]

    def split(index):
        block = pair[index]
        here = pl.ds(pl.multiple_of(index * rows, rows), rows)
        for g in range(group):
            q_out[g, here, :] = block[:, g * HEAD_DIM : (g + 1) * HEAD_DIM]
        k_out[here, :] = block[:, q_wide : q_wide + HEAD_DIM]
        v_out[here, :] = block[:, q_wide + HEAD_DIM :]

    split(c)
    for i in range(1, ctx):
        from_c = lax.rem(c + ctx - i, ctx)
        send_pair(i).wait_recv()
        split(from_c)

    slices_gate.start()
    length = ctx * rows
    span = min(256, length)
    lane = lax.broadcasted_iota(jnp.int32, (span, HEAD_DIM), 1)

    def attend(start, keys, diagonal):
        here = pl.ds(start, span)
        heads = []
        allowed = start + lax.broadcasted_iota(
            jnp.int32, (span, keys), 0
        ) >= lax.broadcasted_iota(jnp.int32, (span, keys), 1)
        for g in range(group):
            scores = lax.dot_general(
                q_out[g, here, :], k_out[0:keys, :], (((1,), (1,)), ((), ())),
                preferred_element_type=F32,
            ) * HEAD_DIM**-0.5
            scores = jnp.where(allowed, scores, MASK_FILL)
            top = jnp.max(scores, axis=1, keepdims=True)
            weights = jnp.exp(scores - top)
            total = jnp.sum(weights, axis=1, keepdims=True)
            mixed = jnp.dot(
                weights.astype(BF), v_out[0:keys, :], preferred_element_type=F32
            ) / total
            pack[g, here, 0:HEAD_DIM] = mixed
            pack[g, here, HEAD_DIM:128] = jnp.where(
                lane[:, : 128 - HEAD_DIM] == 0, top, total
            )
            heads.append(mixed)
        low = jnp.concatenate(heads, axis=1).astype(BF)
        for b in range(span // rows):
            attn_stage[start // rows + b] = low[b * rows : (b + 1) * rows]

    if length <= 1024:
        for start in range(0, length, span):
            attend(start, start + span, start)
    else:

        def attend_at(index, _):
            attend(pl.multiple_of(index * span, span), length, 0)
            return 0

        lax.fori_loop(0, length // span, attend_at, 0)
    for i in range(1, pairs):
        back_copy(first_back + lax.rem(own_pair + i, pairs), i).start()
    attn_in[own_pair] = attn_stage[c]
    spread_cot.pass_on()
    slices_gate.arrive(range(1, slices_gate.line)[:1])
    for i in range(6):
        save(i).start()
    for i in range(1, pairs):
        source = lax.rem(own_pair + pairs - i, pairs)
        arriving = remote(
            attn_stage.at[c], attn_in.at[source],
            back_sem.at[0, i], back_sem.at[1, i], (first_back + source, w),
        )
        arriving.wait_recv()
    load(3).wait()

    def wait_cot():
        slices_up.start()
        load(4).wait()
        load(2).wait()
        for i in range(1, ws):
            spread_cot.wait_block(i - 1)

    def more_ffn():
        slices_gate.arrive(range(2, slices_gate.line - 1))

    def wait_ffn():
        slices_gate.arrive(range(1, slices_gate.line)[1:][-1:])
        slices_gate.finish()
        slices_up.finish()
        load(0).wait()
        load(1).wait()

    spread_x.wait_sent()
    wait_sent = feed_forward(
        ws, own_heads, group, c, w, wait_cot, more_ffn, wait_ffn,
        x, attn_in, w_out, gains_all, cot_all, gate_all, up_all, w_down,
        residual, normed_ffn, hidden, grad_gate, grad_up, grad_sent, grad_keep, out_sent, out_keep,
        x_all, landed, relay, grad_hidden, keep, rs_sem, ag_sem,
    )
    wait_sent()
    for i in range(6):
        save(i).wait()
    for i in range(1, ws):
        send_gain(i).wait_send()
    slices_w.wait_sent()
    slices_gate.wait_sent()
    slices_up.wait_sent()
    spread_cot.wait_sent()
    for i in range(1, ctx):
        send_pair(i).wait_send()
    for i in range(1, pairs):
        back_copy(first_back + lax.rem(own_pair + i, pairs), i).wait_send()


def front(
    x, gains, wq, wk, wv, gate, up, cot, cosines, sines, w_out, w_down, ws, ctx, own_heads, group
):
    rows, features = x.shape
    depth = wq.shape[0]
    q_wide = group * HEAD_DIM
    wide = q_wide + 2 * HEAD_DIM
    pairs = ws * own_heads
    length = ctx * rows
    units = gate.shape[1] // ws
    total = ws * rows
    vmem, anywhere = pl.BlockSpec(memory_space=pltpu.VMEM), pl.BlockSpec(memory_space=pl.ANY)
    shape = jax.ShapeDtypeStruct
    return pl.pallas_call(
        functools.partial(front_kernel, ws, ctx, own_heads, group),
        out_shape=[
            shape((ws, rows, features), BF),
            shape((ws, depth, own_heads * wide), BF),
            shape((group, length, HEAD_DIM), BF),
            shape((length, HEAD_DIM), BF),
            shape((length, HEAD_DIM), BF),
            shape((group, length, 128), F32),
            shape((pairs, rows, q_wide), BF),
            shape((ws, rows, features), BF),
            shape(gains.shape, F32),
            shape((rows, features), F32),
            shape((ws, rows, features), BF),
            shape((total, units), BF),
            shape((total, units), BF),
            shape((total, units), BF),
            shape((ws, rows, features), BF),
            shape((rows, features), F32),
            shape((ws, rows, features), BF),
            shape((rows, features), F32),
        ],
        in_specs=[vmem] * 5 + [anywhere] * 7,
        out_specs=[anywhere] * 6 + [vmem] * 12,
        scratch_shapes=[
            pltpu.VMEM((ws, rows, features), BF),
            pltpu.VMEM((ws, depth, own_heads * wide), BF),
            pltpu.VMEM((group, length, HEAD_DIM), BF),
            pltpu.VMEM((length, HEAD_DIM), BF),
            pltpu.VMEM((length, HEAD_DIM), BF),
            pltpu.VMEM((group, length, 128), F32),
            pltpu.VMEM((features, units), BF),
            pltpu.VMEM((features, units), BF),
            pltpu.VMEM(w_out.shape, BF),
            pltpu.VMEM((units, features), BF),
            pltpu.VMEM((ws, rows, features), BF),
            pltpu.VMEM((2, rows // 2, features), BF),
            pltpu.VMEM((total, units), F32),
            pltpu.VMEM((rows, features), F32),
            dma(2, max(6, ws)), dma(2, max(6, ws)), dma(5), dma(6),
            pltpu.VMEM((ws, rows, features), BF),
            pltpu.VMEM((ws,) + gains.shape, F32),
            pltpu.VMEM((ws, depth, own_heads * wide), BF),
            pltpu.VMEM((ws * rows, own_heads * wide), F32),
            pltpu.VMEM((pairs, rows, wide), BF),
            pltpu.VMEM((ctx, rows, wide), BF),
            pltpu.VMEM((ctx, rows, q_wide), BF),
            pltpu.VMEM((rows, wide), F32),
            pltpu.VMEM((rows, wide), F32),
            dma(2, max(6, ws)), dma(2, ws), dma(2, ws), dma(2, ws, ctx // 2),
            dma(2, 2, ws, ctx // 2), dma(2, 2, ws, ctx // 2), dma(2, 2, ws),
            dma(2, ws, ctx // 2), dma(2, ws, ctx // 2), dma(2, max(6, ws)),
            dma(2, ctx), dma(2, pairs), dma(2),
        ],
        compiler_params=pltpu.CompilerParams(
            collective_id=1, has_side_effects=True, vmem_limit_bytes=63 << 20
        ),
        name="front",
    )(x, gains, wq, wk, wv, gate, up, cot, cosines, sines, w_out, w_down)


SKEW = 2
ROWS = (32, 48, 48, 32, 64)
TICK_NORM, TICK_ATTENDED, TICK_PAIRS, TICK_GATHER = 6, 12, 16, 5
UNITS_PER_TICK = 2


def back_kernel(
    ws, ctx, group, own_heads, moved, rows, ticks,
    x, gains, cosines, sines, q_all, k_all, v_all, pack_all, attn_all, normed_all, w_qkv_all,
    w_out_all, cot_all, residual_all, ffn_all, hidden_all, gate_all, up_all, grad_sent, grad_keep,
    out_sent, out_keep,
    output, grad_input, gain_out, *refs,
):
    count = len(moved)
    outs, refs = refs[:count], refs[count:]
    parts, refs = refs[:count], refs[count:]
    sib_buf, refs = refs[:count], refs[count:]
    red_in, refs = refs[:count], refs[count:]
    red_send, red_recv, hand_send, hand_recv, bc_send, bc_recv, core_send, core_recv = (
        refs[i * count : (i + 1) * count] for i in range(8)
    )
    (
        q, k, v, pack, attn, normed, w_qkv, w_out, cot, residual, hidden, grad_gate, grad_up,
        own_part, turned, turned_hidden, branch, pair_stage, grad_pair, grad_residual,
        grad_q, grad_k, grad_v, key_turned, back_stage, grad_in, grad_rows,
        landed, keep, own_gain, ws_gain, ctx_gain, cos, sin,
        sib_send, sib_recv, load_sem, ag_sem, to_pair_sem, pair_sem, rs_sem, gain_sem, wide_sem,
        rope_sem,
    ) = refs[8 * count :]
    c, w = lax.axis_index("ctx"), lax.axis_index("ws")
    core = lax.rem(c, 2)
    place, line = c // 2, ctx // 2
    sibling = (c + 1 - 2 * core, w)
    before, after = (c - 2, w), (c + 2, w)
    tokens, features = x.shape
    q_wide = group * HEAD_DIM
    wide = q_wide + 2 * HEAD_DIM
    pairs = ws * own_heads
    length = ctx * tokens
    depth = features // ws
    total_rows = ws * tokens
    units = hidden.shape[1]

    sources = (
        hidden_all, cot_all, ffn_all, gate_all, up_all, grad_keep, residual_all, w_out_all,
        attn_all, q_all, k_all, v_all, pack_all, w_qkv_all, normed_all, out_keep,
    )
    targets = (
        hidden, cot, normed, grad_gate, grad_up, own_part, residual, w_out,
        attn, q, k, v, pack, w_qkv, normed, own_part,
    )

    def load(i):
        return pltpu.make_async_copy(sources[i], targets[i], load_sem.at[i])

    for i in range(14):
        if length <= 1024 or i not in (9, 12):
            load(i).start()
    greet(
        [(lax.rem(c + i, ctx), w) for i in range(1, ctx)]
        + [(c, lax.rem(w + i, ws)) for i in range(1, ws)]
    )

    def send_sum(turn, i):
        to = lax.rem(w + i, ws)
        return remote(
            (grad_sent, out_sent, cot)[turn].at[to], landed.at[turn % 2, w],
            rs_sem.at[0, turn, i], rs_sem.at[1, turn, i], (c, to),
        )

    def landed_sum(turn, total):
        for i in range(1, ws):
            send_sum(turn, i).wait_recv()
            total = total + landed[turn % 2, lax.rem(w + ws - i, ws)].astype(F32)
        return total

    for i in range(1, ws):
        send_sum(0, i).start()

    def across_cores(i):
        half = parts[i].at[:, 1 - core] if moved[i] else parts[i].at[1 - core]
        return remote(half, sib_buf[i], sib_send.at[i], sib_recv.at[i], sibling)

    def spot(i, p, odd):
        if not moved[i]:
            return 2 * p + odd, None
        block = p // (ws // 2)
        return block, 2 * lax.rem(p, ws // 2) + lax.rem(block + odd, 2)

    def cut(i, block):
        return pl.ds(pl.multiple_of(block * rows[i], rows[i]), rows[i])

    def piece(i, p, odd, of):
        block, step = spot(i, p, odd)
        if not moved[i]:
            ref = parts[i].at[core] if of is parts else of[i]
            return ref.at[cut(i, block), :]
        owner = lax.rem(w + step, ws)
        ref = parts[i].at[owner, core] if of is parts else of[i].at[owner]
        return ref.at[cut(i, block), :]

    def final(i, p, odd, half, source):
        block, _ = spot(i, p, odd)
        if not moved[i]:
            return outs[i].at[half, cut(i, block), :]
        n = parts[i].shape[-1]
        columns = pl.ds(pl.multiple_of(source * n, 128), n)
        return outs[i].at[half, cut(i, block), columns]

    def source_of(i, p, odd):
        _, step = spot(i, p, odd)
        return None if step is None else lax.rem(w + ws - step, ws)

    def local(i, p, odd):
        here = piece(i, p, odd, parts)[...].astype(F32)
        return here + piece(i, p, odd, sib_buf)[...].astype(F32)

    def up_line(i, p, odd):
        e = 2 * p + odd
        return remote(
            piece(i, p, odd, parts), piece(i, p, odd, red_in),
            red_send[i].at[e], red_recv[i].at[e], after if odd else before,
        )

    def hand_over(i, p, odd):
        _, step = spot(i, p, odd)
        e = 2 * p + odd
        return remote(
            piece(i, p, odd, parts), final(i, p, odd, core, w),
            hand_send[i].at[e], hand_recv[i].at[e], (c, lax.rem(w + step, ws)),
        )

    def hand_here(i, p, odd):
        return pltpu.make_async_copy(
            piece(i, p, odd, parts), final(i, p, odd, core, w), hand_recv[i].at[2 * p + odd]
        )

    def down_line(i, p, odd):
        total = final(i, p, odd, core, source_of(i, p, odd))
        e = 2 * p + odd
        return remote(
            total, total, bc_send[i].at[e], bc_recv[i].at[e], before if odd else after
        )

    def over(i, p, odd, half):
        total = final(i, p, odd, half, source_of(i, p, odd))
        e = 2 * p + odd
        return remote(total, total, core_send[i].at[e], core_recv[i].at[e], sibling)

    def ends(odd):
        low, high = place == 0, place == line - 1
        return (low, high) if odd else (high, low)

    def either(i, p, odd, here, there):
        _, step = spot(i, p, odd)
        if step is None:
            here()
        else:
            pl.when(step == 0)(here)
            pl.when(step != 0)(there)

    def reduce_chunk(i, p, odd):
        start, end = ends(odd)

        @pl.when(start)
        def _():
            piece(i, p, odd, parts)[...] = local(i, p, odd).astype(BF)
            up_line(i, p, odd).start()

        @pl.when(jnp.logical_not(start))
        def _():
            up_line(i, p, odd).wait_recv()
            total = local(i, p, odd) + piece(i, p, odd, red_in)[...].astype(F32)
            piece(i, p, odd, parts)[...] = total.astype(BF)

            @pl.when(jnp.logical_not(end))
            def _():
                up_line(i, p, odd).start()

            @pl.when(end)
            def _():
                either(
                    i, p, odd,
                    lambda: hand_here(i, p, odd).start(), lambda: hand_over(i, p, odd).start(),
                )

    def spread_chunk(i, p, odd):
        end, start = ends(odd)

        @pl.when(start)
        def _():
            def arrived():
                total = final(i, p, odd, core, source_of(i, p, odd))
                e = 2 * p + odd
                remote(
                    total, total, hand_send[i].at[e], hand_recv[i].at[e], (c, lax.rem(w + 1, ws))
                ).wait_recv()

            either(i, p, odd, lambda: hand_here(i, p, odd).wait(), arrived)

        @pl.when(jnp.logical_not(start))
        def _():
            down_line(i, p, odd).wait_recv()

        @pl.when(jnp.logical_not(end))
        def _():
            down_line(i, p, odd).start()

        over(i, p, odd, core).start()

    counts = [red_send[i].shape[0] // 2 for i in range(count)]
    first, total_chunks = [], 0
    for i in range(count):
        first.append(total_chunks)
        total_chunks += counts[i]
    lasts = first[1:] + [total_chunks]
    hops = (line - 1 - place, place)

    def chain(t):
        for i in range(count):

            @pl.when(t == first[i])
            def _():
                across_cores(i).wait_recv()

        for odd in range(2):
            at = t - SKEW * hops[odd]
            down = t - SKEW * (2 * line - 1 - hops[odd])

            @pl.when((at >= 0) & (at < total_chunks))
            def _():
                for i in range(count):

                    @pl.when((at >= first[i]) & (at < lasts[i]))
                    def _():
                        reduce_chunk(i, at - first[i], odd)

            @pl.when((down >= 0) & (down < total_chunks))
            def _():
                for i in range(count):

                    @pl.when((down >= first[i]) & (down < lasts[i]))
                    def _():
                        spread_chunk(i, down - first[i], odd)

    def down_weights():
        load(0).wait()
        load(1).wait()

        def turn(n, _):
            here = pl.ds(pl.multiple_of(n * 256, 256), 256)
            turned_hidden[here, :] = hidden[:, here].T
            return 0

        lax.fori_loop(0, units // 256, turn, 0)
        size = units // 4
        every = cot[...].reshape(total_rows, features)
        for side in range(2):
            h = core if side else 1 - core
            for n in range(2):
                at = pl.multiple_of((2 * h + n) * size, size)
                parts[0][h, n * size : (n + 1) * size, :] = jnp.dot(
                    turned_hidden[pl.ds(at, size), :], every, preferred_element_type=F32
                ).astype(BF)
            if side == 0:
                across_cores(0).start()

    def turn_rows():
        def turn(n, _):
            here = pl.ds(pl.multiple_of(n * 256, 256), 256)
            turned[here, :] = normed[:, :, here].reshape(total_rows, 256).T
            return 0

        lax.fori_loop(0, features // 256, turn, 0)

    def row_products(i, right, side):
        half = depth // 2
        h = core if side else 1 - core

        def one(o, _):
            here = pl.ds(pl.multiple_of(o * depth + h * half, half), half)
            parts[i][o, h] = jnp.dot(
                turned[here, :], right[...], preferred_element_type=F32
            ).astype(BF)
            return 0

        lax.fori_loop(0, ws, one, 0)
        if side == 0:
            across_cores(i).start()

    def turn_ffn():
        load(2).wait()
        turn_rows()
        load(14).start()

    def gate_weights(side):
        if side == 0:
            load(3).wait()
        row_products(1, grad_gate, side)

    def up_weights(side):
        if side == 0:
            load(4).wait()
        row_products(2, grad_up, side)

    def send_rows(i):
        return remote(
            branch.at[w], branch.at[w], ag_sem.at[0, i], ag_sem.at[1, i],
            (c, lax.rem(w + i, ws)),
        )

    def ffn_norm_back():
        load(5).wait()
        load(6).wait()
        grad_normed = landed_sum(0, own_part[...])
        load(15).start()
        here = residual[...]
        factor = lax.rsqrt(jnp.mean(here * here, axis=-1, keepdims=True) + EPSILON)
        unit = here * factor
        own_gain[...] = jnp.broadcast_to(
            jnp.sum(grad_normed * unit, axis=0, keepdims=True), own_gain.shape
        )
        grad = grad_normed * gains[1:2]
        mean = jnp.mean(grad * unit, axis=-1, keepdims=True)
        back_grad = cot[w].astype(F32) + factor * (grad - unit * mean)
        grad_residual[...] = back_grad
        branch[w] = back_grad.astype(BF)
        for i in range(1, ws):
            send_rows(i).start()

    def send_pair(i):
        to = lax.rem(c + i, ctx)
        return remote(
            pair_stage.at[lax.rem(to, pairs)], grad_pair.at[c],
            to_pair_sem.at[0, i], to_pair_sem.at[1, i], (to, w),
        )

    def attended_back():
        load(7).wait()
        for i in range(ws):
            s = lax.rem(w + ws - i, ws)
            if i:
                send_rows(i).wait_recv()
            grad_low = dot_bt(branch[s], w_out[...]).astype(BF)
            for j in range(own_heads):
                pair_stage[s * own_heads + j] = grad_low[:, j * q_wide : (j + 1) * q_wide]
        for i in range(1, ctx):
            send_pair(i).start()
        grad_pair[c] = pair_stage[lax.rem(c, pairs)]
        for i in range(1, ws):
            send_sum(1, i).start()

    def out_weights():
        load(8).wait()
        half = own_heads * q_wide // 2
        for h in range(2):
            j, low = divmod(h * half, q_wide)
            side = jnp.concatenate([attn[s * own_heads + j] for s in range(ws)], axis=0)
            parts[3][h] = jnp.dot(
                side.T[low : low + half], branch[...].reshape(total_rows, features),
                preferred_element_type=F32,
            ).astype(BF)
        across_cores(3).start()

    def finish_output():
        load(15).wait()
        output[...] = (landed_sum(1, residual[...] + own_part[...])).astype(BF)

    first_back = c // pairs * pairs
    own_pair = lax.rem(c, pairs)
    span = min(256, length) if length <= 1024 else tokens

    def back_unit(g, start, low, keys):
        here, there = pl.ds(start, span), pl.ds(low, keys)
        query = q[g, here, :]
        grad = (
            grad_pair[pl.ds(start // tokens, span // tokens), :, g * HEAD_DIM : (g + 1) * HEAD_DIM]
        ).reshape(span, HEAD_DIM)
        kept = pack[g, here, :]
        kept_turned = kept.T
        top, total = kept_turned[HEAD_DIM : HEAD_DIM + 1], kept_turned[HEAD_DIM + 1 : HEAD_DIM + 2]
        grad_wide = grad.astype(F32)
        delta = jnp.sum(grad_wide.T * kept_turned[:HEAD_DIM], axis=0, keepdims=True)
        scaled = (grad_wide / kept[:, HEAD_DIM + 1 : HEAD_DIM + 2]).astype(BF)
        scores = dot_bt(k[there, :], query) * HEAD_DIM**-0.5
        allowed = start + lax.broadcasted_iota(
            jnp.int32, (keys, span), 1
        ) >= low + lax.broadcasted_iota(jnp.int32, (keys, span), 0)
        weights = jnp.exp(jnp.where(allowed, scores, MASK_FILL) - top)
        grad_probs = dot_bt(v[there, :], grad)
        grad_scores = (weights * (1.0 / total) * (grad_probs - delta)).astype(BF)
        grad_k[there, :] += jnp.dot(grad_scores, query, preferred_element_type=F32)
        grad_v[there, :] += jnp.dot(weights.astype(BF), scaled, preferred_element_type=F32)
        turned_grad = jnp.dot(
            key_turned[:, there], grad_scores, preferred_element_type=F32
        )
        if length <= 1024:
            grad_q[g, here, :] = turned_grad.T
        else:
            grad_q[g, here, :] += turned_grad.T

    def send_back(to, i):
        return remote(
            back_stage.at[to], grad_in.at[own_pair],
            pair_sem.at[0, i], pair_sem.at[1, i], (to, w),
        )

    def rope_copy(i, start):
        table, kept = ((cosines, cos), (sines, sin))[i]
        return pltpu.make_async_copy(table.at[pl.ds(start, span), :], kept, rope_sem.at[i])

    def finish_rows(start):
        here = pl.ds(start, span)
        rope_copy(0, start).wait()
        rope_copy(1, start).wait()
        scale = HEAD_DIM**-0.5
        block = jnp.concatenate(
            [grad_q[g, here, :] * scale for g in range(group)]
            + [grad_k[here, :] * scale, grad_v[here, :]],
            axis=1,
        )
        block = (block * cos[...] - swap_lanes(block) * sin[...]).astype(BF)
        for b in range(span // tokens):
            to = start // tokens + b
            back_stage[to] = block[b * tokens : (b + 1) * tokens]

    def send_rows_back(to):
        step = lax.rem(to - c + ctx, pairs)

        @pl.when((to // pairs == c // pairs) & (to != c))
        def _():
            send_back(to, step).start()

        @pl.when(to == c)
        def _():
            grad_in[own_pair] = back_stage[to]

    def prepare():
        for i in range(9, 13):
            load(i).wait()
        for i in range(1, ctx):
            send_pair(i).wait_recv()
        grad_k[...] = jnp.zeros(grad_k.shape, F32)
        grad_v[...] = jnp.zeros(grad_v.shape, F32)
        key_turned[...] = k[...].T

    def turn_normed():
        load(14).wait()
        turn_rows()

    def gather_back():
        for i in range(1, pairs):
            source = lax.rem(own_pair + pairs - i, pairs)
            arriving = remote(
                back_stage.at[c], grad_in.at[source],
                pair_sem.at[0, i], pair_sem.at[1, i], (first_back + source, w),
            )
            arriving.wait_recv()
        for s in range(ws):
            for j in range(own_heads):
                grad_rows[s * tokens : (s + 1) * tokens, j * wide : (j + 1) * wide] = grad_in[
                    s * own_heads + j
                ]

    def sum_rows():
        load(13).wait()

        def one(i, _):
            s = lax.rem(w + i, ws)
            block = grad_rows[pl.ds(pl.multiple_of(s * tokens, tokens), tokens), :]
            for n in range(0, ws):
                part = dot_bt(block, w_qkv[n])

                @pl.when(i < ws)
                def _():
                    cot[s, :, n * depth : (n + 1) * depth] = part.astype(BF)

                @pl.when(i == ws)
                def _():
                    keep[:, n * depth : (n + 1) * depth] = part

            @pl.when(i < ws)
            def _():
                send_sum(2, i).start()

            return 0

        lax.fori_loop(1, ws + 1, one, 0)

    def weight_sums(side):
        row_products(4, grad_rows, side)

    def send_gain(i):
        return remote(
            own_gain, ws_gain.at[w], gain_sem.at[0, i], gain_sem.at[1, i],
            (c, lax.rem(w + i, ws)),
        )

    def send_wide(i):
        return remote(
            ws_gain.at[w], ctx_gain.at[c], wide_sem.at[0, i], wide_sem.at[1, i],
            (lax.rem(c + i, ctx), w),
        )

    def finish_input():
        total = landed_sum(2, keep[...])
        inputs = x[...].astype(F32)
        factor = lax.rsqrt(jnp.mean(inputs * inputs, axis=-1, keepdims=True) + EPSILON)
        unit = inputs * factor
        row = lax.broadcasted_iota(jnp.int32, own_gain.shape, 0)
        attn_gain = jnp.sum(total * unit, axis=0, keepdims=True)
        own_gain[...] = jnp.where(row == 0, attn_gain, own_gain[...])
        for i in range(1, ws):
            send_gain(i).start()
        grad = total * gains[0:1]
        mean = jnp.mean(grad * unit, axis=-1, keepdims=True)
        grad_input[...] = grad_residual[...] + factor * (grad - unit * mean)

    def widen_gain():
        total = own_gain[...]
        for i in range(1, ws):
            send_gain(i).wait_recv()
            total = total + ws_gain[lax.rem(w + ws - i, ws)]
        ws_gain[w] = total
        for i in range(1, ctx):
            send_wide(i).start()

    def finish_gain():
        total = ws_gain[w]
        for i in range(1, ctx):
            send_wide(i).wait_recv()
            total = total + ctx_gain[lax.rem(c + ctx - i, ctx)]
        gain_out[...] = total

    events = [[] for _ in range(ticks)]

    def put(at, *todo):
        events[min(at, ticks - 1)].extend(todo)

    put(0, turn_ffn)
    for side in range(2):
        put(1 + side, functools.partial(gate_weights, side))
        put(3 + side, functools.partial(up_weights, side))
    put(TICK_NORM, ffn_norm_back)
    put(TICK_ATTENDED, attended_back)
    put(TICK_ATTENDED + 1, out_weights)
    put(TICK_PAIRS, prepare)
    starts = list(range(0, length, span))[::-1]
    if length <= 1024:
        for n, start in enumerate(starts):

            def one_head(g, start=start):
                if g == 0:
                    rope_copy(0, start).start()
                    rope_copy(1, start).start()
                back_unit(g, start, 0, start + span)
                if g == group - 1:
                    finish_rows(start)
                    for b in range(span // tokens):
                        send_rows_back(start // tokens + b)

            for g in range(group):
                put(
                    TICK_PAIRS + (n * group + g) // UNITS_PER_TICK,
                    functools.partial(one_head, g, start),
                )
        at = TICK_PAIRS + -(-len(starts) * group // UNITS_PER_TICK)
    else:

        def all_starts():
            grad_q[...] = jnp.zeros(grad_q.shape, F32)

            def one_start(n, _):
                start = pl.multiple_of(n * span, span)

                def one_block(m, _):
                    low = pl.multiple_of(m * 512, 512)

                    @pl.when(low < start + span)
                    def _():
                        for g in range(group):
                            back_unit(g, start, low, 512)

                    return 0

                lax.fori_loop(0, length // 512, one_block, 0)
                return 0

            lax.fori_loop(0, length // span, one_start, 0)

            def finish(n, _):
                start = pl.multiple_of(n * span, span)
                rope_copy(0, start).start()
                rope_copy(1, start).start()
                finish_rows(start)
                return 0

            lax.fori_loop(0, length // span, finish, 0)
            for to in range(ctx):
                send_rows_back(to)

        put(TICK_PAIRS, all_starts)
        at = TICK_PAIRS + 1
    put(at, turn_normed)
    put(at + 1, finish_output)
    put(at + TICK_GATHER, gather_back, functools.partial(weight_sums, 0))
    put(at + TICK_GATHER + 1, functools.partial(weight_sums, 1))
    put(at + TICK_GATHER + 2, sum_rows)
    put(at + TICK_GATHER + 7, finish_input)
    put(at + TICK_GATHER + 9, widen_gain)
    put(at + TICK_GATHER + 12, finish_gain)

    down_weights()

    def tick(t, _):
        chain(t)
        for n, todo in enumerate(events):
            if todo:

                @pl.when(t == n)
                def _():
                    for event in todo:
                        event()

        return 0

    lax.fori_loop(0, ticks, tick, 0)

    for i in range(count):

        def finish_pair(p, _):
            for odd in range(2):
                _, reduce_end = ends(odd)
                spread_end, _ = ends(odd)

                @pl.when(jnp.logical_not(reduce_end))
                def _():
                    up_line(i, p, odd).wait_send()

                if moved[i]:
                    _, step = spot(i, p, odd)

                    @pl.when(reduce_end & (step != 0))
                    def _():
                        hand_over(i, p, odd).wait_send()

                @pl.when(jnp.logical_not(spread_end))
                def _():
                    down_line(i, p, odd).wait_send()

                over(i, p, odd, core).wait_send()
                over(i, p, odd, 1 - core).wait_recv()
            return 0

        lax.fori_loop(0, counts[i], finish_pair, 0)
    for i in range(count):
        across_cores(i).wait_send()
    for i in range(1, ws):
        for turn in range(3):
            send_sum(turn, i).wait_send()
        send_rows(i).wait_send()
        send_gain(i).wait_send()
    for i in range(1, ctx):
        send_wide(i).wait_send()
        send_pair(i).wait_send()
    for i in range(1, pairs):
        send_back(first_back + lax.rem(own_pair + i, pairs), i).wait_send()


def back(
    x, gains, cosines, sines, q, k, v, pack, attn, normed, w_qkv, w_out, cot, residual, ffn,
    hidden, grad_gate, grad_up, grad_sent, grad_keep, out_sent, out_keep, ws, ctx, own_heads,
):
    tokens, features = x.shape
    group, length, _ = q.shape
    units = hidden.shape[1]
    q_wide = group * HEAD_DIM
    wide = q_wide + 2 * HEAD_DIM
    pairs = ws * own_heads
    span = min(256, length) if length <= 1024 else tokens
    kept = length if length <= 1024 else span
    depth = features // ws
    total_rows = ws * tokens
    moved = (False, True, True, False, True)
    held = pltpu.VMEM
    widths = [features, units, units, features, own_heads * wide]
    halves = [units // 2, depth // 2, depth // 2, own_heads * q_wide // 2, depth // 2]
    rows, parts, sib, red, outs, counts = [], [], [], [], [], []
    for is_moved, n, half, want in zip(moved, widths, halves, ROWS):
        while half % want or not is_moved and half % (2 * want):
            want -= 16
        rows.append(want)
        lead = (ws,) if is_moved else ()
        parts.append(held(lead + (2, half, n), BF))
        sib.append(held(lead + (half, n), BF))
        red.append(held(lead + (half, n), BF))
        outs.append((2, half, ws * n if is_moved else n))
        counts.append(half // want * (ws if is_moved else 1))
    ticks = sum(counts) // 2 + SKEW * (ctx - 1)
    k_count = len(parts)
    vmem, anywhere = pl.BlockSpec(memory_space=pltpu.VMEM), pl.BlockSpec(memory_space=pl.ANY)
    shape = jax.ShapeDtypeStruct
    results = pl.pallas_call(
        functools.partial(
            back_kernel, ws, ctx, group, own_heads, moved, tuple(rows), ticks
        ),
        out_shape=[
            shape((tokens, features), BF), shape((tokens, features), F32), shape(gains.shape, F32)
        ]
        + [shape(o, BF) for o in outs],
        in_specs=[vmem] * 2 + [anywhere] * 20,
        out_specs=[vmem] * 3 + [anywhere] * k_count,
        scratch_shapes=parts
        + sib
        + red
        + [dma(n) for _ in range(8) for n in counts]
        + [
            held((group, kept, HEAD_DIM), BF),
            held(k.shape, BF),
            held(v.shape, BF),
            held((group, kept, 128), F32),
            held(attn.shape, BF),
            held(normed.shape, BF),
            held(w_qkv.shape, BF),
            held(w_out.shape, BF),
            held(cot.shape, BF),
            held((tokens, features), F32),
            held((total_rows, units), BF),
            held((total_rows, units), BF),
            held((total_rows, units), BF),
            held((tokens, features), F32),
            held((features, total_rows), BF),
            held((units, total_rows), BF),
            held((ws, tokens, features), BF),
            held((pairs, tokens, q_wide), BF),
            held((ctx, tokens, q_wide), BF),
            held((tokens, features), F32),
            held((group, kept, HEAD_DIM), F32),
            held((length, HEAD_DIM), F32),
            held((length, HEAD_DIM), F32),
            held((HEAD_DIM, length), BF),
            held((ctx, tokens, wide), BF),
            held((pairs, tokens, wide), BF),
            held((total_rows, own_heads * wide), BF),
            held((2, ws, tokens, features), BF),
            held((tokens, features), F32),
            held(gains.shape, F32),
            held((ws,) + gains.shape, F32),
            held((ctx,) + gains.shape, F32),
            held((span, wide), F32),
            held((span, wide), F32),
            dma(k_count), dma(k_count), dma(16), dma(2, ws), dma(2, ctx), dma(2, pairs),
            dma(2, 3, ws), dma(2, ws), dma(2, ctx), dma(2),
        ],
        compiler_params=pltpu.CompilerParams(
            collective_id=3, has_side_effects=True, vmem_limit_bytes=63 << 20
        ),
        name="back",
    )(
        x, gains, cosines, sines, q, k, v, pack, attn, normed, w_qkv, w_out, cot, residual, ffn,
        hidden, grad_gate, grad_up, grad_sent, grad_keep, out_sent, out_keep,
    )
    sums = [s.reshape(s.shape[0] * s.shape[1], s.shape[2]) for s in results[3:]]
    return results[0], results[1], results[2], sums


def tail_kernel(ws, group, *refs):
    low, refs = refs[:8], refs[8:]
    down, out, gate, up, qkv, output, grad_input, gain_sums = low
    (
        output_out, grad_input_out, attn_gain, g_query, g_key, g_value, g_out, ffn_gain, g_gate,
        g_up, g_down,
    ) = refs
    q_wide = group * HEAD_DIM
    wide = q_wide + 2 * HEAD_DIM
    output_out[...] = output[...].reshape(output_out.shape)
    grad_input_out[...] = grad_input[...].reshape(grad_input_out.shape)
    g_down[...] = down[...].astype(F32)
    g_out[...] = out[...].astype(F32)
    g_gate[...] = gate[...].astype(F32)
    g_up[...] = up[...].astype(F32)
    heads = qkv.shape[1] // wide
    blocks = [qkv[:, h * wide : (h + 1) * wide].astype(F32) for h in range(heads)]
    g_query[...] = jnp.concatenate([b[:, :q_wide] for b in blocks], axis=1)
    g_key[...] = jnp.concatenate([b[:, q_wide : q_wide + HEAD_DIM] for b in blocks], axis=1)
    g_value[...] = jnp.concatenate([b[:, q_wide + HEAD_DIM :] for b in blocks], axis=1)
    w = lax.axis_index("ws")
    depth = attn_gain.shape[0]
    for i in range(ws):

        @pl.when(w == i)
        def _():
            here = gain_sums[:, i * depth : (i + 1) * depth]
            attn_gain[...] = here[0]
            ffn_gain[...] = here[1]


def tail(down, out, gate, up, qkv, output, grad_input, gain_sums, token_shape, ws, group):
    depth = qkv.shape[0]
    steps = depth // 96
    features = out.shape[1]
    q_total = qkv.shape[1] * group // (group + 2)
    k_total = q_total // group
    shape = jax.ShapeDtypeStruct

    def split(rows, *rest):
        return pl.BlockSpec((rows // steps,) + rest, lambda n: (n,) + (0,) * len(rest))

    def whole(*dims):
        return pl.BlockSpec(dims, lambda n: (0,) * len(dims))

    out_shape = [
        shape(token_shape, BF), shape(token_shape, F32), shape((depth,), F32),
        shape((depth, q_total), F32), shape((depth, k_total), F32), shape((depth, k_total), F32),
        shape(out.shape, F32), shape((depth,), F32), shape(gate.shape, F32),
        shape(up.shape, F32), shape(down.shape, F32),
    ]
    return pl.pallas_call(
        functools.partial(tail_kernel, ws, group),
        grid=(steps,),
        out_shape=out_shape,
        in_specs=[split(*a.shape) for a in (down, out, gate, up, qkv, output, grad_input)]
        + [whole(*gain_sums.shape)],
        out_specs=[
            whole(*o.shape) if len(o.shape) == 1 else split(*o.shape) for o in out_shape
        ],
        compiler_params=pltpu.CompilerParams(vmem_limit_bytes=63 << 20),
        name="tail",
    )(down, out, gate, up, qkv, output, grad_input, gain_sums)


def body(
    hidden_in,
    attn_gain,
    w_query,
    key_weight,
    value_weight,
    w_out,
    ffn_gain,
    w_gate,
    w_up,
    w_down,
    cotangent,
):
    ws, ctx = lax.axis_size("ws"), lax.axis_size("ctx")
    local_len, local_seqs, features = hidden_in.shape
    row_count = local_len * local_seqs
    q_heads = w_query.shape[1] // HEAD_DIM
    kv_heads = key_weight.shape[1] // HEAD_DIM
    group = q_heads // kv_heads
    own_heads = kv_heads // ws
    wide = (group + 2) * HEAD_DIM
    q_wide = group * HEAD_DIM
    pairs = ws * local_seqs * own_heads
    copies = ctx // pairs
    depth = features // ws
    cosines, sines = rope_tables(ctx * local_len, group + 1, 1)
    gains = jnp.stack([attn_gain, ffn_gain]).astype(F32)
    gains = lax.dynamic_update_slice(
        jnp.zeros((8, features), F32), gains, (0, lax.axis_index("ws") * depth)
    )
    inputs = hidden_in.reshape(row_count, features)
    grad_low = cotangent.reshape(row_count, features)
    (
        normed_attn, w_qkv, q_pair, k_pair, v_pair, pack, attn_in, grad_low_all, gains,
        residual, normed_ffn, hidden, grad_gate, grad_up, grad_sent, grad_keep, out_sent, out_keep,
    ) = front(
        inputs, gains, w_query, key_weight, value_weight, w_gate, w_up, grad_low, cosines, sines,
        w_out, w_down, ws, ctx, own_heads, group,
    )
    output, grad_input, gain_sums, (g_down, g_gate, g_up, g_out, g_qkv) = back(
        inputs, gains, cosines, sines, q_pair, k_pair, v_pair, pack, attn_in, normed_attn, w_qkv,
        w_out, grad_low_all, residual, normed_ffn, hidden, grad_gate, grad_up, grad_sent,
        grad_keep, out_sent, out_keep, ws, ctx, own_heads,
    )
    results = tail(
        g_down, g_out, g_gate, g_up, g_qkv, output, grad_input, gain_sums, hidden_in.shape, ws, group
    )
    output, grad_input, attn_gain_sum, *middle_sums = results
    *middle_sums, ffn_gain_sum, g_gate, g_up, g_down = middle_sums
    return (
        output,
        grad_input,
        attn_gain_sum,
        *middle_sums,
        ffn_gain_sum,
        g_gate,
        g_up,
        g_down,
    )


def solution(mesh):
    tokens, rows, one = P("ctx", "ws", None), P("ws", None), P("ws")
    return jax.shard_map(
        body,
        mesh=mesh,
        in_specs=(tokens, one, rows, rows, rows, rows, one, rows, rows, rows, tokens),
        out_specs=(tokens, tokens, one, rows, rows, rows, rows, one, rows, rows, rows),
        check_vma=False,
    )
```
